32 devices in a mesh: tm: 4 (over x, core), gx: 2 (over y), gy: 4 (over z).
Axes of the slice: x: 2, y: 2, z: 4, core: 2. Of those that a mesh axis runs over, the one named last changes fastest.
Arguments:
- velocity: float32 [3, 32, 128, 256], P(None, 'gx', 'gy'), may hold values from -3 to 3
- start_field: float32 [3, 32, 128, 256], P(None, 'gx', 'gy'), may hold values from -6 to 6
- guess: float32 [4, 3, 32, 128, 256], P('tm', None, 'gx', 'gy'), may hold values from -6 to 6
Outputs:
- slab_ends: float32 [4, 3, 32, 128, 256], P('tm', None, 'gx', 'gy')
The draws below stay inside these ranges and needn't reach their ends.
All inputs are finite; a program needn't handle non-finite values.
Results may differ from the reference program's by a relative error of at most 0.0003.
Values sent between devices are 32-bit elements; how exact they have to be, the bound alone decides.
No kernel may reach another device: no remote copies, remote signals or barrier semaphores. Data moves between devices by JAX's collectives and lax.ppermute only.
A program may use at most 128 MiB of HBM per device.

```python
import jax
import jax.numpy as jnp

NZ = 256
ITERS = 2
SLABS = 4
NX = 32
NY = 128


def block_levels(own_key, dims, cuts, smallest, largest):
    loudness, own = 1.0, jax.random.fold_in(own_key, 6)
    for axis_at, shards_of in cuts:
        draws = jnp.exp(jax.random.uniform(jax.random.fold_in(own, axis_at), (shards_of,), jnp.float32, smallest / len(cuts), largest / len(cuts)))
        loudness = loudness * jnp.repeat(draws, dims[axis_at] // shards_of).reshape([-1 if axis == axis_at else 1 for axis in range(len(dims))])
    return loudness


def centred(own_key, dims, scale, bound, cuts=(), held_as=jnp.bfloat16):
    level = block_levels(own_key, dims, cuts, -0.22, 0.18) if cuts else 1.0
    values = jax.random.normal(own_key, dims, jnp.float32) * scale * level
    return jnp.minimum(jnp.maximum(values, -bound), bound).astype(held_as)


def setup_inputs(seed: int = 0) -> dict:
    seeds = jax.random.split(jax.random.key(seed), 4)
    return {
        "velocity": centred(seeds[0], (3, NX, NY, NZ), 0.5, 3.0, ((1, 2), (2, 4)), jnp.float32),
        "start_field": centred(seeds[1], (3, NX, NY, NZ), 1.0, 6.0, ((1, 2), (2, 4)), jnp.float32),
        "guess": centred(seeds[2], (SLABS, 3, NX, NY, NZ), 1.0, 6.0, ((0, 4), (2, 2), (3, 4)), jnp.float32),
    }


VISCOSITY = 0.25
TIME_STEP = 0.5


def gradients(velocity):
    rows = []
    for target in range(3):
        for across in range(3):
            ahead = jnp.roll(velocity[target], -1, across)
            behind = jnp.roll(velocity[target], 1, across)
            rows.append((ahead - behind) / 2.0)
    return jnp.stack(rows)


def restrict(field):
    extent = field.shape
    blocks = field.reshape(extent[0], extent[1] // 2, 2, extent[2] // 2, 2, extent[3] // 2, 2)
    return jnp.mean(blocks, axis=(2, 4, 6))


def prolong(field):
    extent = field.shape
    spread = jnp.broadcast_to(field[:, :, None, :, None, :, None], (extent[0], extent[1], 2, extent[2], 2, extent[3], 2))
    return spread.reshape(extent[0], extent[1] * 2, extent[2] * 2, extent[3] * 2)


def operator(field, velocity, grads, spacing):
    outputs = []
    for target in range(3):
        component = field[target]
        laplace = -6.0 * component
        advect = jnp.zeros_like(component)
        for across in range(3):
            ahead = jnp.roll(component, -1, across)
            behind = jnp.roll(component, 1, across)
            laplace = laplace + ahead + behind
            advect = advect + velocity[across] * (ahead - behind)
        result_term = (VISCOSITY / (spacing * spacing)) * laplace - advect / (2.0 * spacing)
        for across in range(3):
            result_term = result_term + field[across] * grads[3 * target + across]
        outputs.append(result_term)
    return jnp.stack(outputs)


def reference(velocity, start_field, guess):
    grads = gradients(velocity)
    coarse_vel = restrict(velocity)
    coarse_grads = restrict(grads)
    coarse_init = restrict(start_field)

    def fine(field):
        return operator(field, velocity, grads, 1.0)

    def coarse(field):
        return operator(field, coarse_vel, coarse_grads, 2.0)

    node_values = []
    for slab in range(SLABS):
        begin = start_field if slab == 0 else guess[slab]
        node_values.append([begin, guess[slab], guess[slab]])
    rhs_values = [[fine(field) for field in nodes] for nodes in node_values]
    for sweep_index in range(ITERS):
        if sweep_index > 0:
            for slab in range(SLABS):
                rhs_values[slab][0] = fine(node_values[slab][0])
                rhs_values[slab][2] = fine(node_values[slab][2])
        chained = coarse_init
        for slab in range(SLABS):
            nodes = node_values[slab]
            values = rhs_values[slab]
            integral = TIME_STEP * (values[0] / 6.0 + values[1] * (2.0 / 3.0) + values[2] / 6.0)
            coarse_zero = restrict(nodes[0])
            coarse_end = restrict(nodes[2])
            offset = restrict(integral) - TIME_STEP * coarse(coarse_zero)
            coarse_start = chained
            finish = coarse_start + TIME_STEP * coarse(coarse_start) + offset
            chained = finish
            delta_zero = prolong(coarse_start - coarse_zero)
            delta_end = prolong(finish - coarse_end)
            fixed_zero = nodes[0] + delta_zero
            fixed_mid = nodes[1] + 0.5 * (delta_zero + delta_end)
            fixed_end = nodes[2] + delta_end
            corrected = [fine(fixed_zero), fine(fixed_mid), fine(fixed_end)]
            middle = fixed_zero + TIME_STEP * (corrected[0] * (5.0 / 24.0) + corrected[1] / 3.0 - corrected[2] / 24.0)
            middle_value = fine(middle)
            slab_end = middle + (0.5 * TIME_STEP) * (middle_value - corrected[1]) + TIME_STEP * (-corrected[0] / 24.0 + corrected[1] / 3.0 + corrected[2] * (5.0 / 24.0))
            node_values[slab] = [fixed_zero, middle, slab_end]
            rhs_values[slab] = [corrected[0], middle_value, corrected[2]]
        if sweep_index + 1 < ITERS:
            ends = [node_values[slab][2] for slab in range(SLABS)]
            for slab in range(1, SLABS):
                node_values[slab][0] = ends[slab - 1]
    return jnp.stack([node_values[slab][2] for slab in range(SLABS)])
```

```python
import jax
import jax.numpy as jnp
from jax import lax
from jax.experimental import pallas as pl
from jax.experimental.pallas import tpu as pltpu
from jax.sharding import PartitionSpec as P

ITERS = 2
VISCOSITY = 0.25
TIME_STEP = 0.5
PAD = 8
CHUNK = 16
F32 = jnp.float32
BF16 = jnp.bfloat16


def ring(size, by):
    return [(i, (i + by) % size) for i in range(size)]


def both_faces(faces, permute, size):
    if size == 2:
        return permute(faces, 1)
    before = permute(faces[:, 0:1], 1)
    after = permute(faces[:, 1:2], -1)
    return jnp.concatenate([before, after], axis=1)


def swap_faces(faces):
    x_faces, y_last, y_first = faces
    gx, gy = lax.axis_size("gx"), lax.axis_size("gy")
    before_after = both_faces(x_faces, lambda a, by: lax.ppermute(a, "gx", ring(gx, by)), gx)
    behind = lax.ppermute(y_last, "gy", ring(gy, 1))
    ahead = lax.ppermute(y_first, "gy", ring(gy, -1))
    return before_after, behind, ahead


def hand_on(slabs, value, faces):
    gx, gy = lax.axis_size("gx"), lax.axis_size("gy")

    def permute(array, dx, dy):
        pairs = []
        for t in slabs:
            for x in range(gx):
                for y in range(gy):
                    source = (t * gx + x) * gy + y
                    target = ((t + 1) * gx + (x + dx) % gx) * gy + (y + dy) % gy
                    pairs.append((source, target))
        return lax.ppermute(array, ("tm", "gx", "gy"), pairs)

    moved = [] if value is None else [permute(value, 0, 0)]
    x_faces, y_last, y_first = faces
    moved.append(both_faces(x_faces, lambda a, by: permute(a, by, 0), gx))
    moved.append(permute(y_last, 0, 1))
    moved.append(permute(y_first, 0, -1))
    return moved


class Node:
    def __init__(self, main, x_faces, behind, ahead, off=0):
        self.main, self.x_faces, self.behind, self.ahead, self.off = main, x_faces, behind, ahead, off


def total(terms):
    result = terms[0]
    for term in terms[1:]:
        result = result + term
    return result


def fill(ext, parts, spread=()):
    width, length = ext.shape[1] - 2, ext.shape[2] - 2 * PAD
    inner = slice(PAD, PAD + length)
    for c in range(3):
        for k, at in ((0, 0), (1, width + 1)):
            terms = [w * n.x_faces[n.off + c, k] for w, n in parts]
            terms += [w * p[c, k * (width // 2 + 1)] for w, p, _ in spread]
            ext[c, at, inner] = total(terms)

    @pl.loop(0, width // 2)
    def _(i):
        for q in range(2):
            x = 2 * i + q
            for c in range(3):
                terms = [w * n.main[c, x] for w, n in parts]
                terms += [w * p[c, i + 1] for w, p, _ in spread]
                ext[c, x + 1, inner] = total(terms)
                row = pl.ds(x, 1)
                for k, at in ((0, PAD - 1), (1, PAD + length)):
                    terms = [w * (n.ahead if k else n.behind)[n.off + c, row] for w, n in parts]
                    terms += [w * e[k, c, pl.ds(i, 1)] for w, _, e in spread]
                    ext[c, x + 1, at : at + 1] = total(terms)


def turned(value, by):
    return pltpu.roll(value, by % value.shape[-1], value.ndim - 1)


def sides(ext, c, x, r, n):
    here = ext[c, x, r : r + n]
    return (
        here,
        (ext[c, x + 1, r : r + n], ext[c, x, r + 1 : r + 1 + n], turned(here, -1)),
        (ext[c, x - 1, r : r + n], ext[c, x, r - 1 : r - 1 + n], turned(here, 1)),
    )


def slopes(half, x, r, n):
    rows = []
    for a in range(3):
        _, ahead, behind = sides(half, a, x, r, n)
        rows.append([ahead[b] - behind[b] for b in range(3)])
    return rows


def rates(ext, x, r, n, speeds, grads, strength):
    fields = [sides(ext, a, x, r, n) for a in range(3)]
    toward = [strength - speed for speed in speeds]
    away = [strength + speed for speed in speeds]
    outputs = []
    for a in range(3):
        here, ahead, behind = fields[a]
        result = here * (grads[a][a] - 6.0 * strength)
        for b in range(3):
            if b != a:
                result = result + fields[b][0] * grads[a][b]
        for b in range(3):
            result = result + toward[b] * ahead[b] + away[b] * behind[b]
        outputs.append(result)
    return outputs


def fine_rates(ext, half, x, r, n):
    grads = slopes(half, x, r, n)
    speeds = [half[b, x, r : r + n] for b in range(3)]
    return rates(ext, x, r, n, speeds, grads, VISCOSITY), grads


def split(value):
    high = value.astype(BF16)
    low = (value - high.astype(F32)).astype(BF16)
    return high, low


def pair_table(rows, columns, by_row, entry):
    i = lax.broadcasted_iota(jnp.int32, (rows, columns), 0)
    j = lax.broadcasted_iota(jnp.int32, (rows, columns), 1)
    same = (i >> 1) == j if by_row else i == (j >> 1)
    return jnp.where(same, entry, 0.0).astype(BF16)


def squeeze(summed, rows, store, count):
    cx, y, z = summed.shape[1:]
    table = pair_table(z, z // 2, True, 0.125)
    for c in range(count):
        high, low = split(summed[c].reshape(cx * y, z))
        rows[...] = jnp.dot(high, table, preferred_element_type=F32) + jnp.dot(
            low, table, preferred_element_type=F32
        )
        half = cx * y // 2
        value = rows[pl.ds(0, half, stride=2)] + rows[pl.ds(1, half, stride=2)]
        store(c, value.reshape(cx, y // 2, z // 2))


def prolong(field, wide, edge, rows):
    cx, cy, cz = field.main.shape[1:]
    single = pair_table(cz, 2 * cz, False, 1.0)
    table = jnp.concatenate([single, single], axis=0)

    def along_z(value):
        high, low = split(value)
        return jnp.dot(jnp.concatenate([high, low], axis=1), table, preferred_element_type=F32)

    count = (cx + 2) * cy
    edges = []
    for c in range(3):
        layers = [field.x_faces[c, 0:1], field.main[c], field.x_faces[c, 1:2]]
        value = jnp.concatenate(layers, axis=0).reshape(count, cz)
        rows[pl.ds(0, count, stride=2)] = value
        rows[pl.ds(1, count, stride=2)] = value
        wide[c] = along_z(rows[...]).reshape(cx + 2, 2 * cy, 2 * cz)
        edges += [field.behind[c], field.ahead[c]]
    value = along_z(jnp.concatenate(edges, axis=0))
    for c in range(3):
        for k in range(2):
            at = (2 * c + k) * cx
            edge[k, c] = value[at : at + cx]


def emit_faces(main, outs):
    x_faces, y_last, y_first = outs
    width, length = main.shape[1:3]
    for c in range(3):
        x_faces[c, 0] = main[c, width - 1]
        x_faces[c, 1] = main[c, 0]
        for x in range(width):
            y_last[c, x : x + 1] = main[c, x, length - 1 : length]
            y_first[c, x : x + 1] = main[c, x, 0:1]


def coarsen_kernel(first, v, s, g, speed, zero, end, end_x, end_l, end_f, summed, rows):
    f = first[0]

    def run(field, store):
        @pl.loop(0, field.shape[1] // 2)
        def _(i):
            for c in range(3):
                summed[c, i] = field[c, 2 * i] + field[c, 2 * i + 1]

        squeeze(summed, rows, store, 3)

    def store_end(c, value):
        end[c] = value

    def store_zero(c, value):
        zero[c] = f * value + (1.0 - f) * end[c]

    def store_speed(c, value):
        speed[c] = value * 0.25

    run(g, store_end)
    emit_faces(end, (end_x, end_l, end_f))
    run(s, store_zero)
    run(v, store_speed)


def integral_loop(ext, half, summed, grads_summed):
    width, length = ext.shape[1] - 2, ext.shape[2] - 2 * PAD
    n = min(CHUNK, length)

    @pl.loop(0, width // 2)
    def _(i):
        for r in range(0, length, n):
            pair = [fine_rates(ext, half, 2 * i + 1 + q, PAD + r, n) for q in range(2)]
            for a in range(3):
                summed[a, i, r : r + n] = pair[0][0][a] + pair[1][0][a]
                if grads_summed is not None:
                    for b in range(3):
                        value = pair[0][1][a][b] + pair[1][1][a][b]
                        grads_summed[3 * a + b, i, r : r + n] = value


def offset_start_kernel(
    first, v, s, g, x_faces, behind, ahead, zero,
    integral, coarse_grads, end, end_x, end_l, end_f,
    ext, half, summed, grads_summed, rows,
):
    f = first[0]
    fill(half, [(0.5, Node(v, x_faces, behind, ahead))])
    start = Node(s, x_faces, behind, ahead, 6)
    guess = Node(g, x_faces, behind, ahead, 3)
    share = f * (TIME_STEP / 6.0)
    fill(ext, [(share, start), (TIME_STEP - share, guess)])
    integral_loop(ext, half, summed, grads_summed)

    def store(c, value):
        integral[c] = value
        end[c] = zero[c] + value

    squeeze(summed, rows, store, 3)
    emit_faces(end, (end_x, end_l, end_f))

    def store_grads(c, value):
        coarse_grads[c] = value

    squeeze(grads_summed, rows, store_grads, 9)


def offset_later_kernel(
    first, v, s, x_faces, behind, ahead,
    u0, u0_x, u0_b, u0_a, u1, u1_x, u1_b, u1_a, u2, u2_x, u2_b, u2_a,
    integral, zero, end, end_x, end_l, end_f,
    ext, half, summed, rows,
):
    f = first[0]
    fill(half, [(0.5, Node(v, x_faces, behind, ahead))])
    sixth = TIME_STEP / 6.0
    fill(
        ext,
        [
            (f * sixth, Node(s, x_faces, behind, ahead, 6)),
            (sixth, Node(u0, u0_x, u0_b, u0_a)),
            (TIME_STEP * 2.0 / 3.0, Node(u1, u1_x, u1_b, u1_a)),
            (sixth, Node(u2, u2_x, u2_b, u2_a)),
        ],
    )

    @pl.loop(0, s.shape[1] // 2)
    def _(i):
        for c in range(3):
            summed[c, i] = f * (s[c, 2 * i] + s[c, 2 * i + 1]) + (u0[c, 2 * i] + u0[c, 2 * i + 1])

    def store_zero(c, value):
        zero[c] = value

    squeeze(summed, rows, store_zero, 3)
    integral_loop(ext, half, summed, None)

    def store(c, value):
        integral[c] = value
        end[c] = zero[c] + value

    squeeze(summed, rows, store, 3)
    emit_faces(end, (end_x, end_l, end_f))


def chain_kernel(last, arrivals, *refs):
    refs = list(refs)

    def take(count):
        taken = refs[:count]
        del refs[:count]
        return taken

    first, = take(1)
    arrived = [take(4) for _ in range(arrivals)]
    zero, zero_x, zero_b, zero_a, integral, speed, coarse_grads = take(7)
    f = first[0]
    if last:
        end_two, = take(1)
        d0, d0_x, d0_b, d0_a, d2, d2_x, d2_l, d2_f = take(8)
    else:
        end, end_x, end_l, end_f = take(4)
        d0, d0_x, d0_b, d0_a = take(4)
    ext, = take(1)
    rest = 1.0 - f
    width, length = zero.shape[1:3]
    for out, old, k in ((d0, zero, 0), (d0_x, zero_x, 1), (d0_b, zero_b, 2), (d0_a, zero_a, 3)):
        out[...] = rest * (total([a[k][...] for a in arrived]) - old[...])
    fill(ext, [(TIME_STEP, Node(d0, d0_x, d0_b, d0_a))])

    @pl.loop(0, width)
    def _(x):
        speeds = [speed[b, x] for b in range(3)]
        grads = [[coarse_grads[3 * a + b, x] for b in range(3)] for a in range(3)]
        changes = rates(ext, x + 1, PAD, length, speeds, grads, VISCOSITY / 4.0)
        for a in range(3):
            value = zero[a, x] + d0[a, x] + integral[a, x] + changes[a]
            if last:
                d2[a, x] = value - end_two[a, x]
            else:
                end[a, x] = value

    emit_faces(d2 if last else end, (d2_x, d2_l, d2_f) if last else (end_x, end_l, end_f))


def middle_kernel(nodes, *refs):
    first, v, vx, vb, va = refs[:5]
    at = 5
    parts = []
    for _, _, _, own, off in nodes:
        main = refs[at]
        at += 1
        if own:
            x_faces, behind, ahead = refs[at : at + 3]
            at += 3
        else:
            x_faces, behind, ahead = vx, vb, va
        parts.append(Node(main, x_faces, behind, ahead, off))
    d0 = Node(*refs[at : at + 4])
    d2 = Node(*refs[at + 4 : at + 8])
    a1, a1_x, a1_l, a1_f, rest, rest_x, rest_b, rest_a = refs[at + 8 : at + 16]
    ext, half, wide0, edge0, wide2, edge2, rows = refs[at + 16 :]
    f = first[0]
    begin, first_stage, second_stage = [
        [(spec[k][0] * f + spec[k][1], node) for spec, node in zip(nodes, parts)] for k in range(3)
    ]
    fill(half, [(0.5, Node(v, vx, vb, va))])
    prolong(d0, wide0, edge0, rows)
    prolong(d2, wide2, edge2, rows)
    fill(
        ext,
        [(TIME_STEP * w, node) for w, node in first_stage],
        [(TIME_STEP * 0.375, wide0, edge0), (TIME_STEP * 0.125, wide2, edge2)],
    )
    width, length = a1.shape[1:3]
    n = min(CHUNK, length)
    last_cx = width // 2 + 1

    def rest_of(get, p0, p2):
        return total([w * get(node) for w, node in second_stage]) + 0.125 * (p2 - p0)

    for c in range(3):
        for k in range(2):
            rest_x[c, k] = rest_of(
                lambda nd: nd.x_faces[nd.off + c, k], wide0[c, k * last_cx], wide2[c, k * last_cx]
            )

    @pl.loop(0, width // 2)
    def _(i):
        for q in range(2):
            x = 2 * i + q
            row = pl.ds(x, 1)
            for r in range(0, length, n):
                changes, _ = fine_rates(ext, half, x + 1, PAD + r, n)
                for a in range(3):
                    p0, p2 = wide0[a, i + 1, r : r + n], wide2[a, i + 1, r : r + n]
                    start = total([w * nd.main[a, x, r : r + n] for w, nd in begin])
                    a1[a, x, r : r + n] = start + p0 + changes[a]
                    rest[a, x, r : r + n] = rest_of(lambda nd: nd.main[a, x, r : r + n], p0, p2)
            for c in range(3):
                p0, p2 = edge0[0, c, pl.ds(i, 1)], edge2[0, c, pl.ds(i, 1)]
                rest_b[c, row] = rest_of(lambda nd: nd.behind[nd.off + c, row], p0, p2)
                p0, p2 = edge0[1, c, pl.ds(i, 1)], edge2[1, c, pl.ds(i, 1)]
                rest_a[c, row] = rest_of(lambda nd: nd.ahead[nd.off + c, row], p0, p2)

    emit_faces(a1, (a1_x, a1_l, a1_f))


def finish_kernel(last, first, v, vx, vb, va, a1, a1_x, a1_b, a1_a, rest, rest_x, rest_b, rest_a, *refs):
    if last:
        a2, ext, half = refs
    else:
        a2, a2_x, a2_l, a2_f, end, end_x, end_l, end_f, ext, half, summed, rows = refs
    fill(half, [(0.5, Node(v, vx, vb, va))])
    fill(
        ext,
        [
            (TIME_STEP * 0.5, Node(a1, a1_x, a1_b, a1_a)),
            (TIME_STEP, Node(rest, rest_x, rest_b, rest_a)),
        ],
    )
    width, length = a1.shape[1:3]
    n = min(CHUNK, length)

    @pl.loop(0, width // 2)
    def _(i):
        for r in range(0, length, n):
            pair = []
            for q in range(2):
                x = 2 * i + q
                changes, _ = fine_rates(ext, half, x + 1, PAD + r, n)
                pair.append([a1[a, x, r : r + n] + changes[a] for a in range(3)])
                for a in range(3):
                    a2[a, x, r : r + n] = pair[q][a]
            if not last:
                for a in range(3):
                    summed[a, i, r : r + n] = pair[0][a] + pair[1][a]

    if not last:
        emit_faces(a2, (a2_x, a2_l, a2_f))

        def store(c, value):
            end[c] = value

        squeeze(summed, rows, store, 3)
        emit_faces(end, (end_x, end_l, end_f))


def call(kernel, name, first, args, outs, scratch, flops=0):
    moved = sum(4 * a.size for a in args)
    return pl.pallas_call(
        kernel,
        name=name,
        out_shape=[jax.ShapeDtypeStruct(dims, F32) for dims in outs],
        in_specs=[pl.BlockSpec(memory_space=pltpu.SMEM)] + [pl.BlockSpec(memory_space=pltpu.VMEM)] * len(args),
        out_specs=[pl.BlockSpec(memory_space=pltpu.VMEM)] * len(outs),
        scratch_shapes=[pltpu.VMEM(dims, F32) for dims in scratch],
        compiler_params=pltpu.CompilerParams(vmem_limit_bytes=56 << 20),
        cost_estimate=pl.CostEstimate(flops=flops, bytes_accessed=moved, transcendentals=0),
    )(first, *args)


def shards(velocity, start_field, guess):
    own = guess[0]
    _, nx, ny, nz = own.shape
    cx, cy, cz = nx // 2, ny // 2, nz // 2
    slabs = lax.axis_size("tm")
    first = (lax.axis_index("tm") == 0).astype(F32).reshape(1)

    fine, fine_faces = (3, nx, ny, nz), [(3, 2, ny, nz), (3, nx, nz), (3, nx, nz)]
    coarse, coarse_faces = (3, cx, cy, cz), [(3, 2, cy, cz), (3, cx, cz), (3, cx, cz)]
    ext = (3, nx + 2, ny + 2 * PAD, nz)
    coarse_ext = (3, cx + 2, cy + 2 * PAD, cz)
    summed, rows = (3, cx, ny, nz), (cx * ny, cz)
    wide, edge, wide_rows = (3, cx + 2, ny, nz), (2, 3, cx, nz), ((cx + 2) * ny, cz)

    fields = [velocity, own, start_field]
    packed = (
        jnp.concatenate([jnp.concatenate([f[:, nx - 1 :], f[:, :1]], axis=1) for f in fields], axis=0),
        jnp.concatenate([f[:, :, ny - 1] for f in fields], axis=0),
        jnp.concatenate([f[:, :, 0] for f in fields], axis=0),
    )
    layers = swap_faces(packed)
    speed, zero, end_two, *sent = call(
        coarsen_kernel, "coarsen", first, [velocity, start_field, own],
        [coarse, coarse, coarse] + coarse_faces, [summed, rows], 10_000_000,
    )
    zero_faces = swap_faces(sent)
    integral, coarse_grads, end, *sent = call(
        offset_start_kernel, "offset_start", first, [velocity, start_field, own, *layers, zero],
        [coarse, (9, cx, cy, cz), coarse] + coarse_faces,
        [ext, ext, summed, (9, cx, ny, nz), rows], 40_000_000,
    )
    for sweep_index in range(ITERS):
        final = sweep_index + 1 == ITERS
        arrivals = []
        for slab in range(slabs - 1):
            arrivals.append(hand_on([slab], end, sent))
            last = slab + 2 == slabs
            args = [a for group in arrivals for a in group]
            args += [zero, *zero_faces, integral, speed, coarse_grads]
            if last:
                outs = [coarse] + coarse_faces + [coarse] + coarse_faces
                args.append(end_two)
            else:
                outs = [coarse] + coarse_faces + [coarse] + coarse_faces
            count = len(arrivals)
            results = call(
                lambda *refs, last=last, count=count: chain_kernel(last, count, *refs),
                "chain", first, args, outs, [coarse_ext], 2_000_000,
            )
            if not last:
                end, *sent = results[:4]
        d0, d2 = list(results[:4]), [results[4], *swap_faces(results[5:])]

        if sweep_index == 0:
            nodes = (
                ((1.0, 0.0), (5.0 / 24.0, 0.0), (-1.0 / 24.0, 0.0), False, 6),
                ((-1.0, 1.0), (-5.0 / 24.0, 0.5), (1.0 / 24.0, 0.0), False, 3),
            )
            args = [start_field, own]
        else:
            nodes = (
                ((1.0, 0.0), (5.0 / 24.0, 0.0), (-1.0 / 24.0, 0.0), False, 6),
                ((0.0, 1.0), (0.0, 5.0 / 24.0), (0.0, -1.0 / 24.0), True, 0),
                ((0.0, 0.0), (0.0, 1.0 / 3.0), (0.0, -1.0 / 6.0), True, 0),
                ((0.0, 0.0), (0.0, -1.0 / 24.0), (0.0, 5.0 / 24.0), True, 0),
            )
            args = [start_field, *u0, *u1, *u2]
        middle, m_x, m_l, m_f, *rest = call(
            lambda *refs, nodes=nodes: middle_kernel(nodes, *refs),
            "middle", first, [velocity, *layers, *args, *d0, *d2],
            [fine] + fine_faces + [fine] + fine_faces,
            [ext, ext, wide, edge, wide, edge, wide_rows], 60_000_000,
        )
        u1 = [middle, *swap_faces((m_x, m_l, m_f))]
        results = call(
            lambda *refs, final=final: finish_kernel(final, *refs),
            "finish", first, [velocity, *layers, *u1, *rest],
            [fine] if final else [fine] + fine_faces + [coarse] + coarse_faces,
            [ext, ext] if final else [ext, ext, summed, rows], 40_000_000,
        )
        if final:
            return results[0][None]
        value, *faces = results[:4]
        u0 = hand_on(range(slabs - 1), value, faces)
        u2 = [value, *swap_faces(faces)]
        zero_faces = hand_on(range(slabs - 1), None, results[5:])
        end_two = results[4]
        integral, zero, end, *sent = call(
            offset_later_kernel, "offset_later", first,
            [velocity, start_field, *layers, *u0, *u1, *u2],
            [coarse, coarse, coarse] + coarse_faces, [ext, ext, summed, rows], 40_000_000,
        )


def solution(mesh):
    in_specs = (
        P(None, "gx", "gy", None),
        P(None, "gx", "gy", None),
        P("tm", None, "gx", "gy", None),
    )
    out_specs = P("tm", None, "gx", "gy", None)
    return jax.shard_map(shards, mesh=mesh, in_specs=in_specs, out_specs=out_specs, check_vma=False)
```

```python
import jax
import jax.numpy as jnp
from jax import lax
from jax.experimental import pallas as pl
from jax.experimental.pallas import tpu as pltpu
from jax.sharding import PartitionSpec as P

ITERS = 2
VISCOSITY = 0.25
TIME_STEP = 0.5
PAD = 8
CHUNK = 8
F32 = jnp.float32
BF16 = jnp.bfloat16


def ring(size, by):
    return [(i, (i + by) % size) for i in range(size)]


def both_faces(faces, permute, size):
    if size == 2:
        return permute(faces, 1)
    before = permute(faces[:, 0:1], 1)
    after = permute(faces[:, 1:2], -1)
    return jnp.concatenate([before, after], axis=1)


def swap_faces(faces):
    x_faces, y_last, y_first = faces
    gx, gy = lax.axis_size("gx"), lax.axis_size("gy")
    before_after = both_faces(x_faces, lambda a, by: lax.ppermute(a, "gx", ring(gx, by)), gx)
    behind = lax.ppermute(y_last, "gy", ring(gy, 1))
    ahead = lax.ppermute(y_first, "gy", ring(gy, -1))
    return before_after, behind, ahead


def hand_on(slabs, value, faces):
    gx, gy = lax.axis_size("gx"), lax.axis_size("gy")

    def permute(array, dx, dy):
        pairs = []
        for t in slabs:
            for x in range(gx):
                for y in range(gy):
                    source = (t * gx + x) * gy + y
                    target = ((t + 1) * gx + (x + dx) % gx) * gy + (y + dy) % gy
                    pairs.append((source, target))
        return lax.ppermute(array, ("tm", "gx", "gy"), pairs)

    moved = [] if value is None else [permute(value, 0, 0)]
    x_faces, y_last, y_first = faces
    moved.append(both_faces(x_faces, lambda a, by: permute(a, by, 0), gx))
    moved.append(permute(y_last, 0, 1))
    moved.append(permute(y_first, 0, -1))
    return moved


class Node:
    def __init__(self, main, x_faces, behind, ahead, off=0):
        self.main, self.x_faces, self.behind, self.ahead, self.off = main, x_faces, behind, ahead, off


def total(terms):
    result = terms[0]
    for term in terms[1:]:
        result = result + term
    return result


def each(count, unrolled=False):
    def wrap(body):
        if unrolled:
            for i in range(count):
                body(i)
        else:
            pl.loop(0, count)(body)

    return wrap


def fill(ext, parts, spread=(), unrolled=False):
    width, length = ext.shape[1] - 2, ext.shape[2] - 2 * PAD
    inner = slice(PAD, PAD + length)
    for c in range(3):
        for k, at in ((0, 0), (1, width + 1)):
            terms = [w * n.x_faces[n.off + c, k] for w, n in parts]
            terms += [w * p[c, k * (width // 2 + 1)] for w, p, _ in spread]
            ext[c, at, inner] = total(terms)

    @each(width // 2, unrolled)
    def _(i):
        for q in range(2):
            x = 2 * i + q
            for c in range(3):
                terms = [w * n.main[c, x] for w, n in parts]
                terms += [w * p[c, i + 1] for w, p, _ in spread]
                ext[c, x + 1, inner] = total(terms)
                row = pl.ds(x, 1)
                for k, at in ((0, PAD - 1), (1, PAD + length)):
                    terms = [w * (n.ahead if k else n.behind)[n.off + c, row] for w, n in parts]
                    terms += [w * e[k, c, pl.ds(i, 1)] for w, _, e in spread]
                    ext[c, x + 1, at : at + 1] = total(terms)


def turned(value, by):
    return pltpu.roll(value, by % value.shape[-1], value.ndim - 1)


def sides(ext, c, x, r, n):
    here = ext[c, x, r : r + n]
    return (
        here,
        (ext[c, x + 1, r : r + n], ext[c, x, r + 1 : r + 1 + n], turned(here, -1)),
        (ext[c, x - 1, r : r + n], ext[c, x, r - 1 : r - 1 + n], turned(here, 1)),
    )


def rates(ext, x, r, n, speeds, grads_of, strength):
    here = [ext[b, x, r : r + n] for b in range(3)]
    toward = [strength - speed for speed in speeds]
    away = [strength + speed for speed in speeds]
    outputs = []
    for a in range(3):
        _, ahead, behind = sides(ext, a, x, r, n)
        grads = grads_of(a)
        result = here[a] * (grads[a] - 6.0 * strength)
        for b in range(3):
            if b != a:
                result = result + here[b] * grads[b]
            result = result + toward[b] * ahead[b] + away[b] * behind[b]
        outputs.append(result)
    return outputs


def fine_rates(ext, half, x, r, n):
    rows = []

    def grads_of(a):
        _, ahead, behind = sides(half, a, x, r, n)
        rows.append([ahead[b] - behind[b] for b in range(3)])
        return rows[a]

    speeds = [half[b, x, r : r + n] for b in range(3)]
    return rates(ext, x, r, n, speeds, grads_of, VISCOSITY), rows


def split(value):
    high = value.astype(BF16)
    low = (value - high.astype(F32)).astype(BF16)
    return high, low


def pair_table(rows, columns, by_row, entry):
    i = lax.broadcasted_iota(jnp.int32, (rows, columns), 0)
    j = lax.broadcasted_iota(jnp.int32, (rows, columns), 1)
    same = (i >> 1) == j if by_row else i == (j >> 1)
    return jnp.where(same, entry, 0.0).astype(BF16)


def squeeze(summed, rows, store, count):
    cx, y, z = summed.shape[1:]
    table = pair_table(z, z // 2, True, 0.125)
    for c in range(count):
        high, low = split(summed[c].reshape(cx * y, z))
        rows[...] = jnp.dot(high, table, preferred_element_type=F32) + jnp.dot(
            low, table, preferred_element_type=F32
        )
        half = cx * y // 2
        value = rows[pl.ds(0, half, stride=2)] + rows[pl.ds(1, half, stride=2)]
        store(c, value.reshape(cx, y // 2, z // 2))


def prolong(field, wide, edge, rows):
    cx, cy, cz = field.main.shape[1:]
    single = pair_table(cz, 2 * cz, False, 1.0)
    table = jnp.concatenate([single, single], axis=0)

    def along_z(value):
        high, low = split(value)
        return jnp.dot(jnp.concatenate([high, low], axis=1), table, preferred_element_type=F32)

    count = (cx + 2) * cy
    edges = []
    for c in range(3):
        layers = [field.x_faces[c, 0:1], field.main[c], field.x_faces[c, 1:2]]
        value = jnp.concatenate(layers, axis=0).reshape(count, cz)
        rows[pl.ds(0, count, stride=2)] = value
        rows[pl.ds(1, count, stride=2)] = value
        wide[c] = along_z(rows[...]).reshape(cx + 2, 2 * cy, 2 * cz)
        edges += [field.behind[c], field.ahead[c]]
    value = along_z(jnp.concatenate(edges, axis=0))
    for c in range(3):
        for k in range(2):
            at = (2 * c + k) * cx
            edge[k, c] = value[at : at + cx]


def emit_faces(main, outs, off=0):
    x_faces, y_last, y_first = outs
    width, length = main.shape[1:3]
    for c in range(3):
        x_faces[off + c, 0] = main[c, width - 1]
        x_faces[off + c, 1] = main[c, 0]
        for x in range(width):
            y_last[off + c, x : x + 1] = main[c, x, length - 1 : length]
            y_first[off + c, x : x + 1] = main[c, x, 0:1]


def quadrant(c, rows, columns):
    up, along = c // 2, c % 2
    return slice(up * rows, (up + 1) * rows), slice(along * columns, (along + 1) * columns)


def emit_coarse_faces(main, outs, comp):
    x_faces, y_last, y_first = outs
    cx, cy, cz = main.shape[1:]
    for c in range(3):
        x_faces[(comp, 0) + quadrant(c, cy, cz)] = main[c, cx - 1]
        x_faces[(comp, 1) + quadrant(c, cy, cz)] = main[c, 0]
        rows, columns = quadrant(c, cx, cz)
        for i in range(cx):
            at = slice(rows.start + i, rows.start + i + 1)
            y_last[comp, at, columns] = main[c, i, cy - 1 : cy]
            y_first[comp, at, columns] = main[c, i, 0:1]


def take_coarse_faces(x_faces, behind, ahead, comp, outs):
    out_x, out_b, out_a = outs
    cy, cz = out_x.shape[2:]
    cx = out_b.shape[1]
    for c in range(3):
        for k in range(2):
            out_x[c, k] = x_faces[(comp, k) + quadrant(c, cy, cz)]
        out_b[c] = behind[(comp,) + quadrant(c, cx, cz)]
        out_a[c] = ahead[(comp,) + quadrant(c, cx, cz)]


def coarsen(field, summed, rows, store):
    @pl.loop(0, field.shape[1] // 2)
    def _(i):
        for c in range(3):
            summed[c, i] = field[c, 2 * i] + field[c, 2 * i + 1]

    squeeze(summed, rows, store, 3)


def pack_kernel(first, v, s, g, end, x_faces, y_last, y_first, summed, rows):
    outs = (x_faces, y_last, y_first)
    for k, field in enumerate((v, g, s)):
        emit_faces(field, outs, 3 * k)

    def store(c, value):
        end[c] = value

    coarsen(g, summed, rows, store)
    emit_coarse_faces(end, outs, 9)


def coarsen_kernel(first, v, s, end, speed, zero, summed, rows):
    f = first[0]

    def store_zero(c, value):
        zero[c] = f * value + (1.0 - f) * end[c]

    def store_speed(c, value):
        speed[c] = value * 0.25

    coarsen(s, summed, rows, store_zero)
    coarsen(v, summed, rows, store_speed)


def integral_loop(ext, half, summed, grads_summed):
    width, length = ext.shape[1] - 2, ext.shape[2] - 2 * PAD
    n = min(CHUNK, length)

    @pl.loop(0, width // 2)
    def _(i):
        for r in range(0, length, n):
            pair = [fine_rates(ext, half, 2 * i + 1 + q, PAD + r, n) for q in range(2)]
            for a in range(3):
                summed[a, i, r : r + n] = pair[0][0][a] + pair[1][0][a]
                if grads_summed is not None:
                    for b in range(3):
                        value = pair[0][1][a][b] + pair[1][1][a][b]
                        grads_summed[3 * a + b, i, r : r + n] = value


def offset_start_kernel(
    first, v, s, g, x_faces, behind, ahead, zero,
    integral, coarse_grads, zero_x, zero_b, zero_a, end, end_x, end_l, end_f,
    ext, half, summed, grads_summed, rows,
):
    f = first[0]
    fill(half, [(0.5, Node(v, x_faces, behind, ahead))])
    start = Node(s, x_faces, behind, ahead, 6)
    guess = Node(g, x_faces, behind, ahead, 3)
    share = f * (TIME_STEP / 6.0)
    fill(ext, [(share, start), (TIME_STEP - share, guess)])
    integral_loop(ext, half, summed, grads_summed)

    def store(c, value):
        integral[c] = value
        end[c] = zero[c] + value

    squeeze(summed, rows, store, 3)
    emit_faces(end, (end_x, end_l, end_f))
    take_coarse_faces(x_faces, behind, ahead, 9, (zero_x, zero_b, zero_a))

    def store_grads(c, value):
        coarse_grads[c] = value

    squeeze(grads_summed, rows, store_grads, 9)


def offset_later_kernel(
    first, v, s, x_faces, behind, ahead,
    u0, u0_x, u0_b, u0_a, u1, u1_x, u1_b, u1_a, u2, u2_x, u2_b, u2_a,
    integral, zero, zero_x, zero_b, zero_a, end, end_x, end_l, end_f,
    ext, half, summed, rows,
):
    f = first[0]
    fill(half, [(0.5, Node(v, x_faces, behind, ahead))])
    sixth = TIME_STEP / 6.0
    fill(
        ext,
        [
            (f * sixth, Node(s, x_faces, behind, ahead, 6)),
            (sixth, Node(u0, u0_x, u0_b, u0_a)),
            (TIME_STEP * 2.0 / 3.0, Node(u1, u1_x, u1_b, u1_a)),
            (sixth, Node(u2, u2_x, u2_b, u2_a)),
        ],
    )

    @pl.loop(0, s.shape[1] // 2)
    def _(i):
        for c in range(3):
            summed[c, i] = f * (s[c, 2 * i] + s[c, 2 * i + 1]) + (u0[c, 2 * i] + u0[c, 2 * i + 1])

    def store_zero(c, value):
        zero[c] = value

    squeeze(summed, rows, store_zero, 3)
    integral_loop(ext, half, summed, None)

    def store(c, value):
        integral[c] = value
        end[c] = zero[c] + value

    squeeze(summed, rows, store, 3)
    emit_faces(end, (end_x, end_l, end_f))
    take_coarse_faces(u0_x, u0_b, u0_a, 3, (zero_x, zero_b, zero_a))


def chain_step(rest, arrived, zero, integral, speed, coarse_grads, d0, ext, store):
    for k in range(4):
        d0[k][...] = rest * (total([group[k][...] for group in arrived]) - zero[k][...])
    fill(ext, [(TIME_STEP, Node(*d0))], unrolled=True)
    width, length = zero[0].shape[1:3]
    for x in range(width):
        speeds = [speed[b, x] for b in range(3)]

        def grads_of(a):
            return [coarse_grads[3 * a + b, x] for b in range(3)]

        changes = rates(ext, x + 1, PAD, length, speeds, grads_of, VISCOSITY / 4.0)
        for a in range(3):
            store(a, x, zero[0][a, x] + d0[0][a, x] + integral[a, x] + changes[a])


def pass_kernel(turn, first, *refs):
    arrived, zero = refs[:4], refs[4:8]
    integral, speed, coarse_grads, end, end_x, end_l, end_f = refs[8:15]
    d0, ext = refs[15:19], refs[19]

    @pl.when(first[1] == float(turn))
    def _():
        def store(a, x, value):
            end[a, x] = value

        chain_step(1.0, [arrived], zero, integral, speed, coarse_grads, d0, ext, store)
        emit_faces(end, (end_x, end_l, end_f))


def settle_kernel(count, first, *refs):
    arrived = [refs[4 * k : 4 * k + 4] for k in range(count)]
    refs = refs[4 * count :]
    zero, (integral, speed, coarse_grads, end_two) = refs[:4], refs[4:8]
    d0, (d2, d2_x, d2_l, d2_f, ext) = refs[8:12], refs[12:17]

    def store(a, x, value):
        d2[a, x] = value - end_two[a, x]

    chain_step(1.0 - first[0], arrived, zero, integral, speed, coarse_grads, d0, ext, store)
    emit_faces(d2, (d2_x, d2_l, d2_f))


def middle_kernel(nodes, *refs):
    first, v, vx, vb, va = refs[:5]
    at = 5
    parts = []
    for _, _, _, own, off in nodes:
        main = refs[at]
        at += 1
        if own:
            x_faces, behind, ahead = refs[at : at + 3]
            at += 3
        else:
            x_faces, behind, ahead = vx, vb, va
        parts.append(Node(main, x_faces, behind, ahead, off))
    d0 = Node(*refs[at : at + 4])
    d2 = Node(*refs[at + 4 : at + 8])
    a1, a1_x, a1_l, a1_f, rest, rest_x, rest_b, rest_a = refs[at + 8 : at + 16]
    ext, half, wide0, edge0, wide2, edge2, rows = refs[at + 16 :]
    f = first[0]
    begin, first_stage, second_stage = [
        [(spec[k][0] * f + spec[k][1], node) for spec, node in zip(nodes, parts)] for k in range(3)
    ]
    fill(half, [(0.5, Node(v, vx, vb, va))])
    prolong(d0, wide0, edge0, rows)
    prolong(d2, wide2, edge2, rows)
    fill(
        ext,
        [(TIME_STEP * w, node) for w, node in first_stage],
        [(TIME_STEP * 0.375, wide0, edge0), (TIME_STEP * 0.125, wide2, edge2)],
    )
    width, length = a1.shape[1:3]
    n = min(CHUNK, length)
    last_cx = width // 2 + 1

    def rest_of(get, p0, p2):
        return total([w * get(node) for w, node in second_stage]) + 0.125 * (p2 - p0)

    for c in range(3):
        for k in range(2):
            rest_x[c, k] = rest_of(
                lambda nd: nd.x_faces[nd.off + c, k], wide0[c, k * last_cx], wide2[c, k * last_cx]
            )

    @pl.loop(0, width // 2)
    def _(i):
        for q in range(2):
            x = 2 * i + q
            row = pl.ds(x, 1)
            for r in range(0, length, n):
                changes, _ = fine_rates(ext, half, x + 1, PAD + r, n)
                for a in range(3):
                    p0, p2 = wide0[a, i + 1, r : r + n], wide2[a, i + 1, r : r + n]
                    start = total([w * nd.main[a, x, r : r + n] for w, nd in begin])
                    a1[a, x, r : r + n] = start + p0 + changes[a]
                    rest[a, x, r : r + n] = rest_of(lambda nd: nd.main[a, x, r : r + n], p0, p2)
            for c in range(3):
                p0, p2 = edge0[0, c, pl.ds(i, 1)], edge2[0, c, pl.ds(i, 1)]
                rest_b[c, row] = rest_of(lambda nd: nd.behind[nd.off + c, row], p0, p2)
                p0, p2 = edge0[1, c, pl.ds(i, 1)], edge2[1, c, pl.ds(i, 1)]
                rest_a[c, row] = rest_of(lambda nd: nd.ahead[nd.off + c, row], p0, p2)

    emit_faces(a1, (a1_x, a1_l, a1_f))


def finish_kernel(last, first, v, vx, vb, va, a1, a1_x, a1_b, a1_a, rest, rest_x, rest_b, rest_a, *refs):
    if last:
        a2, ext, half = refs
    else:
        a2, a2_x, a2_l, a2_f, end, ext, half, summed, rows = refs
    fill(half, [(0.5, Node(v, vx, vb, va))])
    fill(
        ext,
        [
            (TIME_STEP * 0.5, Node(a1, a1_x, a1_b, a1_a)),
            (TIME_STEP, Node(rest, rest_x, rest_b, rest_a)),
        ],
    )
    width, length = a1.shape[1:3]
    n = min(CHUNK, length)

    @pl.loop(0, width // 2)
    def _(i):
        for r in range(0, length, n):
            pair = []
            for q in range(2):
                x = 2 * i + q
                changes, _ = fine_rates(ext, half, x + 1, PAD + r, n)
                pair.append([a1[a, x, r : r + n] + changes[a] for a in range(3)])
                for a in range(3):
                    a2[a, x, r : r + n] = pair[q][a]
            if not last:
                for a in range(3):
                    summed[a, i, r : r + n] = pair[0][a] + pair[1][a]

    if not last:
        emit_faces(a2, (a2_x, a2_l, a2_f))

        def store(c, value):
            end[c] = value

        squeeze(summed, rows, store, 3)
        emit_coarse_faces(end, (a2_x, a2_l, a2_f), 3)


def call(kernel, name, first, args, outs, scratch, flops=0):
    moved = sum(4 * a.size for a in args)
    return pl.pallas_call(
        kernel,
        name=name,
        out_shape=[jax.ShapeDtypeStruct(dims, F32) for dims in outs],
        in_specs=[pl.BlockSpec(memory_space=pltpu.SMEM)] + [pl.BlockSpec(memory_space=pltpu.VMEM)] * len(args),
        out_specs=[pl.BlockSpec(memory_space=pltpu.VMEM)] * len(outs),
        scratch_shapes=[pltpu.VMEM(dims, F32) for dims in scratch],
        compiler_params=pltpu.CompilerParams(vmem_limit_bytes=56 << 20),
        cost_estimate=pl.CostEstimate(flops=flops, bytes_accessed=moved, transcendentals=0),
    )(first, *args)


def shards(velocity, start_field, guess):
    own = guess[0]
    _, nx, ny, nz = own.shape
    cx, cy, cz = nx // 2, ny // 2, nz // 2
    slabs = lax.axis_size("tm")
    number = lax.axis_index("tm")
    first = jnp.stack([number == 0, number]).astype(F32)

    def layers_of(count):
        return [(count, 2, ny, nz), (count, nx, nz), (count, nx, nz)]

    fine, coarse = (3, nx, ny, nz), (3, cx, cy, cz)
    fine_faces, coarse_faces = layers_of(3), [(3, 2, cy, cz), (3, cx, cz), (3, cx, cz)]
    ext = (3, nx + 2, ny + 2 * PAD, nz)
    coarse_ext = (3, cx + 2, cy + 2 * PAD, cz)
    summed, rows = (3, cx, ny, nz), (cx * ny, cz)
    wide, edge, wide_rows = (3, cx + 2, ny, nz), (2, 3, cx, nz), ((cx + 2) * ny, cz)

    end_two, *packed = call(
        pack_kernel, "pack", first, [velocity, start_field, own],
        [coarse] + layers_of(10), [summed, rows], 5_000_000,
    )
    layers = swap_faces(packed)
    speed, zero = call(
        coarsen_kernel, "coarsen", first, [velocity, start_field, end_two],
        [coarse, coarse], [summed, rows], 10_000_000,
    )
    integral, coarse_grads, *results = call(
        offset_start_kernel, "offset_start", first, [velocity, start_field, own, *layers, zero],
        [coarse, (9, cx, cy, cz)] + coarse_faces + [coarse] + coarse_faces,
        [ext, ext, summed, (9, cx, ny, nz), rows], 40_000_000,
    )
    zero_faces, end, sent = results[:3], results[3], results[4:]
    for sweep_index in range(ITERS):
        final = sweep_index + 1 == ITERS
        arrivals = []
        for turn in range(1, slabs):
            arrivals.append(hand_on([turn - 1], end, sent))
            if turn + 1 < slabs:
                end, *sent = call(
                    lambda *refs, turn=turn: pass_kernel(turn, *refs), "chain", first,
                    [*arrivals[-1], zero, *zero_faces, integral, speed, coarse_grads],
                    [coarse] + coarse_faces, [coarse, *coarse_faces, coarse_ext], 2_000_000,
                )
        results = call(
            lambda *refs, count=len(arrivals): settle_kernel(count, *refs), "settle", first,
            [a for group in arrivals for a in group]
            + [zero, *zero_faces, integral, speed, coarse_grads, end_two],
            [coarse] + coarse_faces + [coarse] + coarse_faces, [coarse_ext], 2_000_000,
        )
        d0, d2 = list(results[:4]), [results[4], *swap_faces(results[5:])]

        if sweep_index == 0:
            nodes = (
                ((1.0, 0.0), (5.0 / 24.0, 0.0), (-1.0 / 24.0, 0.0), False, 6),
                ((-1.0, 1.0), (-5.0 / 24.0, 0.5), (1.0 / 24.0, 0.0), False, 3),
            )
            args = [start_field, own]
        else:
            nodes = (
                ((1.0, 0.0), (5.0 / 24.0, 0.0), (-1.0 / 24.0, 0.0), False, 6),
                ((0.0, 1.0), (0.0, 5.0 / 24.0), (0.0, -1.0 / 24.0), True, 0),
                ((0.0, 0.0), (0.0, 1.0 / 3.0), (0.0, -1.0 / 6.0), True, 0),
                ((0.0, 0.0), (0.0, -1.0 / 24.0), (0.0, 5.0 / 24.0), True, 0),
            )
            args = [start_field, *u0, *u1, *u2]
        middle, m_x, m_l, m_f, *rest = call(
            lambda *refs, nodes=nodes: middle_kernel(nodes, *refs),
            "middle", first, [velocity, *layers, *args, *d0, *d2],
            [fine] + fine_faces + [fine] + fine_faces,
            [ext, ext, wide, edge, wide, edge, wide_rows], 60_000_000,
        )
        u1 = [middle, *swap_faces((m_x, m_l, m_f))]
        results = call(
            lambda *refs, final=final: finish_kernel(final, *refs),
            "finish", first, [velocity, *layers, *u1, *rest],
            [fine] if final else [fine] + layers_of(4) + [coarse],
            [ext, ext] if final else [ext, ext, summed, rows], 40_000_000,
        )
        if final:
            return results[0][None]
        value, *faces = results[:4]
        end_two = results[4]
        u0 = hand_on(range(slabs - 1), value, faces)
        u2 = [value, *swap_faces(faces)]
        integral, zero, *results = call(
            offset_later_kernel, "offset_later", first,
            [velocity, start_field, *layers, *u0, *u1, *u2],
            [coarse, coarse] + coarse_faces + [coarse] + coarse_faces,
            [ext, ext, summed, rows], 40_000_000,
        )
        zero_faces, end, sent = results[:3], results[3], results[4:]


def solution(mesh):
    in_specs = (
        P(None, "gx", "gy", None),
        P(None, "gx", "gy", None),
        P("tm", None, "gx", "gy", None),
    )
    out_specs = P("tm", None, "gx", "gy", None)
    return jax.shard_map(shards, mesh=mesh, in_specs=in_specs, out_specs=out_specs, check_vma=False)
```

```python
import jax
import jax.numpy as jnp
from jax import lax
from jax.experimental import pallas as pl
from jax.experimental.pallas import tpu as pltpu
from jax.sharding import PartitionSpec as P

ITERS = 2
VISCOSITY = 0.25
TIME_STEP = 0.5
PAD = 8
CHUNK = 8
F32 = jnp.float32
BF16 = jnp.bfloat16


def ring(size, by):
    return [(i, (i + by) % size) for i in range(size)]


def both_faces(faces, permute, size):
    if size == 2:
        return permute(faces, 1)
    before = permute(faces[:, 0:1], 1)
    after = permute(faces[:, 1:2], -1)
    return jnp.concatenate([before, after], axis=1)


def swap_faces(faces):
    x_faces, y_last, y_first = faces
    gx, gy = lax.axis_size("gx"), lax.axis_size("gy")
    before_after = both_faces(x_faces, lambda a, by: lax.ppermute(a, "gx", ring(gx, by)), gx)
    behind = lax.ppermute(y_last, "gy", ring(gy, 1))
    ahead = lax.ppermute(y_first, "gy", ring(gy, -1))
    return before_after, behind, ahead


def hand_on(slabs, value, faces):
    gx, gy = lax.axis_size("gx"), lax.axis_size("gy")

    def permute(array, dx, dy):
        pairs = []
        for t in slabs:
            for x in range(gx):
                for y in range(gy):
                    source = (t * gx + x) * gy + y
                    target = ((t + 1) * gx + (x + dx) % gx) * gy + (y + dy) % gy
                    pairs.append((source, target))
        return lax.ppermute(array, ("tm", "gx", "gy"), pairs)

    moved = [] if value is None else [permute(value, 0, 0)]
    x_faces, y_last, y_first = faces
    moved.append(both_faces(x_faces, lambda a, by: permute(a, by, 0), gx))
    moved.append(permute(y_last, 0, 1))
    moved.append(permute(y_first, 0, -1))
    return moved


class Node:
    def __init__(self, main, x_faces, behind, ahead, off=0):
        self.main, self.x_faces, self.behind, self.ahead, self.off = main, x_faces, behind, ahead, off


def total(terms):
    result = terms[0]
    for term in terms[1:]:
        result = result + term
    return result


def each(count, unrolled=False):
    def wrap(body):
        if unrolled:
            for i in range(count):
                body(i)
        else:
            pl.loop(0, count)(body)

    return wrap


def fill(ext, parts, spread=(), unrolled=False):
    width, length = ext.shape[1] - 2, ext.shape[2] - 2 * PAD
    inner = slice(PAD, PAD + length)
    for c in range(3):
        for k, at in ((0, 0), (1, width + 1)):
            terms = [w * n.x_faces[n.off + c, k] for w, n in parts]
            terms += [w * p[c, k * (width // 2 + 1)] for w, p, _ in spread]
            ext[c, at, inner] = total(terms)

    @each(width // 2, unrolled)
    def _(i):
        for q in range(2):
            x = 2 * i + q
            for c in range(3):
                terms = [w * n.main[c, x] for w, n in parts]
                terms += [w * p[c, i + 1] for w, p, _ in spread]
                ext[c, x + 1, inner] = total(terms)
                row = pl.ds(x, 1)
                for k, at in ((0, PAD - 1), (1, PAD + length)):
                    terms = [w * (n.ahead if k else n.behind)[n.off + c, row] for w, n in parts]
                    terms += [w * e[k, c, pl.ds(i, 1)] for w, _, e in spread]
                    ext[c, x + 1, at : at + 1] = total(terms)


def turned(value, by):
    return pltpu.roll(value, by % value.shape[-1], value.ndim - 1)


def sides(ext, c, x, r, n):
    here = ext[c, x, r : r + n]
    return (
        here,
        (ext[c, x + 1, r : r + n], ext[c, x, r + 1 : r + 1 + n], turned(here, -1)),
        (ext[c, x - 1, r : r + n], ext[c, x, r - 1 : r - 1 + n], turned(here, 1)),
    )


def rates(ext, x, r, n, speeds, grads_of, strength):
    here = [ext[b, x, r : r + n] for b in range(3)]
    toward = [strength - speed for speed in speeds]
    away = [strength + speed for speed in speeds]
    outputs = []
    for a in range(3):
        _, ahead, behind = sides(ext, a, x, r, n)
        grads = grads_of(a)
        result = here[a] * (grads[a] - 6.0 * strength)
        for b in range(3):
            if b != a:
                result = result + here[b] * grads[b]
            result = result + toward[b] * ahead[b] + away[b] * behind[b]
        outputs.append(result)
    return outputs


def fine_rates(ext, half, x, r, n):
    rows = []

    def grads_of(a):
        _, ahead, behind = sides(half, a, x, r, n)
        rows.append([ahead[b] - behind[b] for b in range(3)])
        return rows[a]

    speeds = [half[b, x, r : r + n] for b in range(3)]
    return rates(ext, x, r, n, speeds, grads_of, VISCOSITY), rows


def split(value):
    high = value.astype(BF16)
    low = (value - high.astype(F32)).astype(BF16)
    return high, low


def pair_table(rows, columns, by_row, entry):
    i = lax.broadcasted_iota(jnp.int32, (rows, columns), 0)
    j = lax.broadcasted_iota(jnp.int32, (rows, columns), 1)
    same = (i >> 1) == j if by_row else i == (j >> 1)
    return jnp.where(same, entry, 0.0).astype(BF16)


def squeeze(summed, rows, store, count):
    cx, y, z = summed.shape[1:]
    table = pair_table(z, z // 2, True, 0.125)
    for c in range(count):
        high, low = split(summed[c].reshape(cx * y, z))
        rows[...] = jnp.dot(high, table, preferred_element_type=F32) + jnp.dot(
            low, table, preferred_element_type=F32
        )
        half = cx * y // 2
        value = rows[pl.ds(0, half, stride=2)] + rows[pl.ds(1, half, stride=2)]
        store(c, value.reshape(cx, y // 2, z // 2))


def prolong(field, wide, edge, rows):
    cx, cy, cz = field.main.shape[1:]
    single = pair_table(cz, 2 * cz, False, 1.0)
    table = jnp.concatenate([single, single], axis=0)

    def along_z(value):
        high, low = split(value)
        return jnp.dot(jnp.concatenate([high, low], axis=1), table, preferred_element_type=F32)

    count = (cx + 2) * cy
    edges = []
    for c in range(3):
        layers = [field.x_faces[c, 0:1], field.main[c], field.x_faces[c, 1:2]]
        value = jnp.concatenate(layers, axis=0).reshape(count, cz)
        rows[pl.ds(0, count, stride=2)] = value
        rows[pl.ds(1, count, stride=2)] = value
        wide[c] = along_z(rows[...]).reshape(cx + 2, 2 * cy, 2 * cz)
        edges += [field.behind[c], field.ahead[c]]
    value = along_z(jnp.concatenate(edges, axis=0))
    for c in range(3):
        for k in range(2):
            at = (2 * c + k) * cx
            edge[k, c] = value[at : at + cx]


def emit_faces(main, outs, off=0):
    x_faces, y_last, y_first = outs
    width, length = main.shape[1:3]
    for c in range(3):
        x_faces[off + c, 0] = main[c, width - 1]
        x_faces[off + c, 1] = main[c, 0]
        for x in range(width):
            y_last[off + c, x : x + 1] = main[c, x, length - 1 : length]
            y_first[off + c, x : x + 1] = main[c, x, 0:1]


def quadrant(c, rows, columns):
    up, along = c // 2, c % 2
    return slice(up * rows, (up + 1) * rows), slice(along * columns, (along + 1) * columns)


def emit_coarse_faces(main, outs, comp):
    x_faces, y_last, y_first = outs
    cx, cy, cz = main.shape[1:]
    for c in range(3):
        x_faces[(comp, 0) + quadrant(c, cy, cz)] = main[c, cx - 1]
        x_faces[(comp, 1) + quadrant(c, cy, cz)] = main[c, 0]
        rows, columns = quadrant(c, cx, cz)
        for i in range(cx):
            at = slice(rows.start + i, rows.start + i + 1)
            y_last[comp, at, columns] = main[c, i, cy - 1 : cy]
            y_first[comp, at, columns] = main[c, i, 0:1]


def take_coarse_faces(x_faces, behind, ahead, comp, outs):
    out_x, out_b, out_a = outs
    cy, cz = out_x.shape[2:]
    cx = out_b.shape[1]
    for c in range(3):
        for k in range(2):
            out_x[c, k] = x_faces[(comp, k) + quadrant(c, cy, cz)]
        out_b[c] = behind[(comp,) + quadrant(c, cx, cz)]
        out_a[c] = ahead[(comp,) + quadrant(c, cx, cz)]


def coarsen(field, summed, rows, store):
    @pl.loop(0, field.shape[1] // 2)
    def _(i):
        for c in range(3):
            summed[c, i] = field[c, 2 * i] + field[c, 2 * i + 1]

    squeeze(summed, rows, store, 3)


def pack_kernel(feed, first, g, v, s, end, x_faces, y_last, y_first, summed, rows):
    outs = (x_faces, y_last, y_first)

    def store(c, value):
        end[c] = value

    feed.need(g)
    coarsen(g, summed, rows, store)
    emit_coarse_faces(end, outs, 9)
    for k, field in enumerate((v, g, s)):
        feed.need(field)
        emit_faces(field, outs, 3 * k)


def coarsen_kernel(feed, first, v, s, end, speed, zero, summed, rows):
    f = first[0]

    def store_zero(c, value):
        zero[c] = f * value + (1.0 - f) * end[c]

    def store_speed(c, value):
        speed[c] = value * 0.25

    feed.need(s, end)
    coarsen(s, summed, rows, store_zero)
    feed.need(v)
    coarsen(v, summed, rows, store_speed)


def integral_loop(ext, half, summed, grads_summed):
    width, length = ext.shape[1] - 2, ext.shape[2] - 2 * PAD
    n = min(CHUNK, length)

    @pl.loop(0, width // 2)
    def _(i):
        for r in range(0, length, n):
            pair = [fine_rates(ext, half, 2 * i + 1 + q, PAD + r, n) for q in range(2)]
            for a in range(3):
                summed[a, i, r : r + n] = pair[0][0][a] + pair[1][0][a]
                if grads_summed is not None:
                    for b in range(3):
                        value = pair[0][1][a][b] + pair[1][1][a][b]
                        grads_summed[3 * a + b, i, r : r + n] = value


def offset_start_kernel(
    feed, first, v, s, g, x_faces, behind, ahead, zero,
    integral, coarse_grads, zero_x, zero_b, zero_a, end, end_x, end_l, end_f,
    ext, half, summed, grads_summed, rows,
):
    f = first[0]
    feed.need(v, x_faces, behind, ahead)
    fill(half, [(0.5, Node(v, x_faces, behind, ahead))])
    feed.need(s, g)
    start = Node(s, x_faces, behind, ahead, 6)
    guess = Node(g, x_faces, behind, ahead, 3)
    share = f * (TIME_STEP / 6.0)
    fill(ext, [(share, start), (TIME_STEP - share, guess)])
    integral_loop(ext, half, summed, grads_summed)

    feed.need(zero)

    def store(c, value):
        integral[c] = value
        end[c] = zero[c] + value

    squeeze(summed, rows, store, 3)
    emit_faces(end, (end_x, end_l, end_f))
    take_coarse_faces(x_faces, behind, ahead, 9, (zero_x, zero_b, zero_a))
    feed.send(integral, end, end_x, end_l, end_f, zero_x, zero_b, zero_a)

    def store_grads(c, value):
        coarse_grads[c] = value

    squeeze(grads_summed, rows, store_grads, 9)


def offset_later_kernel(
    feed, first, v, s, x_faces, behind, ahead,
    u0, u0_x, u0_b, u0_a, u1, u1_x, u1_b, u1_a, u2, u2_x, u2_b, u2_a,
    integral, zero, zero_x, zero_b, zero_a, end, end_x, end_l, end_f,
    ext, half, summed, rows,
):
    f = first[0]
    feed.need(v, x_faces, behind, ahead)
    fill(half, [(0.5, Node(v, x_faces, behind, ahead))])
    feed.need(s, u1, u1_x, u1_b, u1_a, u2, u2_x, u2_b, u2_a, u0, u0_x, u0_b, u0_a)
    sixth = TIME_STEP / 6.0
    fill(
        ext,
        [
            (f * sixth, Node(s, x_faces, behind, ahead, 6)),
            (sixth, Node(u0, u0_x, u0_b, u0_a)),
            (TIME_STEP * 2.0 / 3.0, Node(u1, u1_x, u1_b, u1_a)),
            (sixth, Node(u2, u2_x, u2_b, u2_a)),
        ],
    )

    @pl.loop(0, s.shape[1] // 2)
    def _(i):
        for c in range(3):
            summed[c, i] = f * (s[c, 2 * i] + s[c, 2 * i + 1]) + (u0[c, 2 * i] + u0[c, 2 * i + 1])

    def store_zero(c, value):
        zero[c] = value

    squeeze(summed, rows, store_zero, 3)
    integral_loop(ext, half, summed, None)

    def store(c, value):
        integral[c] = value
        end[c] = zero[c] + value

    squeeze(summed, rows, store, 3)
    emit_faces(end, (end_x, end_l, end_f))
    take_coarse_faces(u0_x, u0_b, u0_a, 3, (zero_x, zero_b, zero_a))


def chain_step(rest, arrived, zero, integral, speed, coarse_grads, d0, ext, store):
    for k in range(4):
        d0[k][...] = rest * (total([group[k][...] for group in arrived]) - zero[k][...])
    fill(ext, [(TIME_STEP, Node(*d0))], unrolled=True)
    width, length = zero[0].shape[1:3]
    for x in range(width):
        speeds = [speed[b, x] for b in range(3)]

        def grads_of(a):
            return [coarse_grads[3 * a + b, x] for b in range(3)]

        changes = rates(ext, x + 1, PAD, length, speeds, grads_of, VISCOSITY / 4.0)
        for a in range(3):
            store(a, x, zero[0][a, x] + d0[0][a, x] + integral[a, x] + changes[a])


def pass_kernel(feed, first, *refs):
    arrived, zero = refs[:4], refs[4:8]
    integral, speed, coarse_grads, end, end_x, end_l, end_f = refs[8:15]
    d0, ext = refs[15:19], refs[19]

    def store(a, x, value):
        end[a, x] = value

    feed.need(*arrived, *zero, integral, speed, coarse_grads)
    chain_step(1.0, [arrived], zero, integral, speed, coarse_grads, d0, ext, store)
    emit_faces(end, (end_x, end_l, end_f))


def settle_kernel(count, feed, first, *refs):
    arrived = [refs[4 * k : 4 * k + 4] for k in range(count)]
    refs = refs[4 * count :]
    zero, (integral, speed, coarse_grads, end_two) = refs[:4], refs[4:8]
    d0, (d2, d2_x, d2_l, d2_f, ext) = refs[8:12], refs[12:17]

    def store(a, x, value):
        d2[a, x] = value - end_two[a, x]

    feed.need(*[a for group in arrived for a in group], *zero, integral, speed, coarse_grads, end_two)
    chain_step(1.0 - first[0], arrived, zero, integral, speed, coarse_grads, d0, ext, store)
    emit_faces(d2, (d2_x, d2_l, d2_f))


def middle_kernel(nodes, feed, *refs):
    first, (v, vx, vb, va) = refs[0], refs[9:13]
    d0, d2 = Node(*refs[1:5]), Node(*refs[5:9])
    at = 13
    parts = []
    for _, _, _, own, off in nodes:
        main = refs[at]
        at += 1
        if own:
            x_faces, behind, ahead = refs[at : at + 3]
            at += 3
        else:
            x_faces, behind, ahead = vx, vb, va
        parts.append(Node(main, x_faces, behind, ahead, off))
    a1, a1_x, a1_l, a1_f, rest, rest_x, rest_b, rest_a = refs[at : at + 8]
    ext, half, wide0, edge0, wide2, edge2, rows = refs[at + 8 :]
    f = first[0]
    begin, first_stage, second_stage = [
        [(spec[k][0] * f + spec[k][1], node) for spec, node in zip(nodes, parts)] for k in range(3)
    ]
    feed.need_nodes(d0, d2)
    prolong(d0, wide0, edge0, rows)
    prolong(d2, wide2, edge2, rows)
    feed.need(v, vx, vb, va)
    fill(half, [(0.5, Node(v, vx, vb, va))])
    feed.need_nodes(*parts)
    fill(
        ext,
        [(TIME_STEP * w, node) for w, node in first_stage],
        [(TIME_STEP * 0.375, wide0, edge0), (TIME_STEP * 0.125, wide2, edge2)],
    )
    width, length = a1.shape[1:3]
    n = min(CHUNK, length)
    last_cx = width // 2 + 1

    def rest_of(get, p0, p2):
        return total([w * get(node) for w, node in second_stage]) + 0.125 * (p2 - p0)

    for c in range(3):
        for k in range(2):
            rest_x[c, k] = rest_of(
                lambda nd: nd.x_faces[nd.off + c, k], wide0[c, k * last_cx], wide2[c, k * last_cx]
            )

    @pl.loop(0, width // 2)
    def _(i):
        for q in range(2):
            x = 2 * i + q
            row = pl.ds(x, 1)
            for r in range(0, length, n):
                changes, _ = fine_rates(ext, half, x + 1, PAD + r, n)
                for a in range(3):
                    p0, p2 = wide0[a, i + 1, r : r + n], wide2[a, i + 1, r : r + n]
                    start = total([w * nd.main[a, x, r : r + n] for w, nd in begin])
                    a1[a, x, r : r + n] = start + p0 + changes[a]
                    rest[a, x, r : r + n] = rest_of(lambda nd: nd.main[a, x, r : r + n], p0, p2)
            for c in range(3):
                p0, p2 = edge0[0, c, pl.ds(i, 1)], edge2[0, c, pl.ds(i, 1)]
                rest_b[c, row] = rest_of(lambda nd: nd.behind[nd.off + c, row], p0, p2)
                p0, p2 = edge0[1, c, pl.ds(i, 1)], edge2[1, c, pl.ds(i, 1)]
                rest_a[c, row] = rest_of(lambda nd: nd.ahead[nd.off + c, row], p0, p2)

    emit_faces(a1, (a1_x, a1_l, a1_f))


def finish_kernel(last, feed, first, v, vx, vb, va, a1, a1_x, a1_b, a1_a, rest, rest_x, rest_b, rest_a, *refs):
    if last:
        a2, ext, half = refs
    else:
        a2, a2_x, a2_l, a2_f, end, ext, half, summed, rows = refs
    feed.need(v, vx, vb, va)
    fill(half, [(0.5, Node(v, vx, vb, va))])
    feed.need(a1, a1_x, a1_b, a1_a, rest, rest_x, rest_b, rest_a)
    fill(
        ext,
        [
            (TIME_STEP * 0.5, Node(a1, a1_x, a1_b, a1_a)),
            (TIME_STEP, Node(rest, rest_x, rest_b, rest_a)),
        ],
    )
    width, length = a1.shape[1:3]
    n = min(CHUNK, length)

    @pl.loop(0, width // 2)
    def _(i):
        for r in range(0, length, n):
            pair = []
            for q in range(2):
                x = 2 * i + q
                changes, _ = fine_rates(ext, half, x + 1, PAD + r, n)
                pair.append([a1[a, x, r : r + n] + changes[a] for a in range(3)])
                for a in range(3):
                    a2[a, x, r : r + n] = pair[q][a]
            if not last:
                for a in range(3):
                    summed[a, i, r : r + n] = pair[0][a] + pair[1][a]

    if not last:
        emit_faces(a2, (a2_x, a2_l, a2_f))

        def store(c, value):
            end[c] = value

        squeeze(summed, rows, store, 3)
        emit_coarse_faces(end, (a2_x, a2_l, a2_f), 3)


class Feed:
    def __init__(self, inward, outward):
        self.inward = {id(buffer): copy for buffer, copy in inward}
        self.outward = {id(buffer): copy for buffer, copy in outward}
        self.going = []
        for copy in self.inward.values():
            copy.start()

    def need(self, *buffers):
        for buffer in buffers:
            copy = self.inward.pop(id(buffer), None)
            if copy is not None:
                copy.wait()

    def need_nodes(self, *nodes):
        for node in nodes:
            self.need(node.main, node.x_faces, node.behind, node.ahead)

    def send(self, *buffers):
        for buffer in buffers:
            copy = self.outward.pop(id(buffer), None)
            if copy is not None:
                copy.start()
                self.going.append(copy)

    def finish(self):
        for copy in self.inward.values():
            copy.wait()
        for copy in self.outward.values():
            copy.start()
        for copy in self.going + list(self.outward.values()):
            copy.wait()


def call(kernel, name, first, args, outs, scratch, flops=0, turn=None):
    n_in, n_out = len(args), len(outs)
    moved = sum(4 * a.size for a in args)

    def body(first_ref, *refs):
        sources, refs = refs[:n_in], refs[n_in:]
        targets, refs = refs[:n_out], refs[n_out:]
        held, refs = refs[:n_in], refs[n_in:]
        made, refs = refs[:n_out], refs[n_out:]
        in_sem, out_sem = refs[-2:]

        def work():
            feed = Feed(
                [(h, pltpu.make_async_copy(s, h, in_sem.at[k])) for k, (s, h) in enumerate(zip(sources, held))],
                [(m, pltpu.make_async_copy(m, t, out_sem.at[k])) for k, (m, t) in enumerate(zip(made, targets))],
            )
            kernel(feed, first_ref, *held, *made, *refs[:-2])
            feed.finish()

        if turn is None:
            work()
        else:
            pl.when(first_ref[1] == float(turn))(work)

    return pl.pallas_call(
        body,
        name=name,
        out_shape=[jax.ShapeDtypeStruct(dims, F32) for dims in outs],
        in_specs=[pl.BlockSpec(memory_space=pltpu.SMEM)] + [pl.BlockSpec(memory_space=pltpu.HBM)] * n_in,
        out_specs=[pl.BlockSpec(memory_space=pltpu.HBM)] * n_out,
        scratch_shapes=[pltpu.VMEM(a.shape, F32) for a in args]
        + [pltpu.VMEM(dims, F32) for dims in outs + scratch]
        + [pltpu.SemaphoreType.DMA((n_in,)), pltpu.SemaphoreType.DMA((n_out,))],
        compiler_params=pltpu.CompilerParams(vmem_limit_bytes=56 << 20),
        cost_estimate=pl.CostEstimate(flops=flops, bytes_accessed=moved, transcendentals=0),
    )(first, *args)


def shards(velocity, start_field, guess):
    own = guess[0]
    _, nx, ny, nz = own.shape
    cx, cy, cz = nx // 2, ny // 2, nz // 2
    slabs = lax.axis_size("tm")
    number = lax.axis_index("tm")
    first = jnp.stack([number == 0, number]).astype(F32)

    def layers_of(count):
        return [(count, 2, ny, nz), (count, nx, nz), (count, nx, nz)]

    fine, coarse = (3, nx, ny, nz), (3, cx, cy, cz)
    fine_faces, coarse_faces = layers_of(3), [(3, 2, cy, cz), (3, cx, cz), (3, cx, cz)]
    ext = (3, nx + 2, ny + 2 * PAD, nz)
    coarse_ext = (3, cx + 2, cy + 2 * PAD, cz)
    summed, rows = (3, cx, ny, nz), (cx * ny, cz)
    wide, edge, wide_rows = (3, cx + 2, ny, nz), (2, 3, cx, nz), ((cx + 2) * ny, cz)

    end_two, *packed = call(
        pack_kernel, "pack", first, [own, velocity, start_field],
        [coarse] + layers_of(10), [summed, rows], 5_000_000,
    )
    layers = swap_faces(packed)
    speed, zero = call(
        coarsen_kernel, "coarsen", first, [velocity, start_field, end_two],
        [coarse, coarse], [summed, rows], 10_000_000,
    )
    integral, coarse_grads, *results = call(
        offset_start_kernel, "offset_start", first, [velocity, start_field, own, *layers, zero],
        [coarse, (9, cx, cy, cz)] + coarse_faces + [coarse] + coarse_faces,
        [ext, ext, summed, (9, cx, ny, nz), rows], 40_000_000,
    )
    zero_faces, end, sent = results[:3], results[3], results[4:]
    for sweep_index in range(ITERS):
        final = sweep_index + 1 == ITERS
        arrivals = []
        for turn in range(1, slabs):
            arrivals.append(hand_on([turn - 1], end, sent))
            if turn + 1 < slabs:
                end, *sent = call(
                    pass_kernel, "chain", first,
                    [*arrivals[-1], zero, *zero_faces, integral, speed, coarse_grads],
                    [coarse] + coarse_faces, [coarse, *coarse_faces, coarse_ext], 2_000_000, turn,
                )
        results = call(
            lambda *refs, count=len(arrivals): settle_kernel(count, *refs), "settle", first,
            [a for group in arrivals for a in group]
            + [zero, *zero_faces, integral, speed, coarse_grads, end_two],
            [coarse] + coarse_faces + [coarse] + coarse_faces, [coarse_ext], 2_000_000,
        )
        d0, d2 = list(results[:4]), [results[4], *swap_faces(results[5:])]

        if sweep_index == 0:
            nodes = (
                ((1.0, 0.0), (5.0 / 24.0, 0.0), (-1.0 / 24.0, 0.0), False, 6),
                ((-1.0, 1.0), (-5.0 / 24.0, 0.5), (1.0 / 24.0, 0.0), False, 3),
            )
            args = [start_field, own]
        else:
            nodes = (
                ((1.0, 0.0), (5.0 / 24.0, 0.0), (-1.0 / 24.0, 0.0), False, 6),
                ((0.0, 1.0), (0.0, 5.0 / 24.0), (0.0, -1.0 / 24.0), True, 0),
                ((0.0, 0.0), (0.0, 1.0 / 3.0), (0.0, -1.0 / 6.0), True, 0),
                ((0.0, 0.0), (0.0, -1.0 / 24.0), (0.0, 5.0 / 24.0), True, 0),
            )
            args = [start_field, *u0, *u1, *u2]
        middle, m_x, m_l, m_f, *rest = call(
            lambda *refs, nodes=nodes: middle_kernel(nodes, *refs),
            "middle", first, [*d0, *d2, velocity, *layers, *args],
            [fine] + fine_faces + [fine] + fine_faces,
            [ext, ext, wide, edge, wide, edge, wide_rows], 60_000_000,
        )
        u1 = [middle, *swap_faces((m_x, m_l, m_f))]
        results = call(
            lambda *refs, final=final: finish_kernel(final, *refs),
            "finish", first, [velocity, *layers, *u1, *rest],
            [fine] if final else [fine] + layers_of(4) + [coarse],
            [ext, ext] if final else [ext, ext, summed, rows], 40_000_000,
        )
        if final:
            return results[0][None]
        value, *faces = results[:4]
        end_two = results[4]
        u0 = hand_on(range(slabs - 1), value, faces)
        u2 = [value, *swap_faces(faces)]
        integral, zero, *results = call(
            offset_later_kernel, "offset_later", first,
            [velocity, start_field, *layers, *u0, *u1, *u2],
            [coarse, coarse] + coarse_faces + [coarse] + coarse_faces,
            [ext, ext, summed, rows], 40_000_000,
        )
        zero_faces, end, sent = results[:3], results[3], results[4:]


def solution(mesh):
    in_specs = (
        P(None, "gx", "gy", None),
        P(None, "gx", "gy", None),
        P("tm", None, "gx", "gy", None),
    )
    out_specs = P("tm", None, "gx", "gy", None)
    return jax.shard_map(shards, mesh=mesh, in_specs=in_specs, out_specs=out_specs, check_vma=False)
```

```python
import math

import jax
import jax.numpy as jnp
from jax import lax
from jax.experimental import pallas as pl
from jax.experimental.pallas import tpu as pltpu
from jax.sharding import PartitionSpec as P

ITERS = 2
VISCOSITY = 0.25
TIME_STEP = 0.5
PAD = 8
CHUNK = 8
ROOM = 4 << 20
F32 = jnp.float32
BF16 = jnp.bfloat16


def ring(size, by):
    return [(i, (i + by) % size) for i in range(size)]


def both_faces(faces, permute, size):
    if size == 2:
        return permute(faces, 1)
    before = permute(faces[:, 0:1], 1)
    after = permute(faces[:, 1:2], -1)
    return jnp.concatenate([before, after], axis=1)


def swap_faces(faces):
    x_faces, y_last, y_first = faces
    gx, gy = lax.axis_size("gx"), lax.axis_size("gy")
    before_after = both_faces(x_faces, lambda a, by: lax.ppermute(a, "gx", ring(gx, by)), gx)
    behind = lax.ppermute(y_last, "gy", ring(gy, 1))
    ahead = lax.ppermute(y_first, "gy", ring(gy, -1))
    return before_after, behind, ahead


def hand_on(slabs, value, faces):
    gx, gy = lax.axis_size("gx"), lax.axis_size("gy")

    def permute(array, dx, dy):
        pairs = []
        for t in slabs:
            for x in range(gx):
                for y in range(gy):
                    source = (t * gx + x) * gy + y
                    target = ((t + 1) * gx + (x + dx) % gx) * gy + (y + dy) % gy
                    pairs.append((source, target))
        return lax.ppermute(array, ("tm", "gx", "gy"), pairs)

    moved = [] if value is None else [permute(value, 0, 0)]
    x_faces, y_last, y_first = faces
    moved.append(both_faces(x_faces, lambda a, by: permute(a, by, 0), gx))
    moved.append(permute(y_last, 0, 1))
    moved.append(permute(y_first, 0, -1))
    return moved


class Node:
    def __init__(self, main, x_faces, behind, ahead, off=0):
        self.main, self.x_faces, self.behind, self.ahead, self.off = main, x_faces, behind, ahead, off


def total(terms):
    result = terms[0]
    for term in terms[1:]:
        result = result + term
    return result


def each(count, unrolled=False):
    def wrap(body):
        if unrolled:
            for i in range(count):
                body(i)
        else:
            pl.loop(0, count)(body)

    return wrap


def fill(ext, parts, spread=(), unrolled=False):
    width, length = ext.shape[1] - 2, ext.shape[2] - 2 * PAD
    inner = slice(PAD, PAD + length)
    for c in range(3):
        for k, at in ((0, 0), (1, width + 1)):
            terms = [w * n.x_faces[n.off + c, k] for w, n in parts]
            terms += [w * p[c, k * (width // 2 + 1)] for w, p, _ in spread]
            ext[c, at, inner] = total(terms)

    @each(width // 2, unrolled)
    def _(i):
        for q in range(2):
            x = 2 * i + q
            for c in range(3):
                terms = [w * n.main[c, x] for w, n in parts]
                terms += [w * p[c, i + 1] for w, p, _ in spread]
                ext[c, x + 1, inner] = total(terms)
                row = pl.ds(x, 1)
                for k, at in ((0, PAD - 1), (1, PAD + length)):
                    terms = [w * (n.ahead if k else n.behind)[n.off + c, row] for w, n in parts]
                    terms += [w * e[k, c, pl.ds(i, 1)] for w, _, e in spread]
                    ext[c, x + 1, at : at + 1] = total(terms)


def turned(value, by):
    return pltpu.roll(value, by % value.shape[-1], value.ndim - 1)


def sides(ext, c, x, r, n):
    here = ext[c, x, r : r + n]
    return (
        here,
        (ext[c, x + 1, r : r + n], ext[c, x, r + 1 : r + 1 + n], turned(here, -1)),
        (ext[c, x - 1, r : r + n], ext[c, x, r - 1 : r - 1 + n], turned(here, 1)),
    )


def rates(ext, x, r, n, speeds, grads_of, strength):
    here = [ext[b, x, r : r + n] for b in range(3)]
    toward = [strength - speed for speed in speeds]
    away = [strength + speed for speed in speeds]
    outputs = []
    for a in range(3):
        _, ahead, behind = sides(ext, a, x, r, n)
        grads = grads_of(a)
        result = here[a] * (grads[a] - 6.0 * strength)
        for b in range(3):
            if b != a:
                result = result + here[b] * grads[b]
            result = result + toward[b] * ahead[b] + away[b] * behind[b]
        outputs.append(result)
    return outputs


def fine_rates(ext, half, x, r, n):
    rows = []

    def grads_of(a):
        _, ahead, behind = sides(half, a, x, r, n)
        rows.append([ahead[b] - behind[b] for b in range(3)])
        return rows[a]

    speeds = [half[b, x, r : r + n] for b in range(3)]
    return rates(ext, x, r, n, speeds, grads_of, VISCOSITY), rows


def split(value):
    high = value.astype(BF16)
    low = (value - high.astype(F32)).astype(BF16)
    return high, low


def pair_table(rows, columns, by_row, entry):
    i = lax.broadcasted_iota(jnp.int32, (rows, columns), 0)
    j = lax.broadcasted_iota(jnp.int32, (rows, columns), 1)
    same = (i >> 1) == j if by_row else i == (j >> 1)
    return jnp.where(same, entry, 0.0).astype(BF16)


def squeeze(summed, rows, store, count):
    cx, y, z = summed.shape[1:]
    table = pair_table(z, z // 2, True, 0.125)
    for c in range(count):
        high, low = split(summed[c].reshape(cx * y, z))
        rows[...] = jnp.dot(high, table, preferred_element_type=F32) + jnp.dot(
            low, table, preferred_element_type=F32
        )
        half = cx * y // 2
        value = rows[pl.ds(0, half, stride=2)] + rows[pl.ds(1, half, stride=2)]
        store(c, value.reshape(cx, y // 2, z // 2))


def prolong(field, wide, edge, rows):
    cx, cy, cz = field.main.shape[1:]
    single = pair_table(cz, 2 * cz, False, 1.0)
    table = jnp.concatenate([single, single], axis=0)

    def along_z(value):
        high, low = split(value)
        return jnp.dot(jnp.concatenate([high, low], axis=1), table, preferred_element_type=F32)

    count = (cx + 2) * cy
    edges = []
    for c in range(3):
        layers = [field.x_faces[c, 0:1], field.main[c], field.x_faces[c, 1:2]]
        value = jnp.concatenate(layers, axis=0).reshape(count, cz)
        rows[pl.ds(0, count, stride=2)] = value
        rows[pl.ds(1, count, stride=2)] = value
        wide[c] = along_z(rows[...]).reshape(cx + 2, 2 * cy, 2 * cz)
        edges += [field.behind[c], field.ahead[c]]
    value = along_z(jnp.concatenate(edges, axis=0))
    for c in range(3):
        for k in range(2):
            at = (2 * c + k) * cx
            edge[k, c] = value[at : at + cx]


def emit_faces(main, outs, off=0):
    x_faces, y_last, y_first = outs
    width, length = main.shape[1:3]
    for c in range(3):
        x_faces[off + c, 0] = main[c, width - 1]
        x_faces[off + c, 1] = main[c, 0]
        for x in range(width):
            y_last[off + c, x : x + 1] = main[c, x, length - 1 : length]
            y_first[off + c, x : x + 1] = main[c, x, 0:1]


def quadrant(c, rows, columns):
    up, along = c // 2, c % 2
    return slice(up * rows, (up + 1) * rows), slice(along * columns, (along + 1) * columns)


def emit_coarse_faces(main, outs, comp):
    x_faces, y_last, y_first = outs
    cx, cy, cz = main.shape[1:]
    for c in range(3):
        x_faces[(comp, 0) + quadrant(c, cy, cz)] = main[c, cx - 1]
        x_faces[(comp, 1) + quadrant(c, cy, cz)] = main[c, 0]
        rows, columns = quadrant(c, cx, cz)
        for i in range(cx):
            at = slice(rows.start + i, rows.start + i + 1)
            y_last[comp, at, columns] = main[c, i, cy - 1 : cy]
            y_first[comp, at, columns] = main[c, i, 0:1]


def take_coarse_faces(x_faces, behind, ahead, comp, outs):
    out_x, out_b, out_a = outs
    cy, cz = out_x.shape[2:]
    cx = out_b.shape[1]
    for c in range(3):
        for k in range(2):
            out_x[c, k] = x_faces[(comp, k) + quadrant(c, cy, cz)]
        out_b[c] = behind[(comp,) + quadrant(c, cx, cz)]
        out_a[c] = ahead[(comp,) + quadrant(c, cx, cz)]


def coarsen(field, summed, rows, store):
    @pl.loop(0, field.shape[1] // 2)
    def _(i):
        for c in range(3):
            summed[c, i] = field[c, 2 * i] + field[c, 2 * i + 1]

    squeeze(summed, rows, store, 3)


def pack_kernel(first, v, s, g, end, x_faces, y_last, y_first, summed, rows):
    outs = (x_faces, y_last, y_first)
    for k, field in enumerate((v, g, s)):
        emit_faces(field, outs, 3 * k)

    def store(c, value):
        end[c] = value

    coarsen(g, summed, rows, store)
    emit_coarse_faces(end, outs, 9)


def coarsen_kernel(first, v, s, end, speed, zero, summed, rows):
    f = first[0]

    def store_zero(c, value):
        zero[c] = f * value + (1.0 - f) * end[c]

    def store_speed(c, value):
        speed[c] = value * 0.25

    coarsen(s, summed, rows, store_zero)
    coarsen(v, summed, rows, store_speed)


def integral_loop(ext, half, summed, grads_summed):
    width, length = ext.shape[1] - 2, ext.shape[2] - 2 * PAD
    n = min(CHUNK, length)

    @pl.loop(0, width // 2)
    def _(i):
        for r in range(0, length, n):
            pair = [fine_rates(ext, half, 2 * i + 1 + q, PAD + r, n) for q in range(2)]
            for a in range(3):
                summed[a, i, r : r + n] = pair[0][0][a] + pair[1][0][a]
                if grads_summed is not None:
                    for b in range(3):
                        value = pair[0][1][a][b] + pair[1][1][a][b]
                        grads_summed[3 * a + b, i, r : r + n] = value


def offset_start_kernel(
    first, v, s, g, x_faces, behind, ahead, zero,
    integral, coarse_grads, zero_x, zero_b, zero_a, end, end_x, end_l, end_f,
    ext, half, summed, grads_summed, rows,
):
    f = first[0]
    fill(half, [(0.5, Node(v, x_faces, behind, ahead))])
    start = Node(s, x_faces, behind, ahead, 6)
    guess = Node(g, x_faces, behind, ahead, 3)
    share = f * (TIME_STEP / 6.0)
    fill(ext, [(share, start), (TIME_STEP - share, guess)])
    integral_loop(ext, half, summed, grads_summed)

    def store(c, value):
        integral[c] = value
        end[c] = zero[c] + value

    squeeze(summed, rows, store, 3)
    emit_faces(end, (end_x, end_l, end_f))
    take_coarse_faces(x_faces, behind, ahead, 9, (zero_x, zero_b, zero_a))

    def store_grads(c, value):
        coarse_grads[c] = value

    squeeze(grads_summed, rows, store_grads, 9)


def offset_later_kernel(
    first, v, s, x_faces, behind, ahead,
    u0, u0_x, u0_b, u0_a, u1, u1_x, u1_b, u1_a, u2, u2_x, u2_b, u2_a,
    integral, zero, zero_x, zero_b, zero_a, end, end_x, end_l, end_f,
    ext, half, summed, rows,
):
    f = first[0]
    fill(half, [(0.5, Node(v, x_faces, behind, ahead))])
    sixth = TIME_STEP / 6.0
    fill(
        ext,
        [
            (f * sixth, Node(s, x_faces, behind, ahead, 6)),
            (sixth, Node(u0, u0_x, u0_b, u0_a)),
            (TIME_STEP * 2.0 / 3.0, Node(u1, u1_x, u1_b, u1_a)),
            (sixth, Node(u2, u2_x, u2_b, u2_a)),
        ],
    )

    @pl.loop(0, s.shape[1] // 2)
    def _(i):
        for c in range(3):
            summed[c, i] = f * (s[c, 2 * i] + s[c, 2 * i + 1]) + (u0[c, 2 * i] + u0[c, 2 * i + 1])

    def store_zero(c, value):
        zero[c] = value

    squeeze(summed, rows, store_zero, 3)
    integral_loop(ext, half, summed, None)

    def store(c, value):
        integral[c] = value
        end[c] = zero[c] + value

    squeeze(summed, rows, store, 3)
    emit_faces(end, (end_x, end_l, end_f))
    take_coarse_faces(u0_x, u0_b, u0_a, 3, (zero_x, zero_b, zero_a))


def chain_step(rest, arrived, zero, integral, speed, coarse_grads, d0, ext, store):
    for k in range(4):
        d0[k][...] = rest * (total([group[k][...] for group in arrived]) - zero[k][...])
    fill(ext, [(TIME_STEP, Node(*d0))], unrolled=True)
    width, length = zero[0].shape[1:3]
    for x in range(width):
        speeds = [speed[b, x] for b in range(3)]

        def grads_of(a):
            return [coarse_grads[3 * a + b, x] for b in range(3)]

        changes = rates(ext, x + 1, PAD, length, speeds, grads_of, VISCOSITY / 4.0)
        for a in range(3):
            store(a, x, zero[0][a, x] + d0[0][a, x] + integral[a, x] + changes[a])


def pass_kernel(turn, first, *refs):
    arrived, zero = refs[:4], refs[4:8]
    integral, speed, coarse_grads, end, end_x, end_l, end_f = refs[8:15]
    d0, ext = refs[15:19], refs[19]

    @pl.when(first[1] == float(turn))
    def _():
        def store(a, x, value):
            end[a, x] = value

        chain_step(1.0, [arrived], zero, integral, speed, coarse_grads, d0, ext, store)
        emit_faces(end, (end_x, end_l, end_f))


def settle_kernel(count, first, *refs):
    arrived = [refs[4 * k : 4 * k + 4] for k in range(count)]
    refs = refs[4 * count :]
    zero, (integral, speed, coarse_grads, end_two) = refs[:4], refs[4:8]
    d0, (d2, d2_x, d2_l, d2_f, ext) = refs[8:12], refs[12:17]

    def store(a, x, value):
        d2[a, x] = value - end_two[a, x]

    chain_step(1.0 - first[0], arrived, zero, integral, speed, coarse_grads, d0, ext, store)
    emit_faces(d2, (d2_x, d2_l, d2_f))


def middle_kernel(nodes, *refs):
    first, v, vx, vb, va = refs[:5]
    at = 5
    parts = []
    for _, _, _, own, off in nodes:
        main = refs[at]
        at += 1
        if own:
            x_faces, behind, ahead = refs[at : at + 3]
            at += 3
        else:
            x_faces, behind, ahead = vx, vb, va
        parts.append(Node(main, x_faces, behind, ahead, off))
    d0 = Node(*refs[at : at + 4])
    d2 = Node(*refs[at + 4 : at + 8])
    a1, a1_x, a1_l, a1_f, rest, rest_x, rest_b, rest_a = refs[at + 8 : at + 16]
    ext, half, wide0, edge0, wide2, edge2, rows = refs[at + 16 :]
    f = first[0]
    begin, first_stage, second_stage = [
        [(spec[k][0] * f + spec[k][1], node) for spec, node in zip(nodes, parts)] for k in range(3)
    ]
    fill(half, [(0.5, Node(v, vx, vb, va))])
    prolong(d0, wide0, edge0, rows)
    prolong(d2, wide2, edge2, rows)
    fill(
        ext,
        [(TIME_STEP * w, node) for w, node in first_stage],
        [(TIME_STEP * 0.375, wide0, edge0), (TIME_STEP * 0.125, wide2, edge2)],
    )
    width, length = a1.shape[1:3]
    n = min(CHUNK, length)
    last_cx = width // 2 + 1

    def rest_of(get, p0, p2):
        return total([w * get(node) for w, node in second_stage]) + 0.125 * (p2 - p0)

    for c in range(3):
        for k in range(2):
            rest_x[c, k] = rest_of(
                lambda nd: nd.x_faces[nd.off + c, k], wide0[c, k * last_cx], wide2[c, k * last_cx]
            )

    @pl.loop(0, width // 2)
    def _(i):
        for q in range(2):
            x = 2 * i + q
            row = pl.ds(x, 1)
            for r in range(0, length, n):
                changes, _ = fine_rates(ext, half, x + 1, PAD + r, n)
                for a in range(3):
                    p0, p2 = wide0[a, i + 1, r : r + n], wide2[a, i + 1, r : r + n]
                    start = total([w * nd.main[a, x, r : r + n] for w, nd in begin])
                    a1[a, x, r : r + n] = start + p0 + changes[a]
                    rest[a, x, r : r + n] = rest_of(lambda nd: nd.main[a, x, r : r + n], p0, p2)
            for c in range(3):
                p0, p2 = edge0[0, c, pl.ds(i, 1)], edge2[0, c, pl.ds(i, 1)]
                rest_b[c, row] = rest_of(lambda nd: nd.behind[nd.off + c, row], p0, p2)
                p0, p2 = edge0[1, c, pl.ds(i, 1)], edge2[1, c, pl.ds(i, 1)]
                rest_a[c, row] = rest_of(lambda nd: nd.ahead[nd.off + c, row], p0, p2)

    emit_faces(a1, (a1_x, a1_l, a1_f))


def finish_kernel(last, first, v, vx, vb, va, a1, a1_x, a1_b, a1_a, rest, rest_x, rest_b, rest_a, *refs):
    if last:
        a2, ext, half = refs
    else:
        a2, a2_x, a2_l, a2_f, end, ext, half, summed, rows = refs
    fill(half, [(0.5, Node(v, vx, vb, va))])
    fill(
        ext,
        [
            (TIME_STEP * 0.5, Node(a1, a1_x, a1_b, a1_a)),
            (TIME_STEP, Node(rest, rest_x, rest_b, rest_a)),
        ],
    )
    width, length = a1.shape[1:3]
    n = min(CHUNK, length)

    @pl.loop(0, width // 2)
    def _(i):
        for r in range(0, length, n):
            pair = []
            for q in range(2):
                x = 2 * i + q
                changes, _ = fine_rates(ext, half, x + 1, PAD + r, n)
                pair.append([a1[a, x, r : r + n] + changes[a] for a in range(3)])
                for a in range(3):
                    a2[a, x, r : r + n] = pair[q][a]
            if not last:
                for a in range(3):
                    summed[a, i, r : r + n] = pair[0][a] + pair[1][a]

    if not last:
        emit_faces(a2, (a2_x, a2_l, a2_f))

        def store(c, value):
            end[c] = value

        squeeze(summed, rows, store, 3)
        emit_coarse_faces(end, (a2_x, a2_l, a2_f), 3)


def call(kernel, name, first, args, outs, scratch, flops=0):
    moved = sum(4 * a.size for a in args)
    room = moved + sum(4 * math.prod(dims) for dims in outs + scratch)
    return pl.pallas_call(
        kernel,
        name=name,
        out_shape=[jax.ShapeDtypeStruct(dims, F32) for dims in outs],
        in_specs=[pl.BlockSpec(memory_space=pltpu.SMEM)] + [pl.BlockSpec(memory_space=pltpu.VMEM)] * len(args),
        out_specs=[pl.BlockSpec(memory_space=pltpu.VMEM)] * len(outs),
        scratch_shapes=[pltpu.VMEM(dims, F32) for dims in scratch],
        compiler_params=pltpu.CompilerParams(vmem_limit_bytes=min(room + ROOM, 56 << 20)),
        cost_estimate=pl.CostEstimate(flops=flops, bytes_accessed=moved, transcendentals=0),
    )(first, *args)


def shards(velocity, start_field, guess):
    own = guess[0]
    _, nx, ny, nz = own.shape
    cx, cy, cz = nx // 2, ny // 2, nz // 2
    slabs = lax.axis_size("tm")
    number = lax.axis_index("tm")
    first = jnp.stack([number == 0, number]).astype(F32)

    def layers_of(count):
        return [(count, 2, ny, nz), (count, nx, nz), (count, nx, nz)]

    fine, coarse = (3, nx, ny, nz), (3, cx, cy, cz)
    fine_faces, coarse_faces = layers_of(3), [(3, 2, cy, cz), (3, cx, cz), (3, cx, cz)]
    ext = (3, nx + 2, ny + 2 * PAD, nz)
    coarse_ext = (3, cx + 2, cy + 2 * PAD, cz)
    summed, rows = (3, cx, ny, nz), (cx * ny, cz)
    wide, edge, wide_rows = (3, cx + 2, ny, nz), (2, 3, cx, nz), ((cx + 2) * ny, cz)

    end_two, *packed = call(
        pack_kernel, "pack", first, [velocity, start_field, own],
        [coarse] + layers_of(10), [summed, rows], 5_000_000,
    )
    layers = swap_faces(packed)
    speed, zero = call(
        coarsen_kernel, "coarsen", first, [velocity, start_field, end_two],
        [coarse, coarse], [summed, rows], 10_000_000,
    )
    integral, coarse_grads, *results = call(
        offset_start_kernel, "offset_start", first, [velocity, start_field, own, *layers, zero],
        [coarse, (9, cx, cy, cz)] + coarse_faces + [coarse] + coarse_faces,
        [ext, ext, summed, (9, cx, ny, nz), rows], 40_000_000,
    )
    zero_faces, end, sent = results[:3], results[3], results[4:]
    for sweep_index in range(ITERS):
        final = sweep_index + 1 == ITERS
        arrivals = []
        for turn in range(1, slabs):
            arrivals.append(hand_on([turn - 1], end, sent))
            if turn + 1 < slabs:
                end, *sent = call(
                    lambda *refs, turn=turn: pass_kernel(turn, *refs), "chain", first,
                    [*arrivals[-1], zero, *zero_faces, integral, speed, coarse_grads],
                    [coarse] + coarse_faces, [coarse, *coarse_faces, coarse_ext], 2_000_000,
                )
        results = call(
            lambda *refs, count=len(arrivals): settle_kernel(count, *refs), "settle", first,
            [a for group in arrivals for a in group]
            + [zero, *zero_faces, integral, speed, coarse_grads, end_two],
            [coarse] + coarse_faces + [coarse] + coarse_faces, [coarse_ext], 2_000_000,
        )
        d0, d2 = list(results[:4]), [results[4], *swap_faces(results[5:])]

        if sweep_index == 0:
            nodes = (
                ((1.0, 0.0), (5.0 / 24.0, 0.0), (-1.0 / 24.0, 0.0), False, 6),
                ((-1.0, 1.0), (-5.0 / 24.0, 0.5), (1.0 / 24.0, 0.0), False, 3),
            )
            args = [start_field, own]
        else:
            nodes = (
                ((1.0, 0.0), (5.0 / 24.0, 0.0), (-1.0 / 24.0, 0.0), False, 6),
                ((0.0, 1.0), (0.0, 5.0 / 24.0), (0.0, -1.0 / 24.0), True, 0),
                ((0.0, 0.0), (0.0, 1.0 / 3.0), (0.0, -1.0 / 6.0), True, 0),
                ((0.0, 0.0), (0.0, -1.0 / 24.0), (0.0, 5.0 / 24.0), True, 0),
            )
            args = [start_field, *u0, *u1, *u2]
        middle, m_x, m_l, m_f, *rest = call(
            lambda *refs, nodes=nodes: middle_kernel(nodes, *refs),
            "middle", first, [velocity, *layers, *args, *d0, *d2],
            [fine] + fine_faces + [fine] + fine_faces,
            [ext, ext, wide, edge, wide, edge, wide_rows], 60_000_000,
        )
        u1 = [middle, *swap_faces((m_x, m_l, m_f))]
        results = call(
            lambda *refs, final=final: finish_kernel(final, *refs),
            "finish", first, [velocity, *layers, *u1, *rest],
            [fine] if final else [fine] + layers_of(4) + [coarse],
            [ext, ext] if final else [ext, ext, summed, rows], 40_000_000,
        )
        if final:
            return results[0][None]
        value, *faces = results[:4]
        end_two = results[4]
        u0 = hand_on(range(slabs - 1), value, faces)
        u2 = [value, *swap_faces(faces)]
        integral, zero, *results = call(
            offset_later_kernel, "offset_later", first,
            [velocity, start_field, *layers, *u0, *u1, *u2],
            [coarse, coarse] + coarse_faces + [coarse] + coarse_faces,
            [ext, ext, summed, rows], 40_000_000,
        )
        zero_faces, end, sent = results[:3], results[3], results[4:]


def solution(mesh):
    in_specs = (
        P(None, "gx", "gy", None),
        P(None, "gx", "gy", None),
        P("tm", None, "gx", "gy", None),
    )
    out_specs = P("tm", None, "gx", "gy", None)
    return jax.shard_map(shards, mesh=mesh, in_specs=in_specs, out_specs=out_specs, check_vma=False)
```

```python
import math

import jax
import jax.numpy as jnp
from jax import lax
from jax.experimental import pallas as pl
from jax.experimental.pallas import tpu as pltpu
from jax.sharding import PartitionSpec as P

ITERS = 2
VISCOSITY = 0.25
TIME_STEP = 0.5
PAD = 8
CHUNK = 8
ROOM = 4 << 20
F32 = jnp.float32
BF16 = jnp.bfloat16


def ring(size, by):
    return [(i, (i + by) % size) for i in range(size)]


def both_faces(faces, permute, size):
    if size == 2:
        return permute(faces, 1)
    before = permute(faces[:, 0:1], 1)
    after = permute(faces[:, 1:2], -1)
    return jnp.concatenate([before, after], axis=1)


def swap_faces(faces):
    x_faces, y_last, y_first = faces
    gx, gy = lax.axis_size("gx"), lax.axis_size("gy")
    before_after = both_faces(x_faces, lambda a, by: lax.ppermute(a, "gx", ring(gx, by)), gx)
    behind = lax.ppermute(y_last, "gy", ring(gy, 1))
    ahead = lax.ppermute(y_first, "gy", ring(gy, -1))
    return before_after, behind, ahead


def hand_on(slabs, value, faces):
    gx, gy = lax.axis_size("gx"), lax.axis_size("gy")

    def permute(array, dx, dy):
        pairs = []
        for t in slabs:
            for x in range(gx):
                for y in range(gy):
                    source = (t * gx + x) * gy + y
                    target = ((t + 1) * gx + (x + dx) % gx) * gy + (y + dy) % gy
                    pairs.append((source, target))
        return lax.ppermute(array, ("tm", "gx", "gy"), pairs)

    moved = [] if value is None else [permute(value, 0, 0)]
    x_faces, y_last, y_first = faces
    moved.append(both_faces(x_faces, lambda a, by: permute(a, by, 0), gx))
    moved.append(permute(y_last, 0, 1))
    moved.append(permute(y_first, 0, -1))
    return moved


class Node:
    def __init__(self, main, x_faces, behind, ahead, off=0):
        self.main, self.x_faces, self.behind, self.ahead, self.off = main, x_faces, behind, ahead, off


def total(terms):
    result = terms[0]
    for term in terms[1:]:
        result = result + term
    return result


def each(count, unrolled=False):
    def wrap(body):
        if unrolled:
            for i in range(count):
                body(i)
        else:
            pl.loop(0, count)(body)

    return wrap


def fill(ext, parts, spread=(), unrolled=False):
    width, length = ext.shape[1] - 2, ext.shape[2] - 2 * PAD
    inner = slice(PAD, PAD + length)
    for c in range(3):
        for k, at in ((0, 0), (1, width + 1)):
            terms = [w * n.x_faces[n.off + c, k] for w, n in parts]
            terms += [w * p[c, k * (width // 2 + 1)] for w, p, _ in spread]
            ext[c, at, inner] = total(terms)

    @each(width // 2, unrolled)
    def _(i):
        for q in range(2):
            x = 2 * i + q
            for c in range(3):
                terms = [w * n.main[c, x] for w, n in parts]
                terms += [w * p[c, i + 1] for w, p, _ in spread]
                ext[c, x + 1, inner] = total(terms)
                row = pl.ds(x, 1)
                for k, at in ((0, PAD - 1), (1, PAD + length)):
                    terms = [w * (n.ahead if k else n.behind)[n.off + c, row] for w, n in parts]
                    terms += [w * e[k, c, pl.ds(i, 1)] for w, _, e in spread]
                    ext[c, x + 1, at : at + 1] = total(terms)


def turned(value, by):
    return pltpu.roll(value, by % value.shape[-1], value.ndim - 1)


def sides(ext, c, x, r, n):
    here = ext[c, x, r : r + n]
    return (
        here,
        (ext[c, x + 1, r : r + n], ext[c, x, r + 1 : r + 1 + n], turned(here, -1)),
        (ext[c, x - 1, r : r + n], ext[c, x, r - 1 : r - 1 + n], turned(here, 1)),
    )


def rates(ext, x, r, n, speeds, grads_of, strength):
    here = [ext[b, x, r : r + n] for b in range(3)]
    toward = [strength - speed for speed in speeds]
    away = [strength + speed for speed in speeds]
    outputs = []
    for a in range(3):
        _, ahead, behind = sides(ext, a, x, r, n)
        grads = grads_of(a)
        result = here[a] * (grads[a] - 6.0 * strength)
        for b in range(3):
            if b != a:
                result = result + here[b] * grads[b]
            result = result + toward[b] * ahead[b] + away[b] * behind[b]
        outputs.append(result)
    return outputs


def slopes(half, a, x, r, n):
    _, ahead, behind = sides(half, a, x, r, n)
    return [ahead[b] - behind[b] for b in range(3)]


def fine_rates(ext, v, grads, x, r, n):
    speeds = [0.5 * v[b, x, r : r + n] for b in range(3)]

    def grads_of(a):
        return [grads[3 * a + b, x, r : r + n] for b in range(3)]

    return rates(ext, x + 1, PAD + r, n, speeds, grads_of, VISCOSITY)


def split(value):
    high = value.astype(BF16)
    low = (value - high.astype(F32)).astype(BF16)
    return high, low


def pair_table(rows, columns, by_row, entry):
    i = lax.broadcasted_iota(jnp.int32, (rows, columns), 0)
    j = lax.broadcasted_iota(jnp.int32, (rows, columns), 1)
    same = (i >> 1) == j if by_row else i == (j >> 1)
    return jnp.where(same, entry, 0.0).astype(BF16)


def squeeze(summed, rows, store, count):
    cx, y, z = summed.shape[1:]
    table = pair_table(z, z // 2, True, 0.125)
    for c in range(count):
        high, low = split(summed[c].reshape(cx * y, z))
        rows[...] = jnp.dot(high, table, preferred_element_type=F32) + jnp.dot(
            low, table, preferred_element_type=F32
        )
        half = cx * y // 2
        value = rows[pl.ds(0, half, stride=2)] + rows[pl.ds(1, half, stride=2)]
        store(c, value.reshape(cx, y // 2, z // 2))


def prolong(field, wide, edge, rows):
    cx, cy, cz = field.main.shape[1:]
    single = pair_table(cz, 2 * cz, False, 1.0)
    table = jnp.concatenate([single, single], axis=0)

    def along_z(value):
        high, low = split(value)
        return jnp.dot(jnp.concatenate([high, low], axis=1), table, preferred_element_type=F32)

    count = (cx + 2) * cy
    edges = []
    for c in range(3):
        layers = [field.x_faces[c, 0:1], field.main[c], field.x_faces[c, 1:2]]
        value = jnp.concatenate(layers, axis=0).reshape(count, cz)
        rows[pl.ds(0, count, stride=2)] = value
        rows[pl.ds(1, count, stride=2)] = value
        wide[c] = along_z(rows[...]).reshape(cx + 2, 2 * cy, 2 * cz)
        edges += [field.behind[c], field.ahead[c]]
    value = along_z(jnp.concatenate(edges, axis=0))
    for c in range(3):
        for k in range(2):
            at = (2 * c + k) * cx
            edge[k, c] = value[at : at + cx]


def emit_faces(main, outs, off=0):
    x_faces, y_last, y_first = outs
    width, length = main.shape[1:3]
    for c in range(3):
        x_faces[off + c, 0] = main[c, width - 1]
        x_faces[off + c, 1] = main[c, 0]
        for x in range(width):
            y_last[off + c, x : x + 1] = main[c, x, length - 1 : length]
            y_first[off + c, x : x + 1] = main[c, x, 0:1]


def quadrant(c, rows, columns):
    up, along = c // 2, c % 2
    return slice(up * rows, (up + 1) * rows), slice(along * columns, (along + 1) * columns)


def emit_coarse_faces(main, outs, comp):
    x_faces, y_last, y_first = outs
    cx, cy, cz = main.shape[1:]
    for c in range(3):
        x_faces[(comp, 0) + quadrant(c, cy, cz)] = main[c, cx - 1]
        x_faces[(comp, 1) + quadrant(c, cy, cz)] = main[c, 0]
        rows, columns = quadrant(c, cx, cz)
        for i in range(cx):
            at = slice(rows.start + i, rows.start + i + 1)
            y_last[comp, at, columns] = main[c, i, cy - 1 : cy]
            y_first[comp, at, columns] = main[c, i, 0:1]


def take_coarse_faces(x_faces, behind, ahead, comp, outs):
    out_x, out_b, out_a = outs
    cy, cz = out_x.shape[2:]
    cx = out_b.shape[1]
    for c in range(3):
        for k in range(2):
            out_x[c, k] = x_faces[(comp, k) + quadrant(c, cy, cz)]
        out_b[c] = behind[(comp,) + quadrant(c, cx, cz)]
        out_a[c] = ahead[(comp,) + quadrant(c, cx, cz)]


def coarsen(field, summed, rows, store):
    @pl.loop(0, field.shape[1] // 2)
    def _(i):
        for c in range(3):
            summed[c, i] = field[c, 2 * i] + field[c, 2 * i + 1]

    squeeze(summed, rows, store, 3)


def pack_kernel(first, v, s, g, end, x_faces, y_last, y_first, summed, rows):
    outs = (x_faces, y_last, y_first)
    for k, field in enumerate((v, g, s)):
        emit_faces(field, outs, 3 * k)

    def store(c, value):
        end[c] = value

    coarsen(g, summed, rows, store)
    emit_coarse_faces(end, outs, 9)


def coarsen_kernel(first, v, s, end, speed, zero, summed, rows):
    f = first[0]

    def store_zero(c, value):
        zero[c] = f * value + (1.0 - f) * end[c]

    def store_speed(c, value):
        speed[c] = value * 0.25

    coarsen(s, summed, rows, store_zero)
    coarsen(v, summed, rows, store_speed)


def offset_start_kernel(
    first, v, s, g, x_faces, behind, ahead, zero,
    grads, integral, coarse_grads, zero_x, zero_b, zero_a, end, end_x, end_l, end_f,
    ext, half, summed, grads_summed, rows,
):
    f = first[0]
    fill(half, [(0.5, Node(v, x_faces, behind, ahead))])
    start = Node(s, x_faces, behind, ahead, 6)
    guess = Node(g, x_faces, behind, ahead, 3)
    share = f * (TIME_STEP / 6.0)
    fill(ext, [(share, start), (TIME_STEP - share, guess)])
    width, length = v.shape[1:3]
    n = min(CHUNK, length)

    @pl.loop(0, width // 2)
    def _(i):
        for r in range(0, length, n):
            at = slice(r, r + n)
            for q in range(2):
                x = 2 * i + q
                for a in range(3):
                    row = slopes(half, a, x + 1, PAD + r, n)
                    for b in range(3):
                        grads[3 * a + b, x, at] = row[b]
                        if q:
                            row[b] = row[b] + grads_summed[3 * a + b, i, at]
                        grads_summed[3 * a + b, i, at] = row[b]
            pair = [fine_rates(ext, v, grads, 2 * i + q, r, n) for q in range(2)]
            for a in range(3):
                summed[a, i, at] = pair[0][a] + pair[1][a]

    def store(c, value):
        integral[c] = value
        end[c] = zero[c] + value

    squeeze(summed, rows, store, 3)
    emit_faces(end, (end_x, end_l, end_f))
    take_coarse_faces(x_faces, behind, ahead, 9, (zero_x, zero_b, zero_a))

    def store_grads(c, value):
        coarse_grads[c] = value

    squeeze(grads_summed, rows, store_grads, 9)


def offset_later_kernel(
    first, v, grads, s, x_faces, behind, ahead,
    u1, u1_x, u1_b, u1_a, u2, u2_x, u2_b, u2_a, zero, end_two,
    own, following, sent, sent_x, sent_l, sent_f,
    ext, ext_two, summed, summed_two, rows,
):
    f = first[0]
    sixth = TIME_STEP / 6.0
    last = Node(u2, u2_x, u2_b, u2_a)
    fill(ext_two, [(sixth, last)])
    fill(
        ext,
        [
            (f * sixth, Node(s, x_faces, behind, ahead, 6)),
            (TIME_STEP * 2.0 / 3.0, Node(u1, u1_x, u1_b, u1_a)),
            (sixth, last),
        ],
    )
    width, length = v.shape[1:3]
    n = min(CHUNK, length)

    @pl.loop(0, width // 2)
    def _(i):
        for r in range(0, length, n):
            at = slice(r, r + n)
            pair = [fine_rates(ext, v, grads, 2 * i + q, r, n) for q in range(2)]
            for a in range(3):
                summed[a, i, at] = pair[0][a] + pair[1][a]
            pair = [fine_rates(ext_two, v, grads, 2 * i + q, r, n) for q in range(2)]
            for a in range(3):
                summed_two[a, i, at] = (pair[0][a] + u2[a, 2 * i, at]) + (pair[1][a] + u2[a, 2 * i + 1, at])

    def store(c, value):
        own[c] = value + (f * zero[c] - end_two[c])
        sent[c] = own[c]

    squeeze(summed, rows, store, 3)
    emit_faces(own, (sent_x, sent_l, sent_f))

    def store_following(c, value):
        following[c] = value
        sent[3 + c] = value

    squeeze(summed_two, rows, store_following, 3)


def chain_step(base, speed, coarse_grads, d0, ext, store):
    fill(ext, [(TIME_STEP, Node(*d0))], unrolled=True)
    width, length = speed.shape[1:3]
    for x in range(width):
        speeds = [speed[b, x] for b in range(3)]

        def grads_of(a):
            return [coarse_grads[3 * a + b, x] for b in range(3)]

        changes = rates(ext, x + 1, PAD, length, speeds, grads_of, VISCOSITY / 4.0)
        for a in range(3):
            store(a, x, base(a, x) + d0[0][a, x] + changes[a])


def pass_start_kernel(turn, first, *refs):
    arrived, zero = refs[:4], refs[4:8]
    integral, speed, coarse_grads, end, end_x, end_l, end_f = refs[8:15]
    d0, ext = refs[15:19], refs[19]

    @pl.when(first[1] == float(turn))
    def _():
        def base(a, x):
            return zero[0][a, x] + integral[a, x]

        def store(a, x, value):
            end[a, x] = value

        for k in range(4):
            d0[k][...] = arrived[k][...] - zero[k][...]
        chain_step(base, speed, coarse_grads, d0, ext, store)
        emit_faces(end, (end_x, end_l, end_f))


def settle_start_kernel(count, first, *refs):
    arrived = [refs[4 * k : 4 * k + 4] for k in range(count)]
    refs = refs[4 * count :]
    zero, (integral, speed, coarse_grads, end_two) = refs[:4], refs[4:8]
    d0, (d2, d2_x, d2_l, d2_f, ext) = refs[8:12], refs[12:17]
    rest = 1.0 - first[0]

    def base(a, x):
        return zero[0][a, x] + integral[a, x] - end_two[a, x]

    def store(a, x, value):
        d2[a, x] = value

    for k in range(4):
        d0[k][...] = rest * (total([group[k][...] for group in arrived]) - zero[k][...])
    chain_step(base, speed, coarse_grads, d0, ext, store)
    emit_faces(d2, (d2_x, d2_l, d2_f))


def pass_later_kernel(turn, first, *refs):
    arrived, (own, following, speed, coarse_grads) = refs[:4], refs[4:8]
    sent, sent_x, sent_l, sent_f, ext = refs[8:13]

    @pl.when(first[1] == float(turn))
    def _():
        def base(a, x):
            return own[a, x] + arrived[0][3 + a, x]

        def store(a, x, value):
            sent[a, x] = value
            sent[3 + a, x] = following[a, x]

        chain_step(base, speed, coarse_grads, arrived, ext, store)
        emit_faces(sent, (sent_x, sent_l, sent_f))


def settle_later_kernel(count, first, *refs):
    arrived = [refs[4 * k : 4 * k + 4] for k in range(count)]
    own, speed, coarse_grads = refs[4 * count : 4 * count + 3]
    refs = refs[4 * count + 3 :]
    d0, (d2, d2_x, d2_l, d2_f, ext) = refs[:4], refs[4:9]

    def base(a, x):
        return own[a, x] + total([group[0][3 + a, x] for group in arrived])

    def store(a, x, value):
        d2[a, x] = value

    d0[0][...] = total([group[0][0:3] for group in arrived])
    for k in range(1, 4):
        d0[k][...] = total([group[k][...] for group in arrived])
    chain_step(base, speed, coarse_grads, d0, ext, store)
    emit_faces(d2, (d2_x, d2_l, d2_f))


def middle_kernel(nodes, *refs):
    first, v, grads, vx, vb, va = refs[:6]
    at = 6
    parts = []
    for _, _, _, own, off in nodes:
        main = refs[at]
        at += 1
        if own:
            x_faces, behind, ahead = refs[at : at + 3]
            at += 3
        else:
            x_faces, behind, ahead = vx, vb, va
        parts.append(Node(main, x_faces, behind, ahead, off))
    d0 = Node(*refs[at : at + 4])
    d2 = Node(*refs[at + 4 : at + 8])
    a1, a1_x, a1_l, a1_f, rest, rest_x, rest_b, rest_a = refs[at + 8 : at + 16]
    ext, wide0, edge0, wide2, edge2, rows = refs[at + 16 :]
    f = first[0]
    begin, first_stage, second_stage = [
        [(spec[k][0] * f + spec[k][1], node) for spec, node in zip(nodes, parts)] for k in range(3)
    ]
    prolong(d0, wide0, edge0, rows)
    prolong(d2, wide2, edge2, rows)
    fill(
        ext,
        [(TIME_STEP * w, node) for w, node in first_stage],
        [(TIME_STEP * 0.375, wide0, edge0), (TIME_STEP * 0.125, wide2, edge2)],
    )
    width, length = a1.shape[1:3]
    n = min(CHUNK, length)
    last_cx = width // 2 + 1

    def rest_of(get, p0, p2):
        return total([w * get(node) for w, node in second_stage]) + 0.125 * (p2 - p0)

    for c in range(3):
        for k in range(2):
            rest_x[c, k] = rest_of(
                lambda nd: nd.x_faces[nd.off + c, k], wide0[c, k * last_cx], wide2[c, k * last_cx]
            )

    @pl.loop(0, width // 2)
    def _(i):
        for q in range(2):
            x = 2 * i + q
            row = pl.ds(x, 1)
            for r in range(0, length, n):
                changes = fine_rates(ext, v, grads, x, r, n)
                for a in range(3):
                    p0, p2 = wide0[a, i + 1, r : r + n], wide2[a, i + 1, r : r + n]
                    start = total([w * nd.main[a, x, r : r + n] for w, nd in begin])
                    a1[a, x, r : r + n] = start + p0 + changes[a]
                    rest[a, x, r : r + n] = rest_of(lambda nd: nd.main[a, x, r : r + n], p0, p2)
            for c in range(3):
                p0, p2 = edge0[0, c, pl.ds(i, 1)], edge2[0, c, pl.ds(i, 1)]
                rest_b[c, row] = rest_of(lambda nd: nd.behind[nd.off + c, row], p0, p2)
                p0, p2 = edge0[1, c, pl.ds(i, 1)], edge2[1, c, pl.ds(i, 1)]
                rest_a[c, row] = rest_of(lambda nd: nd.ahead[nd.off + c, row], p0, p2)

    emit_faces(a1, (a1_x, a1_l, a1_f))


def finish_kernel(last, first, v, grads, a1, a1_x, a1_b, a1_a, rest, rest_x, rest_b, rest_a, *refs):
    if last:
        a2, ext = refs
    else:
        a2, a2_x, a2_l, a2_f, end, ext, summed, rows = refs
    fill(
        ext,
        [
            (TIME_STEP * 0.5, Node(a1, a1_x, a1_b, a1_a)),
            (TIME_STEP, Node(rest, rest_x, rest_b, rest_a)),
        ],
    )
    width, length = a1.shape[1:3]
    n = min(CHUNK, length)

    @pl.loop(0, width // 2)
    def _(i):
        for r in range(0, length, n):
            pair = []
            for q in range(2):
                x = 2 * i + q
                changes = fine_rates(ext, v, grads, x, r, n)
                pair.append([a1[a, x, r : r + n] + changes[a] for a in range(3)])
                for a in range(3):
                    a2[a, x, r : r + n] = pair[q][a]
            if not last:
                for a in range(3):
                    summed[a, i, r : r + n] = pair[0][a] + pair[1][a]

    if not last:
        emit_faces(a2, (a2_x, a2_l, a2_f))

        def store(c, value):
            end[c] = value

        squeeze(summed, rows, store, 3)


def call(kernel, name, first, args, outs, scratch, flops=0):
    moved = sum(4 * a.size for a in args)
    room = moved + sum(4 * math.prod(dims) for dims in outs + scratch)
    return pl.pallas_call(
        kernel,
        name=name,
        out_shape=[jax.ShapeDtypeStruct(dims, F32) for dims in outs],
        in_specs=[pl.BlockSpec(memory_space=pltpu.SMEM)] + [pl.BlockSpec(memory_space=pltpu.VMEM)] * len(args),
        out_specs=[pl.BlockSpec(memory_space=pltpu.VMEM)] * len(outs),
        scratch_shapes=[pltpu.VMEM(dims, F32) for dims in scratch],
        compiler_params=pltpu.CompilerParams(vmem_limit_bytes=min(room + ROOM, 56 << 20)),
        cost_estimate=pl.CostEstimate(flops=flops, bytes_accessed=moved, transcendentals=0),
    )(first, *args)


def shards(velocity, start_field, guess):
    own = guess[0]
    _, nx, ny, nz = own.shape
    cx, cy, cz = nx // 2, ny // 2, nz // 2
    slabs = lax.axis_size("tm")
    number = lax.axis_index("tm")
    first = jnp.stack([number == 0, number]).astype(F32)

    def layers_of(count):
        return [(count, 2, ny, nz), (count, nx, nz), (count, nx, nz)]

    fine, coarse = (3, nx, ny, nz), (3, cx, cy, cz)
    fine_faces, coarse_faces = layers_of(3), [(3, 2, cy, cz), (3, cx, cz), (3, cx, cz)]
    ext = (3, nx + 2, ny + 2 * PAD, nz)
    coarse_ext = (3, cx + 2, cy + 2 * PAD, cz)
    summed, rows = (3, cx, ny, nz), (cx * ny, cz)
    wide, edge, wide_rows = (3, cx + 2, ny, nz), (2, 3, cx, nz), ((cx + 2) * ny, cz)

    end_two, *packed = call(
        pack_kernel, "pack", first, [velocity, start_field, own],
        [coarse] + layers_of(10), [summed, rows], 5_000_000,
    )
    layers = swap_faces(packed)
    speed, zero = call(
        coarsen_kernel, "coarsen", first, [velocity, start_field, end_two],
        [coarse, coarse], [summed, rows], 10_000_000,
    )
    grads, integral, coarse_grads, *results = call(
        offset_start_kernel, "offset_start", first, [velocity, start_field, own, *layers, zero],
        [(9, nx, ny, nz), coarse, (9, cx, cy, cz)] + coarse_faces + [coarse] + coarse_faces,
        [ext, ext, summed, (9, cx, ny, nz), rows], 40_000_000,
    )
    zero_faces, sent = results[:3], results[3:]
    for sweep_index in range(ITERS):
        final = sweep_index + 1 == ITERS
        if sweep_index == 0:
            step, settle, outs, scratch = pass_start_kernel, settle_start_kernel, coarse, [coarse, *coarse_faces]
            own_terms, end_terms = [zero, *zero_faces, integral], [end_two]
            held = own_terms
        else:
            step, settle, outs, scratch = pass_later_kernel, settle_later_kernel, (6, cx, cy, cz), []
            own_terms, end_terms = [own_part, following], []
            held = [own_part]
        arrivals = []
        for turn in range(1, slabs):
            arrivals.append(hand_on([turn - 1], sent[0], sent[1:]))
            if turn + 1 < slabs:
                sent = call(
                    lambda *refs, step=step, turn=turn: step(turn, *refs), "chain", first,
                    [*arrivals[-1], *own_terms, speed, coarse_grads],
                    [outs] + coarse_faces, scratch + [coarse_ext], 2_000_000,
                )
        results = call(
            lambda *refs, settle=settle, count=len(arrivals): settle(count, *refs), "settle", first,
            [a for group in arrivals for a in group] + held + [speed, coarse_grads] + end_terms,
            [coarse] + coarse_faces + [coarse] + coarse_faces, [coarse_ext], 2_000_000,
        )
        d0, d2 = list(results[:4]), [results[4], *swap_faces(results[5:])]

        if sweep_index == 0:
            nodes = (
                ((1.0, 0.0), (5.0 / 24.0, 0.0), (-1.0 / 24.0, 0.0), False, 6),
                ((-1.0, 1.0), (-5.0 / 24.0, 0.5), (1.0 / 24.0, 0.0), False, 3),
            )
            args = [start_field, own]
        else:
            nodes = (
                ((1.0, 0.0), (5.0 / 24.0, 0.0), (-1.0 / 24.0, 0.0), False, 6),
                ((0.0, 1.0), (0.0, 5.0 / 24.0), (0.0, -1.0 / 24.0), True, 0),
                ((0.0, 0.0), (0.0, 1.0 / 3.0), (0.0, -1.0 / 6.0), True, 0),
                ((0.0, 0.0), (0.0, -1.0 / 24.0), (0.0, 5.0 / 24.0), True, 0),
            )
            args = [start_field, *u0, *u1, *u2]
        middle, m_x, m_l, m_f, *rest = call(
            lambda *refs, nodes=nodes: middle_kernel(nodes, *refs),
            "middle", first, [velocity, grads, *layers, *args, *d0, *d2],
            [fine] + fine_faces + [fine] + fine_faces,
            [ext, wide, edge, wide, edge, wide_rows], 60_000_000,
        )
        u1 = [middle, *swap_faces((m_x, m_l, m_f))]
        results = call(
            lambda *refs, final=final: finish_kernel(final, *refs),
            "finish", first, [velocity, grads, *u1, *rest],
            [fine] if final else [fine] + fine_faces + [coarse],
            [ext] if final else [ext, summed, rows], 40_000_000,
        )
        if final:
            return results[0][None]
        value, *faces = results[:4]
        end_two = results[4]
        u0 = hand_on(range(slabs - 1), value, faces)
        u2 = [value, *swap_faces(faces)]
        own_part, following, *sent = call(
            offset_later_kernel, "offset_later", first,
            [velocity, grads, start_field, *layers, *u1, *u2, zero, end_two],
            [coarse, coarse, (6, cx, cy, cz)] + coarse_faces,
            [ext, ext, summed, summed, rows], 60_000_000,
        )


def solution(mesh):
    in_specs = (
        P(None, "gx", "gy", None),
        P(None, "gx", "gy", None),
        P("tm", None, "gx", "gy", None),
    )
    out_specs = P("tm", None, "gx", "gy", None)
    return jax.shard_map(shards, mesh=mesh, in_specs=in_specs, out_specs=out_specs, check_vma=False)
```

```python
import math

import jax
import jax.numpy as jnp
from jax import lax
from jax.experimental import pallas as pl
from jax.experimental.pallas import tpu as pltpu
from jax.sharding import PartitionSpec as P

VISCOSITY = 0.25
TIME_STEP = 0.5
PAD = 8
CHUNK = 8
ROOM = 4 << 20
F32 = jnp.float32
BF16 = jnp.bfloat16


def ring(size, by):
    return [(i, (i + by) % size) for i in range(size)]


def both_faces(faces, permute, size):
    if size == 2:
        return permute(faces, 1)
    before = permute(faces[:, 0:1], 1)
    after = permute(faces[:, 1:2], -1)
    return jnp.concatenate([before, after], axis=1)


def swap_faces(faces):
    x_faces, y_last, y_first = faces
    gx, gy = lax.axis_size("gx"), lax.axis_size("gy")
    before_after = both_faces(x_faces, lambda a, by: lax.ppermute(a, "gx", ring(gx, by)), gx)
    behind = lax.ppermute(y_last, "gy", ring(gy, 1))
    ahead = lax.ppermute(y_first, "gy", ring(gy, -1))
    return before_after, behind, ahead


def pass_on(slabs, array, dx=0, dy=0):
    gx, gy = lax.axis_size("gx"), lax.axis_size("gy")
    pairs = []
    for t in slabs:
        for x in range(gx):
            for y in range(gy):
                source = (t * gx + x) * gy + y
                target = ((t + 1) * gx + (x + dx) % gx) * gy + (y + dy) % gy
                pairs.append((source, target))
    return lax.ppermute(array, ("tm", "gx", "gy"), pairs)


def hand_on(slabs, value, faces):
    x_faces, y_last, y_first = faces
    return [
        pass_on(slabs, value),
        both_faces(x_faces, lambda a, by: pass_on(slabs, a, by, 0), lax.axis_size("gx")),
        pass_on(slabs, y_last, 0, 1),
        pass_on(slabs, y_first, 0, -1),
    ]


class Node:
    def __init__(self, main, x_faces, behind, ahead, off=0):
        self.main, self.x_faces, self.behind, self.ahead, self.off = main, x_faces, behind, ahead, off


def scaled(weight, value):
    return value if isinstance(weight, float) and weight == 1.0 else weight * value


def total(terms):
    result = terms[0]
    for term in terms[1:]:
        result = result + term
    return result


def each(count, unrolled=False):
    def wrap(body):
        if unrolled:
            for i in range(count):
                body(i)
        else:
            pl.loop(0, count)(body)

    return wrap


def fill(ext, parts, spread=(), unrolled=False):
    width, length = ext.shape[1] - 2, ext.shape[2] - 2 * PAD
    inner = slice(PAD, PAD + length)
    for c in range(3):
        for k, at in ((0, 0), (1, width + 1)):
            terms = [scaled(w, n.x_faces[n.off + c, k]) for w, n in parts]
            terms += [w * p[c, k * (width // 2 + 1)] for w, p, _ in spread]
            ext[c, at, inner] = total(terms)

    @each(width // 2, unrolled)
    def _(i):
        for q in range(2):
            x = 2 * i + q
            for c in range(3):
                terms = [scaled(w, n.main[c, x]) for w, n in parts]
                terms += [w * p[c, i + 1] for w, p, _ in spread]
                ext[c, x + 1, inner] = total(terms)
                row = pl.ds(x, 1)
                for k, at in ((0, PAD - 1), (1, PAD + length)):
                    terms = [scaled(w, (n.ahead if k else n.behind)[n.off + c, row]) for w, n in parts]
                    terms += [w * e[k, c, pl.ds(i, 1)] for w, _, e in spread]
                    ext[c, x + 1, at : at + 1] = total(terms)


def turned(value, by):
    return pltpu.roll(value, by % value.shape[-1], value.ndim - 1)


def sides(ext, c, x, r, n):
    here = ext[c, x, r : r + n]
    return (
        here,
        (ext[c, x + 1, r : r + n], ext[c, x, r + 1 : r + 1 + n], turned(here, -1)),
        (ext[c, x - 1, r : r + n], ext[c, x, r - 1 : r - 1 + n], turned(here, 1)),
    )


def rates(ext, x, r, n, speeds, grads_of, strength):
    here = [ext[b, x, r : r + n] for b in range(3)]
    toward = [strength - speed for speed in speeds]
    away = [strength + speed for speed in speeds]
    outputs = []
    for a in range(3):
        _, ahead, behind = sides(ext, a, x, r, n)
        grads = grads_of(a)
        result = here[a] * (grads[a] - 6.0 * strength)
        for b in range(3):
            if b != a:
                result = result + here[b] * grads[b]
            result = result + toward[b] * ahead[b] + away[b] * behind[b]
        outputs.append(result)
    return outputs


def slopes(half, a, x, r, n):
    _, ahead, behind = sides(half, a, x, r, n)
    return [ahead[b] - behind[b] for b in range(3)]


def fine_rates(ext, v, grads, x, r, n):
    speeds = [0.5 * v[b, x, r : r + n] for b in range(3)]

    def grads_of(a):
        return [grads[3 * a + b, x, r : r + n] for b in range(3)]

    return rates(ext, x + 1, PAD + r, n, speeds, grads_of, VISCOSITY)


def split(value):
    high = value.astype(BF16)
    low = (value - high.astype(F32)).astype(BF16)
    return high, low


def pair_table(rows, columns, by_row, entry):
    i = lax.broadcasted_iota(jnp.int32, (rows, columns), 0)
    j = lax.broadcasted_iota(jnp.int32, (rows, columns), 1)
    same = (i >> 1) == j if by_row else i == (j >> 1)
    return jnp.where(same, entry, 0.0).astype(BF16)


def squeeze(summed, rows, store, count):
    cx, y, z = summed.shape[1:]
    table = pair_table(z, z // 2, True, 0.125)
    for c in range(count):
        high, low = split(summed[c].reshape(cx * y, z))
        rows[...] = jnp.dot(high, table, preferred_element_type=F32) + jnp.dot(
            low, table, preferred_element_type=F32
        )
        half = cx * y // 2
        value = rows[pl.ds(0, half, stride=2)] + rows[pl.ds(1, half, stride=2)]
        store(c, value.reshape(cx, y // 2, z // 2))


def spread_along(value):
    cz = value.shape[1]
    single = pair_table(cz, 2 * cz, False, 1.0)
    table = jnp.concatenate([single, single], axis=0)
    high, low = split(value)
    return jnp.dot(jnp.concatenate([high, low], axis=1), table, preferred_element_type=F32)


def doubled(value, rows):
    count = value.shape[0]
    rows[pl.ds(0, count, stride=2)] = value
    rows[pl.ds(1, count, stride=2)] = value
    return rows[...]


def prolong_own(main, wide, rows):
    cx, cy, cz = main.shape[1:]
    for c in range(3):
        value = doubled(main[c].reshape(cx * cy, cz), rows)
        wide[c] = spread_along(value).reshape(cx, 2 * cy, 2 * cz)


def prolong(field, wide, edge, rows):
    cx, cy, cz = field.main.shape[1:]
    edges = []
    for c in range(3):
        layers = [field.x_faces[c, 0:1], field.main[c], field.x_faces[c, 1:2]]
        value = doubled(jnp.concatenate(layers, axis=0).reshape((cx + 2) * cy, cz), rows)
        wide[c] = spread_along(value).reshape(cx + 2, 2 * cy, 2 * cz)
        edges += [field.behind[c], field.ahead[c]]
    value = spread_along(jnp.concatenate(edges, axis=0))
    for c in range(3):
        for k in range(2):
            at = (2 * c + k) * cx
            edge[k, c] = value[at : at + cx]


def emit_faces(main, outs, off=0):
    x_faces, y_last, y_first = outs
    width, length = main.shape[1:3]
    for c in range(3):
        x_faces[off + c, 0] = main[c, width - 1]
        x_faces[off + c, 1] = main[c, 0]
        for x in range(width):
            y_last[off + c, x : x + 1] = main[c, x, length - 1 : length]
            y_first[off + c, x : x + 1] = main[c, x, 0:1]


def quadrant(c, rows, columns):
    up, along = c // 2, c % 2
    return slice(up * rows, (up + 1) * rows), slice(along * columns, (along + 1) * columns)


def emit_coarse_faces(main, outs, comp):
    x_faces, y_last, y_first = outs
    cx, cy, cz = main.shape[1:]
    for c in range(3):
        x_faces[(comp, 0) + quadrant(c, cy, cz)] = main[c, cx - 1]
        x_faces[(comp, 1) + quadrant(c, cy, cz)] = main[c, 0]
        rows, columns = quadrant(c, cx, cz)
        for i in range(cx):
            at = slice(rows.start + i, rows.start + i + 1)
            y_last[comp, at, columns] = main[c, i, cy - 1 : cy]
            y_first[comp, at, columns] = main[c, i, 0:1]


def take_coarse_faces(x_faces, behind, ahead, comp, outs):
    out_x, out_b, out_a = outs
    cy, cz = out_x.shape[2:]
    cx = out_b.shape[1]
    for c in range(3):
        for k in range(2):
            out_x[c, k] = x_faces[(comp, k) + quadrant(c, cy, cz)]
        out_b[c] = behind[(comp,) + quadrant(c, cx, cz)]
        out_a[c] = ahead[(comp,) + quadrant(c, cx, cz)]


def coarsen(field, summed, rows, store):
    @pl.loop(0, field.shape[1] // 2)
    def _(i):
        for c in range(3):
            summed[c, i] = field[c, 2 * i] + field[c, 2 * i + 1]

    squeeze(summed, rows, store, 3)


def pack_kernel(first, v, s, g, end, x_faces, y_last, y_first, summed, rows):
    outs = (x_faces, y_last, y_first)
    for k, field in enumerate((v, g, s)):
        emit_faces(field, outs, 3 * k)

    def store(c, value):
        end[c] = value

    coarsen(g, summed, rows, store)
    emit_coarse_faces(end, outs, 9)


def coarsen_kernel(first, v, s, end, speed, zero, summed, rows):
    f = first[0]

    def store_zero(c, value):
        zero[c] = f * value + (1.0 - f) * end[c]

    def store_speed(c, value):
        speed[c] = value * 0.25

    coarsen(s, summed, rows, store_zero)
    coarsen(v, summed, rows, store_speed)


def offset_start_kernel(
    first, v, s, g, x_faces, behind, ahead, zero,
    grads, integral, coarse_grads, zero_x, zero_b, zero_a, end, end_x, end_l, end_f,
    ext, half, summed, grads_summed, rows,
):
    f = first[0]
    fill(half, [(0.5, Node(v, x_faces, behind, ahead))])
    start = Node(s, x_faces, behind, ahead, 6)
    guess = Node(g, x_faces, behind, ahead, 3)
    share = f * (TIME_STEP / 6.0)
    fill(ext, [(share, start), (TIME_STEP - share, guess)])
    width, length = v.shape[1:3]
    n = min(CHUNK, length)

    @pl.loop(0, width // 2)
    def _(i):
        for r in range(0, length, n):
            at = slice(r, r + n)
            for q in range(2):
                x = 2 * i + q
                for a in range(3):
                    row = slopes(half, a, x + 1, PAD + r, n)
                    for b in range(3):
                        grads[3 * a + b, x, at] = row[b]
                        if q:
                            row[b] = row[b] + grads_summed[3 * a + b, i, at]
                        grads_summed[3 * a + b, i, at] = row[b]
            pair = [fine_rates(ext, v, grads, 2 * i + q, r, n) for q in range(2)]
            for a in range(3):
                summed[a, i, at] = pair[0][a] + pair[1][a]

    def store(c, value):
        integral[c] = value
        end[c] = zero[c] + value

    squeeze(summed, rows, store, 3)
    emit_faces(end, (end_x, end_l, end_f))
    take_coarse_faces(x_faces, behind, ahead, 9, (zero_x, zero_b, zero_a))

    def store_grads(c, value):
        coarse_grads[c] = value

    squeeze(grads_summed, rows, store_grads, 9)


def offset_later_kernel(
    first, v, grads, s, x_faces, behind, ahead,
    u1, u1_x, u1_b, u1_a, u2, u2_x, u2_b, u2_a, zero, end_two,
    own, following, sent, sent_x, sent_l, sent_f,
    ext, ext_two, summed, summed_two, rows,
):
    f = first[0]
    sixth = TIME_STEP / 6.0
    last = Node(u2, u2_x, u2_b, u2_a)
    fill(ext_two, [(sixth, last)])
    fill(
        ext,
        [
            (f * sixth, Node(s, x_faces, behind, ahead, 6)),
            (TIME_STEP * 2.0 / 3.0, Node(u1, u1_x, u1_b, u1_a)),
            (sixth, last),
        ],
    )
    width, length = v.shape[1:3]
    n = min(CHUNK, length)

    @pl.loop(0, width // 2)
    def _(i):
        for r in range(0, length, n):
            at = slice(r, r + n)
            pair = [fine_rates(ext, v, grads, 2 * i + q, r, n) for q in range(2)]
            for a in range(3):
                summed[a, i, at] = pair[0][a] + pair[1][a]
            pair = [fine_rates(ext_two, v, grads, 2 * i + q, r, n) for q in range(2)]
            for a in range(3):
                summed_two[a, i, at] = (pair[0][a] + u2[a, 2 * i, at]) + (pair[1][a] + u2[a, 2 * i + 1, at])

    def store(c, value):
        own[c] = value + (f * zero[c] - end_two[c])
        sent[c] = own[c]

    squeeze(summed, rows, store, 3)
    emit_faces(own, (sent_x, sent_l, sent_f))

    def store_following(c, value):
        following[c] = value
        sent[3 + c] = value

    squeeze(summed_two, rows, store_following, 3)


def chain_step(base, speed, coarse_grads, d0, ext, store):
    fill(ext, [(TIME_STEP, Node(*d0))], unrolled=True)
    width, length = speed.shape[1:3]
    for x in range(width):
        speeds = [speed[b, x] for b in range(3)]

        def grads_of(a):
            return [coarse_grads[3 * a + b, x] for b in range(3)]

        changes = rates(ext, x + 1, PAD, length, speeds, grads_of, VISCOSITY / 4.0)
        for a in range(3):
            store(a, x, base(a, x) + d0[0][a, x] + changes[a])


def pass_start_kernel(turn, first, *refs):
    arrived, zero = refs[:4], refs[4:8]
    integral, speed, coarse_grads, end, end_x, end_l, end_f = refs[8:15]
    d0, ext = refs[15:19], refs[19]

    @pl.when(first[1] == float(turn))
    def _():
        def base(a, x):
            return zero[0][a, x] + integral[a, x]

        def store(a, x, value):
            end[a, x] = value

        for k in range(4):
            d0[k][...] = arrived[k][...] - zero[k][...]
        chain_step(base, speed, coarse_grads, d0, ext, store)
        emit_faces(end, (end_x, end_l, end_f))


def settle_start_kernel(count, first, *refs):
    arrived = [refs[4 * k : 4 * k + 4] for k in range(count)]
    refs = refs[4 * count :]
    zero, (integral, speed, coarse_grads, end_two) = refs[:4], refs[4:8]
    d0, (d2, d2_x, d2_l, d2_f, ext) = refs[8:12], refs[12:17]
    rest = 1.0 - first[0]

    def base(a, x):
        return zero[0][a, x] + integral[a, x] - end_two[a, x]

    def store(a, x, value):
        d2[a, x] = value

    for k in range(4):
        d0[k][...] = rest * (total([group[k][...] for group in arrived]) - zero[k][...])
    chain_step(base, speed, coarse_grads, d0, ext, store)
    emit_faces(d2, (d2_x, d2_l, d2_f))


def pass_later_kernel(turn, first, *refs):
    arrived, (own, following, speed, coarse_grads) = refs[:4], refs[4:8]
    sent, sent_x, sent_l, sent_f, ext = refs[8:13]

    @pl.when(first[1] == float(turn))
    def _():
        def base(a, x):
            return own[a, x] + arrived[0][3 + a, x]

        def store(a, x, value):
            sent[a, x] = value
            sent[3 + a, x] = following[a, x]

        chain_step(base, speed, coarse_grads, arrived, ext, store)
        emit_faces(sent, (sent_x, sent_l, sent_f))


def settle_later_kernel(count, first, *refs):
    arrived = [refs[4 * k : 4 * k + 4] for k in range(count)]
    own, speed, coarse_grads, s, u0, u1, u2, stage, stage_x, stage_l, stage_f, begin, rest = refs[4 * count : 4 * count + 13]
    d0, (d2, ext, wide0, wide2, rows) = refs[4 * count + 13 : 4 * count + 17], refs[4 * count + 17 :]
    f = first[0]

    def base(a, x):
        return own[a, x] + total([group[0][3 + a, x] for group in arrived])

    def store(a, x, value):
        d2[a, x] = value

    d0[0][...] = total([group[0][0:3] for group in arrived])
    for k in range(1, 4):
        d0[k][...] = total([group[k][...] for group in arrived])
    chain_step(base, speed, coarse_grads, d0, ext, store)
    prolong_own(d0[0], wide0, rows)
    prolong_own(d2, wide2, rows)

    @pl.loop(0, u0.shape[1] // 2)
    def _(i):
        for c in range(3):
            p0, p2 = wide0[c, i], wide2[c, i]
            toward_stage = TIME_STEP * (0.375 * p0 + 0.125 * p2)
            toward_rest = 0.125 * (p2 - p0)
            for q in range(2):
                x = 2 * i + q
                start, one, two = f * s[c, x] + u0[c, x], u1[c, x], u2[c, x]
                stage[c, x] = toward_stage + TIME_STEP * (start * (5.0 / 24.0) + one / 3.0 - two / 24.0)
                begin[c, x] = start + p0
                rest[c, x] = toward_rest + (two * (5.0 / 24.0) - one / 6.0 - start / 24.0)

    emit_faces(stage, (stage_x, stage_l, stage_f))


def stage_kernel(first, v, grads, y, y_x, y_b, y_a, begin, *refs):
    if len(refs) == 2:
        out, ext = refs
    else:
        rest, out, following, following_x, following_l, following_f, ext = refs
    fill(ext, [(1.0, Node(y, y_x, y_b, y_a))])
    width, length = v.shape[1:3]
    n = min(CHUNK, length)

    @pl.loop(0, width)
    def _(x):
        for r in range(0, length, n):
            at = slice(r, r + n)
            changes = fine_rates(ext, v, grads, x, r, n)
            for a in range(3):
                value = begin[a, x, at] + changes[a]
                out[a, x, at] = value
                if len(refs) > 2:
                    following[a, x, at] = TIME_STEP * (0.5 * value + rest[a, x, at])

    if len(refs) > 2:
        emit_faces(following, (following_x, following_l, following_f))


def middle_kernel(nodes, *refs):
    first, v, grads, vx, vb, va = refs[:6]
    at = 6
    parts = []
    for _, _, _, own, off in nodes:
        main = refs[at]
        at += 1
        if own:
            x_faces, behind, ahead = refs[at : at + 3]
            at += 3
        else:
            x_faces, behind, ahead = vx, vb, va
        parts.append(Node(main, x_faces, behind, ahead, off))
    d0 = Node(*refs[at : at + 4])
    d2 = Node(*refs[at + 4 : at + 8])
    a1, a1_x, a1_l, a1_f, rest, rest_x, rest_b, rest_a = refs[at + 8 : at + 16]
    ext, wide0, edge0, wide2, edge2, rows = refs[at + 16 :]
    f = first[0]
    begin, first_stage, second_stage = [
        [(spec[k][0] * f + spec[k][1], node) for spec, node in zip(nodes, parts)] for k in range(3)
    ]
    prolong(d0, wide0, edge0, rows)
    prolong(d2, wide2, edge2, rows)
    fill(
        ext,
        [(TIME_STEP * w, node) for w, node in first_stage],
        [(TIME_STEP * 0.375, wide0, edge0), (TIME_STEP * 0.125, wide2, edge2)],
    )
    width, length = a1.shape[1:3]
    n = min(CHUNK, length)
    last_cx = width // 2 + 1

    def rest_of(get, p0, p2):
        return total([w * get(node) for w, node in second_stage]) + 0.125 * (p2 - p0)

    for c in range(3):
        for k in range(2):
            rest_x[c, k] = rest_of(
                lambda nd: nd.x_faces[nd.off + c, k], wide0[c, k * last_cx], wide2[c, k * last_cx]
            )

    @pl.loop(0, width // 2)
    def _(i):
        for q in range(2):
            x = 2 * i + q
            row = pl.ds(x, 1)
            for r in range(0, length, n):
                changes = fine_rates(ext, v, grads, x, r, n)
                for a in range(3):
                    p0, p2 = wide0[a, i + 1, r : r + n], wide2[a, i + 1, r : r + n]
                    start = total([w * nd.main[a, x, r : r + n] for w, nd in begin])
                    a1[a, x, r : r + n] = start + p0 + changes[a]
                    rest[a, x, r : r + n] = rest_of(lambda nd: nd.main[a, x, r : r + n], p0, p2)
            for c in range(3):
                p0, p2 = edge0[0, c, pl.ds(i, 1)], edge2[0, c, pl.ds(i, 1)]
                rest_b[c, row] = rest_of(lambda nd: nd.behind[nd.off + c, row], p0, p2)
                p0, p2 = edge0[1, c, pl.ds(i, 1)], edge2[1, c, pl.ds(i, 1)]
                rest_a[c, row] = rest_of(lambda nd: nd.ahead[nd.off + c, row], p0, p2)

    emit_faces(a1, (a1_x, a1_l, a1_f))


def finish_kernel(
    first, v, grads, a1, a1_x, a1_b, a1_a, rest, rest_x, rest_b, rest_a,
    a2, a2_x, a2_l, a2_f, end, ext, summed, rows,
):
    fill(
        ext,
        [
            (TIME_STEP * 0.5, Node(a1, a1_x, a1_b, a1_a)),
            (TIME_STEP, Node(rest, rest_x, rest_b, rest_a)),
        ],
    )
    width, length = a1.shape[1:3]
    n = min(CHUNK, length)

    @pl.loop(0, width // 2)
    def _(i):
        for r in range(0, length, n):
            pair = []
            for q in range(2):
                x = 2 * i + q
                changes = fine_rates(ext, v, grads, x, r, n)
                pair.append([a1[a, x, r : r + n] + changes[a] for a in range(3)])
                for a in range(3):
                    a2[a, x, r : r + n] = pair[q][a]
            for a in range(3):
                summed[a, i, r : r + n] = pair[0][a] + pair[1][a]

    emit_faces(a2, (a2_x, a2_l, a2_f))

    def store(c, value):
        end[c] = value

    squeeze(summed, rows, store, 3)


def call(kernel, name, first, args, outs, scratch, flops=0):
    moved = sum(4 * a.size for a in args)
    room = moved + sum(4 * math.prod(dims) for dims in outs + scratch)
    return pl.pallas_call(
        kernel,
        name=name,
        out_shape=[jax.ShapeDtypeStruct(dims, F32) for dims in outs],
        in_specs=[pl.BlockSpec(memory_space=pltpu.SMEM)] + [pl.BlockSpec(memory_space=pltpu.VMEM)] * len(args),
        out_specs=[pl.BlockSpec(memory_space=pltpu.VMEM)] * len(outs),
        scratch_shapes=[pltpu.VMEM(dims, F32) for dims in scratch],
        compiler_params=pltpu.CompilerParams(vmem_limit_bytes=min(room + ROOM, 56 << 20)),
        cost_estimate=pl.CostEstimate(flops=flops, bytes_accessed=moved, transcendentals=0),
    )(first, *args)


def shards(velocity, start_field, guess):
    own = guess[0]
    _, nx, ny, nz = own.shape
    cx, cy, cz = nx // 2, ny // 2, nz // 2
    slabs = lax.axis_size("tm")
    number = lax.axis_index("tm")
    first = jnp.stack([number == 0, number]).astype(F32)

    def layers_of(count):
        return [(count, 2, ny, nz), (count, nx, nz), (count, nx, nz)]

    fine, coarse = (3, nx, ny, nz), (3, cx, cy, cz)
    fine_faces, coarse_faces = layers_of(3), [(3, 2, cy, cz), (3, cx, cz), (3, cx, cz)]
    ext = (3, nx + 2, ny + 2 * PAD, nz)
    coarse_ext = (3, cx + 2, cy + 2 * PAD, cz)
    summed, rows = (3, cx, ny, nz), (cx * ny, cz)
    wide, edge, wide_rows = (3, cx + 2, ny, nz), (2, 3, cx, nz), ((cx + 2) * ny, cz)

    end_two, *packed = call(
        pack_kernel, "pack", first, [velocity, start_field, own],
        [coarse] + layers_of(10), [summed, rows], 5_000_000,
    )
    layers = swap_faces(packed)
    speed, zero = call(
        coarsen_kernel, "coarsen", first, [velocity, start_field, end_two],
        [coarse, coarse], [summed, rows], 10_000_000,
    )
    grads, integral, coarse_grads, *results = call(
        offset_start_kernel, "offset_start", first, [velocity, start_field, own, *layers, zero],
        [(9, nx, ny, nz), coarse, (9, cx, cy, cz)] + coarse_faces + [coarse] + coarse_faces,
        [ext, ext, summed, (9, cx, ny, nz), rows], 40_000_000,
    )
    zero_faces, sent = results[:3], results[3:]

    def chain(step, sent, outs, scratch, own_terms):
        arrivals = []
        for turn in range(1, slabs):
            arrivals += hand_on([turn - 1], sent[0], sent[1:])
            if turn + 1 < slabs:
                sent = call(
                    lambda *refs, turn=turn: step(turn, *refs), "chain", first,
                    [*arrivals[-4:], *own_terms, speed, coarse_grads],
                    [outs] + coarse_faces, scratch + [coarse_ext], 2_000_000,
                )
        return arrivals

    terms = [zero, *zero_faces, integral]
    arrivals = chain(pass_start_kernel, sent, coarse, [coarse] + coarse_faces, terms)
    results = call(
        lambda *refs: settle_start_kernel(slabs - 1, *refs), "settle", first,
        [*arrivals, *terms, speed, coarse_grads, end_two],
        [coarse] + coarse_faces + [coarse] + coarse_faces, [coarse_ext], 2_000_000,
    )
    d0, d2 = list(results[:4]), [results[4], *swap_faces(results[5:])]
    nodes = (
        ((1.0, 0.0), (5.0 / 24.0, 0.0), (-1.0 / 24.0, 0.0), False, 6),
        ((-1.0, 1.0), (-5.0 / 24.0, 0.5), (1.0 / 24.0, 0.0), False, 3),
    )
    middle, m_x, m_l, m_f, *rest = call(
        lambda *refs: middle_kernel(nodes, *refs), "middle", first,
        [velocity, grads, *layers, start_field, own, *d0, *d2],
        [fine] + fine_faces + [fine] + fine_faces,
        [ext, wide, edge, wide, edge, wide_rows], 60_000_000,
    )
    u1 = [middle, *swap_faces((m_x, m_l, m_f))]
    value, *results = call(
        finish_kernel, "finish", first, [velocity, grads, *u1, *rest],
        [fine] + fine_faces + [coarse], [ext, summed, rows], 40_000_000,
    )
    faces, end_two = results[:3], results[3]
    u0 = pass_on(range(slabs - 1), value)
    u2 = [value, *swap_faces(faces)]

    own_part, following, *sent = call(
        offset_later_kernel, "offset_later", first,
        [velocity, grads, start_field, *layers, *u1, *u2, zero, end_two],
        [coarse, coarse, (6, cx, cy, cz)] + coarse_faces,
        [ext, ext, summed, summed, rows], 60_000_000,
    )
    arrivals = chain(pass_later_kernel, sent, (6, cx, cy, cz), [], [own_part, following])
    stage, *faces, begin, rest = call(
        lambda *refs: settle_later_kernel(slabs - 1, *refs), "settle", first,
        [*arrivals, own_part, speed, coarse_grads, start_field, u0, middle, value],
        [fine] + fine_faces + [fine, fine],
        [coarse, *coarse_faces, coarse, coarse_ext, summed, summed, rows], 10_000_000,
    )
    middle, stage, *faces = call(
        stage_kernel, "stage", first, [velocity, grads, stage, *swap_faces(faces), begin, rest],
        [fine, fine] + fine_faces, [ext], 40_000_000,
    )
    result, = call(
        stage_kernel, "stage", first, [velocity, grads, stage, *swap_faces(faces), middle],
        [fine], [ext], 40_000_000,
    )
    return result[None]


def solution(mesh):
    in_specs = (
        P(None, "gx", "gy", None),
        P(None, "gx", "gy", None),
        P("tm", None, "gx", "gy", None),
    )
    out_specs = P("tm", None, "gx", "gy", None)
    return jax.shard_map(shards, mesh=mesh, in_specs=in_specs, out_specs=out_specs, check_vma=False)
```

```python
import math

import jax
import jax.numpy as jnp
from jax import lax
from jax.experimental import pallas as pl
from jax.experimental.pallas import tpu as pltpu
from jax.sharding import PartitionSpec as P

VISCOSITY = 0.25
TIME_STEP = 0.5
PAD = 8
CHUNK = 8
ROOM = 4 << 20
F32 = jnp.float32
BF16 = jnp.bfloat16


def ring(size, by):
    return [(i, (i + by) % size) for i in range(size)]


def both_faces(faces, permute, size):
    if size == 2:
        return permute(faces, 1)
    before = permute(faces[:, 0:1], 1)
    after = permute(faces[:, 1:2], -1)
    return jnp.concatenate([before, after], axis=1)


def swap_faces(faces):
    x_faces, y_last, y_first = faces
    gx, gy = lax.axis_size("gx"), lax.axis_size("gy")
    before_after = both_faces(x_faces, lambda a, by: lax.ppermute(a, "gx", ring(gx, by)), gx)
    behind = lax.ppermute(y_last, "gy", ring(gy, 1))
    ahead = lax.ppermute(y_first, "gy", ring(gy, -1))
    return before_after, behind, ahead


def pass_on(slabs, array, dx=0, dy=0):
    gx, gy = lax.axis_size("gx"), lax.axis_size("gy")
    pairs = []
    for t in slabs:
        for x in range(gx):
            for y in range(gy):
                source = (t * gx + x) * gy + y
                target = ((t + 1) * gx + (x + dx) % gx) * gy + (y + dy) % gy
                pairs.append((source, target))
    return lax.ppermute(array, ("tm", "gx", "gy"), pairs)


def hand_on(slabs, value, faces):
    x_faces, y_last, y_first = faces
    main = pass_on(slabs, value)
    behind = pass_on(slabs, y_last, 0, 1)
    ahead = pass_on(slabs, y_first, 0, -1)
    before_after = both_faces(x_faces, lambda a, by: pass_on(slabs, a, by, 0), lax.axis_size("gx"))
    return [main, behind, ahead, before_after]


class Node:
    def __init__(self, main, x_faces, behind, ahead, off=0):
        self.main, self.x_faces, self.behind, self.ahead, self.off = main, x_faces, behind, ahead, off


class Mix:
    def __init__(self, *parts):
        self.parts, self.shape = parts, parts[0][1].shape

    def __getitem__(self, key):
        return total([w * field[key] for w, field in self.parts])


def scaled(weight, value):
    return value if isinstance(weight, float) and weight == 1.0 else weight * value


def total(terms):
    result = terms[0]
    for term in terms[1:]:
        result = result + term
    return result


def each(count, unrolled=False):
    def wrap(body):
        if unrolled:
            for i in range(count):
                body(i)
        else:
            pl.loop(0, count)(body)

    return wrap


def fill(ext, parts, spread=(), unrolled=False):
    width, length = ext.shape[1] - 2, ext.shape[2] - 2 * PAD
    inner = slice(PAD, PAD + length)
    for c in range(3):
        for k, at in ((0, 0), (1, width + 1)):
            terms = [scaled(w, n.x_faces[n.off + c, k]) for w, n in parts]
            terms += [w * p[c, k * (width // 2 + 1)] for w, p, _ in spread]
            ext[c, at, inner] = total(terms)

    @each(width // 2, unrolled)
    def _(i):
        for q in range(2):
            x = 2 * i + q
            for c in range(3):
                terms = [scaled(w, n.main[c, x]) for w, n in parts]
                terms += [w * p[c, i + 1] for w, p, _ in spread]
                ext[c, x + 1, inner] = total(terms)
                row = pl.ds(x, 1)
                for k, at in ((0, PAD - 1), (1, PAD + length)):
                    terms = [scaled(w, (n.ahead if k else n.behind)[n.off + c, row]) for w, n in parts]
                    terms += [w * e[k, c, pl.ds(i, 1)] for w, _, e in spread]
                    ext[c, x + 1, at : at + 1] = total(terms)


def turned(value, by):
    return pltpu.roll(value, by % value.shape[-1], value.ndim - 1)


def sides(ext, c, x, r, n):
    here = ext[c, x, r : r + n]
    return (
        here,
        (ext[c, x + 1, r : r + n], ext[c, x, r + 1 : r + 1 + n], turned(here, -1)),
        (ext[c, x - 1, r : r + n], ext[c, x, r - 1 : r - 1 + n], turned(here, 1)),
    )


def rates(ext, x, r, n, speeds, grads_of, strength):
    here = [ext[b, x, r : r + n] for b in range(3)]
    toward = [strength - speed for speed in speeds]
    away = [strength + speed for speed in speeds]
    outputs = []
    for a in range(3):
        _, ahead, behind = sides(ext, a, x, r, n)
        grads = grads_of(a)
        result = here[a] * (grads[a] - 6.0 * strength)
        for b in range(3):
            if b != a:
                result = result + here[b] * grads[b]
            result = result + toward[b] * ahead[b] + away[b] * behind[b]
        outputs.append(result)
    return outputs


def slopes(half, a, x, r, n):
    _, ahead, behind = sides(half, a, x, r, n)
    return [ahead[b] - behind[b] for b in range(3)]


def fine_rates(ext, v, grads, x, r, n):
    speeds = [0.5 * v[b, x, r : r + n] for b in range(3)]

    def grads_of(a):
        return [grads[3 * a + b, x, r : r + n] for b in range(3)]

    return rates(ext, x + 1, PAD + r, n, speeds, grads_of, VISCOSITY)


def split(value):
    high = value.astype(BF16)
    low = (value - high.astype(F32)).astype(BF16)
    return high, low


def pair_table(rows, columns, by_row, entry):
    i = lax.broadcasted_iota(jnp.int32, (rows, columns), 0)
    j = lax.broadcasted_iota(jnp.int32, (rows, columns), 1)
    same = (i >> 1) == j if by_row else i == (j >> 1)
    return jnp.where(same, entry, 0.0).astype(BF16)


def squeeze(summed, rows, store, count):
    cx, y, z = summed.shape[1:]
    table = pair_table(z, z // 2, True, 0.125)
    for c in range(count):
        high, low = split(summed[c].reshape(cx * y, z))
        rows[...] = jnp.dot(high, table, preferred_element_type=F32) + jnp.dot(
            low, table, preferred_element_type=F32
        )
        half = cx * y // 2
        value = rows[pl.ds(0, half, stride=2)] + rows[pl.ds(1, half, stride=2)]
        store(c, value.reshape(cx, y // 2, z // 2))


def spread_along(value):
    cz = value.shape[1]
    single = pair_table(cz, 2 * cz, False, 1.0)
    table = jnp.concatenate([single, single], axis=0)
    high, low = split(value)
    return jnp.dot(jnp.concatenate([high, low], axis=1), table, preferred_element_type=F32)


def doubled(value, rows):
    count = value.shape[0]
    rows[pl.ds(0, count, stride=2)] = value
    rows[pl.ds(1, count, stride=2)] = value
    return rows[...]


def prolong_own(main, wide, rows):
    cx, cy, cz = main.shape[1:]
    for c in range(3):
        value = doubled(main[c].reshape(cx * cy, cz), rows)
        wide[c] = spread_along(value).reshape(cx, 2 * cy, 2 * cz)


def prolong(field, wide, edge, rows):
    cx, cy, cz = field.main.shape[1:]
    edges = []
    for c in range(3):
        layers = [field.x_faces[c, 0:1], field.main[c], field.x_faces[c, 1:2]]
        value = doubled(jnp.concatenate(layers, axis=0).reshape((cx + 2) * cy, cz), rows)
        wide[c] = spread_along(value).reshape(cx + 2, 2 * cy, 2 * cz)
        edges += [field.behind[c], field.ahead[c]]
    value = spread_along(jnp.concatenate(edges, axis=0))
    for c in range(3):
        for k in range(2):
            at = (2 * c + k) * cx
            edge[k, c] = value[at : at + cx]


def emit_faces(main, outs, off=0):
    x_faces, y_last, y_first = outs
    width, length = main.shape[1:3]
    for c in range(3):
        x_faces[off + c, 0] = main[c, width - 1]
        x_faces[off + c, 1] = main[c, 0]
        for x in range(width):
            y_last[off + c, x : x + 1] = main[c, x, length - 1 : length]
            y_first[off + c, x : x + 1] = main[c, x, 0:1]


def quadrant(c, rows, columns):
    up, along = c // 2, c % 2
    return slice(up * rows, (up + 1) * rows), slice(along * columns, (along + 1) * columns)


def emit_coarse_faces(main, outs, comp):
    x_faces, y_last, y_first = outs
    cx, cy, cz = main.shape[1:]
    for c in range(3):
        x_faces[(comp, 0) + quadrant(c, cy, cz)] = main[c, cx - 1]
        x_faces[(comp, 1) + quadrant(c, cy, cz)] = main[c, 0]
        rows, columns = quadrant(c, cx, cz)
        for i in range(cx):
            at = slice(rows.start + i, rows.start + i + 1)
            y_last[comp, at, columns] = main[c, i, cy - 1 : cy]
            y_first[comp, at, columns] = main[c, i, 0:1]


def take_coarse_faces(x_faces, behind, ahead, comp, outs):
    out_x, out_b, out_a = outs
    cy, cz = out_x.shape[2:]
    cx = out_b.shape[1]
    for c in range(3):
        for k in range(2):
            out_x[c, k] = x_faces[(comp, k) + quadrant(c, cy, cz)]
        out_b[c] = behind[(comp,) + quadrant(c, cx, cz)]
        out_a[c] = ahead[(comp,) + quadrant(c, cx, cz)]


def coarsen(field, summed, rows, store):
    @pl.loop(0, field.shape[1] // 2)
    def _(i):
        for c in range(3):
            summed[c, i] = field[c, 2 * i] + field[c, 2 * i + 1]

    squeeze(summed, rows, store, 3)


def offset_mix(f, s, g):
    return Mix((f / 6.0, s), (1.0 - f / 6.0, g))


def pack_kernel(first, v, s, g, end, x_faces, y_last, y_first, summed, rows):
    outs = (x_faces, y_last, y_first)
    emit_faces(v, outs, 0)
    emit_faces(offset_mix(first[0], s, g), outs, 3)

    def store(c, value):
        end[c] = value

    coarsen(g, summed, rows, store)
    emit_coarse_faces(end, outs, 6)


def coarsen_kernel(first, v, s, end, speed, zero, summed, rows):
    f = first[0]

    def store_zero(c, value):
        zero[c] = f * value + (1.0 - f) * end[c]

    def store_speed(c, value):
        speed[c] = value * 0.25

    coarsen(s, summed, rows, store_zero)
    coarsen(v, summed, rows, store_speed)


def offset_start_kernel(
    first, v, s, g, x_faces, behind, ahead, zero,
    grads, integral, coarse_grads, zero_x, zero_b, zero_a, end, end_x, end_l, end_f,
    ext, half, summed, grads_summed, rows,
):
    f = first[0]
    fill(half, [(0.5, Node(v, x_faces, behind, ahead))])
    fill(ext, [(TIME_STEP, Node(offset_mix(f, s, g), x_faces, behind, ahead, 3))])
    width, length = v.shape[1:3]
    n = min(CHUNK, length)

    @pl.loop(0, width // 2)
    def _(i):
        for r in range(0, length, n):
            at = slice(r, r + n)
            for q in range(2):
                x = 2 * i + q
                for a in range(3):
                    row = slopes(half, a, x + 1, PAD + r, n)
                    for b in range(3):
                        grads[3 * a + b, x, at] = row[b]
                        if q:
                            row[b] = row[b] + grads_summed[3 * a + b, i, at]
                        grads_summed[3 * a + b, i, at] = row[b]
            pair = [fine_rates(ext, v, grads, 2 * i + q, r, n) for q in range(2)]
            for a in range(3):
                summed[a, i, at] = pair[0][a] + pair[1][a]

    def store(c, value):
        integral[c] = value
        end[c] = zero[c] + value

    squeeze(summed, rows, store, 3)
    emit_faces(end, (end_x, end_l, end_f))
    take_coarse_faces(x_faces, behind, ahead, 6, (zero_x, zero_b, zero_a))

    def store_grads(c, value):
        coarse_grads[c] = value

    squeeze(grads_summed, rows, store_grads, 9)


def offset_later_kernel(
    first, v, grads, s, x_faces, behind, ahead,
    u1, u1_x, u1_b, u1_a, u2, u2_x, u2_b, u2_a, zero, end_two,
    own, following, sent, sent_x, sent_l, sent_f,
    ext, ext_two, summed, summed_two, rows,
):
    f = first[0]
    sixth = TIME_STEP / 6.0
    last = Node(u2, u2_x, u2_b, u2_a)
    fill(ext_two, [(sixth, last)])
    fill(
        ext,
        [
            (f * sixth, Node(s, x_faces, behind, ahead)),
            (TIME_STEP * 2.0 / 3.0, Node(u1, u1_x, u1_b, u1_a)),
            (sixth, last),
        ],
    )
    width, length = v.shape[1:3]
    n = min(CHUNK, length)

    @pl.loop(0, width // 2)
    def _(i):
        for r in range(0, length, n):
            at = slice(r, r + n)
            pair = [fine_rates(ext, v, grads, 2 * i + q, r, n) for q in range(2)]
            for a in range(3):
                summed[a, i, at] = pair[0][a] + pair[1][a]
            pair = [fine_rates(ext_two, v, grads, 2 * i + q, r, n) for q in range(2)]
            for a in range(3):
                summed_two[a, i, at] = (pair[0][a] + u2[a, 2 * i, at]) + (pair[1][a] + u2[a, 2 * i + 1, at])

    def store(c, value):
        own[c] = value + (f * zero[c] - end_two[c])
        sent[c] = own[c]

    squeeze(summed, rows, store, 3)
    emit_faces(own, (sent_x, sent_l, sent_f))

    def store_following(c, value):
        following[c] = value
        sent[3 + c] = value

    squeeze(summed_two, rows, store_following, 3)


def chain_step(base, speed, coarse_grads, d0, ext, store):
    fill(ext, [(TIME_STEP, Node(*d0))], unrolled=True)
    width, length = speed.shape[1:3]
    for x in range(width):
        speeds = [speed[b, x] for b in range(3)]

        def grads_of(a):
            return [coarse_grads[3 * a + b, x] for b in range(3)]

        changes = rates(ext, x + 1, PAD, length, speeds, grads_of, VISCOSITY / 4.0)
        for a in range(3):
            store(a, x, base(a, x) + d0[0][a, x] + changes[a])


def arrival(refs):
    main, behind, ahead, x_faces = refs
    return main, x_faces, behind, ahead


def pass_start_kernel(turn, first, *refs):
    arrived, zero = arrival(refs[:4]), refs[4:8]
    integral, speed, coarse_grads, end, end_x, end_l, end_f = refs[8:15]
    d0, ext = refs[15:19], refs[19]

    @pl.when(first[1] == float(turn))
    def _():
        def base(a, x):
            return zero[0][a, x] + integral[a, x]

        def store(a, x, value):
            end[a, x] = value

        for k in range(4):
            d0[k][...] = arrived[k][...] - zero[k][...]
        chain_step(base, speed, coarse_grads, d0, ext, store)
        emit_faces(end, (end_x, end_l, end_f))


def settle_start_kernel(count, first, *refs):
    arrived = [arrival(refs[4 * k : 4 * k + 4]) for k in range(count)]
    refs = refs[4 * count :]
    zero, (integral, speed, coarse_grads, end_two, s) = refs[:4], refs[4:9]
    d0, d2, outs, ext = refs[9:13], refs[13], refs[14:17], refs[17]
    rest = 1.0 - first[0]

    def base(a, x):
        return zero[0][a, x] + integral[a, x] - end_two[a, x]

    def store(a, x, value):
        d2[a, x] = value

    for k in range(4):
        d0[k][...] = rest * (total([group[k][...] for group in arrived]) - zero[k][...])
    chain_step(base, speed, coarse_grads, d0, ext, store)
    emit_faces(s, outs, 0)
    emit_coarse_faces(d2, outs, 3)


def pass_later_kernel(turn, first, *refs):
    arrived, (own, following, speed, coarse_grads) = arrival(refs[:4]), refs[4:8]
    sent, sent_x, sent_l, sent_f, ext = refs[8:13]

    @pl.when(first[1] == float(turn))
    def _():
        def base(a, x):
            return own[a, x] + arrived[0][3 + a, x]

        def store(a, x, value):
            sent[a, x] = value
            sent[3 + a, x] = following[a, x]

        chain_step(base, speed, coarse_grads, arrived, ext, store)
        emit_faces(sent, (sent_x, sent_l, sent_f))


def settle_later_kernel(count, first, *refs):
    arrived = [arrival(refs[4 * k : 4 * k + 4]) for k in range(count)]
    own, speed, coarse_grads, s, u0, u1, u2, stage, stage_x, stage_l, stage_f, begin, rest = refs[4 * count : 4 * count + 13]
    d0, (d2, ext, wide0, wide2, rows) = refs[4 * count + 13 : 4 * count + 17], refs[4 * count + 17 :]
    f = first[0]

    def base(a, x):
        return own[a, x] + total([group[0][3 + a, x] for group in arrived])

    def store(a, x, value):
        d2[a, x] = value

    d0[0][...] = total([group[0][0:3] for group in arrived])
    for k in range(1, 4):
        d0[k][...] = total([group[k][...] for group in arrived])
    chain_step(base, speed, coarse_grads, d0, ext, store)
    prolong_own(d0[0], wide0, rows)
    prolong_own(d2, wide2, rows)

    @pl.loop(0, u0.shape[1] // 2)
    def _(i):
        for c in range(3):
            p0, p2 = wide0[c, i], wide2[c, i]
            toward_stage = TIME_STEP * (0.375 * p0 + 0.125 * p2)
            toward_rest = 0.125 * (p2 - p0)
            for q in range(2):
                x = 2 * i + q
                start, one, two = f * s[c, x] + u0[c, x], u1[c, x], u2[c, x]
                stage[c, x] = toward_stage + TIME_STEP * (start * (5.0 / 24.0) + one / 3.0 - two / 24.0)
                begin[c, x] = start + p0
                rest[c, x] = toward_rest + (two * (5.0 / 24.0) - one / 6.0 - start / 24.0)

    emit_faces(stage, (stage_x, stage_l, stage_f))


def stage_kernel(first, v, grads, y, y_x, y_b, y_a, begin, *refs):
    if len(refs) == 2:
        out, ext = refs
    else:
        rest, out, following, following_x, following_l, following_f, ext = refs
    fill(ext, [(1.0, Node(y, y_x, y_b, y_a))])
    width, length = v.shape[1:3]
    n = min(CHUNK, length)

    @pl.loop(0, width)
    def _(x):
        for r in range(0, length, n):
            at = slice(r, r + n)
            changes = fine_rates(ext, v, grads, x, r, n)
            for a in range(3):
                value = begin[a, x, at] + changes[a]
                out[a, x, at] = value
                if len(refs) > 2:
                    following[a, x, at] = TIME_STEP * (0.5 * value + rest[a, x, at])

    if len(refs) > 2:
        emit_faces(following, (following_x, following_l, following_f))


def middle_kernel(
    first, v, grads, s, g, w_x, w_b, w_a, d0, d0_x, d0_b, d0_a, d2, m_x, m_b, m_a,
    a1, a1_x, a1_l, a1_f, rest, rest_x, rest_b, rest_a,
    ext, wide0, edge0, wide2, edge2, rows, d2_x, d2_b, d2_a, g_x, g_b, g_a,
):
    f = first[0]
    take_coarse_faces(m_x, m_b, m_a, 3, (d2_x, d2_b, d2_a))
    for out, mixed, start, off in ((g_x, w_x, m_x, 3), (g_b, w_b, m_b, 3), (g_a, w_a, m_a, 3)):
        for c in range(3):
            out[c] = (1.0 + 0.2 * f) * mixed[off + c] - (0.2 * f) * start[c]
    parts = [Node(s, m_x, m_b, m_a), Node(g, g_x, g_b, g_a)]
    begin = list(zip((f, 1.0 - f), parts))
    first_stage = list(zip((5.0 / 24.0 * f, 0.5 - 5.0 / 24.0 * f), parts))
    second_stage = list(zip((f / -24.0, f / 24.0), parts))
    prolong(Node(d0, d0_x, d0_b, d0_a), wide0, edge0, rows)
    prolong(Node(d2, d2_x, d2_b, d2_a), wide2, edge2, rows)
    fill(
        ext,
        [(TIME_STEP * w, node) for w, node in first_stage],
        [(TIME_STEP * 0.375, wide0, edge0), (TIME_STEP * 0.125, wide2, edge2)],
    )
    width, length = a1.shape[1:3]
    n = min(CHUNK, length)
    last_cx = width // 2 + 1

    def rest_of(get, p0, p2):
        return total([w * get(node) for w, node in second_stage]) + 0.125 * (p2 - p0)

    for c in range(3):
        for k in range(2):
            rest_x[c, k] = rest_of(
                lambda nd: nd.x_faces[nd.off + c, k], wide0[c, k * last_cx], wide2[c, k * last_cx]
            )

    @pl.loop(0, width // 2)
    def _(i):
        for q in range(2):
            x = 2 * i + q
            row = pl.ds(x, 1)
            for r in range(0, length, n):
                changes = fine_rates(ext, v, grads, x, r, n)
                for a in range(3):
                    p0, p2 = wide0[a, i + 1, r : r + n], wide2[a, i + 1, r : r + n]
                    start = total([w * nd.main[a, x, r : r + n] for w, nd in begin])
                    a1[a, x, r : r + n] = start + p0 + changes[a]
                    rest[a, x, r : r + n] = rest_of(lambda nd: nd.main[a, x, r : r + n], p0, p2)
            for c in range(3):
                p0, p2 = edge0[0, c, pl.ds(i, 1)], edge2[0, c, pl.ds(i, 1)]
                rest_b[c, row] = rest_of(lambda nd: nd.behind[nd.off + c, row], p0, p2)
                p0, p2 = edge0[1, c, pl.ds(i, 1)], edge2[1, c, pl.ds(i, 1)]
                rest_a[c, row] = rest_of(lambda nd: nd.ahead[nd.off + c, row], p0, p2)

    emit_faces(a1, (a1_x, a1_l, a1_f))


def finish_kernel(
    first, v, grads, a1, a1_x, a1_b, a1_a, rest, rest_x, rest_b, rest_a,
    a2, a2_x, a2_l, a2_f, end, ext, summed, rows,
):
    fill(
        ext,
        [
            (TIME_STEP * 0.5, Node(a1, a1_x, a1_b, a1_a)),
            (TIME_STEP, Node(rest, rest_x, rest_b, rest_a)),
        ],
    )
    width, length = a1.shape[1:3]
    n = min(CHUNK, length)

    @pl.loop(0, width // 2)
    def _(i):
        for r in range(0, length, n):
            pair = []
            for q in range(2):
                x = 2 * i + q
                changes = fine_rates(ext, v, grads, x, r, n)
                pair.append([a1[a, x, r : r + n] + changes[a] for a in range(3)])
                for a in range(3):
                    a2[a, x, r : r + n] = pair[q][a]
            for a in range(3):
                summed[a, i, r : r + n] = pair[0][a] + pair[1][a]

    emit_faces(a2, (a2_x, a2_l, a2_f))

    def store(c, value):
        end[c] = value

    squeeze(summed, rows, store, 3)


def call(kernel, name, first, args, outs, scratch, flops=0, least=0):
    moved = sum(4 * a.size for a in args)
    room = moved + sum(4 * math.prod(dims) for dims in outs + scratch)
    return pl.pallas_call(
        kernel,
        name=name,
        out_shape=[jax.ShapeDtypeStruct(dims, F32) for dims in outs],
        in_specs=[pl.BlockSpec(memory_space=pltpu.SMEM)] + [pl.BlockSpec(memory_space=pltpu.VMEM)] * len(args),
        out_specs=[pl.BlockSpec(memory_space=pltpu.VMEM)] * len(outs),
        scratch_shapes=[pltpu.VMEM(dims, F32) for dims in scratch],
        compiler_params=pltpu.CompilerParams(vmem_limit_bytes=min(max(room + ROOM, least), 56 << 20)),
        cost_estimate=pl.CostEstimate(flops=flops, bytes_accessed=moved, transcendentals=0),
    )(first, *args)


def shards(velocity, start_field, guess):
    own = guess[0]
    _, nx, ny, nz = own.shape
    cx, cy, cz = nx // 2, ny // 2, nz // 2
    slabs = lax.axis_size("tm")
    number = lax.axis_index("tm")
    first = jnp.stack([number == 0, number]).astype(F32)

    def layers_of(count):
        return [(count, 2, ny, nz), (count, nx, nz), (count, nx, nz)]

    fine, coarse = (3, nx, ny, nz), (3, cx, cy, cz)
    fine_faces, coarse_faces = layers_of(3), [(3, 2, cy, cz), (3, cx, cz), (3, cx, cz)]
    ext = (3, nx + 2, ny + 2 * PAD, nz)
    coarse_ext = (3, cx + 2, cy + 2 * PAD, cz)
    summed, rows = (3, cx, ny, nz), (cx * ny, cz)
    wide, edge, wide_rows = (3, cx + 2, ny, nz), (2, 3, cx, nz), ((cx + 2) * ny, cz)

    end_two, *packed = call(
        pack_kernel, "pack", first, [velocity, start_field, own],
        [coarse] + layers_of(7), [summed, rows], 5_000_000, 56 << 20,
    )
    layers = swap_faces(packed)
    speed, zero = call(
        coarsen_kernel, "coarsen", first, [velocity, start_field, end_two],
        [coarse, coarse], [summed, rows], 10_000_000,
    )
    grads, integral, coarse_grads, *results = call(
        offset_start_kernel, "offset_start", first, [velocity, start_field, own, *layers, zero],
        [(9, nx, ny, nz), coarse, (9, cx, cy, cz)] + coarse_faces + [coarse] + coarse_faces,
        [ext, ext, summed, (9, cx, ny, nz), rows], 40_000_000,
    )
    zero_faces, sent = results[:3], results[3:]

    def chain(step, sent, outs, scratch, own_terms):
        arrivals = []
        for turn in range(1, slabs):
            arrivals += hand_on([turn - 1], sent[0], sent[1:])
            if turn + 1 < slabs:
                sent = call(
                    lambda *refs, turn=turn: step(turn, *refs), "chain", first,
                    [*arrivals[-4:], *own_terms, speed, coarse_grads],
                    [outs] + coarse_faces, scratch + [coarse_ext], 2_000_000,
                )
        return arrivals

    terms = [zero, *zero_faces, integral]
    arrivals = chain(pass_start_kernel, sent, coarse, [coarse] + coarse_faces, terms)
    results = call(
        lambda *refs: settle_start_kernel(slabs - 1, *refs), "settle", first,
        [*arrivals, *terms, speed, coarse_grads, end_two, start_field],
        [coarse] + coarse_faces + [coarse] + layers_of(4), [coarse_ext], 2_000_000,
    )
    start_layers = swap_faces(results[5:])
    middle, m_x, m_l, m_f, *rest = call(
        middle_kernel, "middle", first,
        [velocity, grads, start_field, own, *layers, *results[:5], *start_layers],
        [fine] + fine_faces + [fine] + fine_faces,
        [ext, wide, edge, wide, edge, wide_rows] + coarse_faces + fine_faces, 60_000_000,
    )
    u1 = [middle, *swap_faces((m_x, m_l, m_f))]
    value, *results = call(
        finish_kernel, "finish", first, [velocity, grads, *u1, *rest],
        [fine] + fine_faces + [coarse], [ext, summed, rows], 40_000_000,
    )
    faces, end_two = results[:3], results[3]
    u0 = pass_on(range(slabs - 1), value)
    u2 = [value, *swap_faces(faces)]

    own_part, following, *sent = call(
        offset_later_kernel, "offset_later", first,
        [velocity, grads, start_field, *start_layers, *u1, *u2, zero, end_two],
        [coarse, coarse, (6, cx, cy, cz)] + coarse_faces,
        [ext, ext, summed, summed, rows], 60_000_000,
    )
    arrivals = chain(pass_later_kernel, sent, (6, cx, cy, cz), [], [own_part, following])
    stage, *faces, begin, rest = call(
        lambda *refs: settle_later_kernel(slabs - 1, *refs), "settle", first,
        [*arrivals, own_part, speed, coarse_grads, start_field, u0, middle, value],
        [fine] + fine_faces + [fine, fine],
        [coarse, *coarse_faces, coarse, coarse_ext, summed, summed, rows], 10_000_000,
    )
    middle, stage, *faces = call(
        stage_kernel, "stage", first, [velocity, grads, stage, *swap_faces(faces), begin, rest],
        [fine, fine] + fine_faces, [ext], 40_000_000,
    )
    result, = call(
        stage_kernel, "stage", first, [velocity, grads, stage, *swap_faces(faces), middle],
        [fine], [ext], 40_000_000,
    )
    return result[None]


def solution(mesh):
    in_specs = (
        P(None, "gx", "gy", None),
        P(None, "gx", "gy", None),
        P("tm", None, "gx", "gy", None),
    )
    out_specs = P("tm", None, "gx", "gy", None)
    return jax.shard_map(shards, mesh=mesh, in_specs=in_specs, out_specs=out_specs, check_vma=False)
```

```python
import math

import jax
import jax.numpy as jnp
from jax import lax
from jax.experimental import pallas as pl
from jax.experimental.pallas import tpu as pltpu
from jax.sharding import PartitionSpec as P

VISCOSITY = 0.25
TIME_STEP = 0.5
PAD = 8
CHUNK = 8
ROOM = 4 << 20
F32 = jnp.float32
BF16 = jnp.bfloat16


def ring(size, by):
    return [(i, (i + by) % size) for i in range(size)]


def both_faces(faces, permute, size):
    if size == 2:
        return permute(faces, 1)
    before = permute(faces[:, 0:1], 1)
    after = permute(faces[:, 1:2], -1)
    return jnp.concatenate([before, after], axis=1)


def swap_faces(faces):
    x_faces, y_last, y_first = faces
    gx, gy = lax.axis_size("gx"), lax.axis_size("gy")
    before_after = both_faces(x_faces, lambda a, by: lax.ppermute(a, "gx", ring(gx, by)), gx)
    behind = lax.ppermute(y_last, "gy", ring(gy, 1))
    ahead = lax.ppermute(y_first, "gy", ring(gy, -1))
    return before_after, behind, ahead


def pass_on(slabs, array, dx=0, dy=0):
    gx, gy = lax.axis_size("gx"), lax.axis_size("gy")
    pairs = []
    for t in slabs:
        for x in range(gx):
            for y in range(gy):
                source = (t * gx + x) * gy + y
                target = ((t + 1) * gx + (x + dx) % gx) * gy + (y + dy) % gy
                pairs.append((source, target))
    return lax.ppermute(array, ("tm", "gx", "gy"), pairs)


def hand_on(slabs, value, faces):
    x_faces, y_last, y_first = faces
    main = pass_on(slabs, value)
    behind = pass_on(slabs, y_last, 0, 1)
    ahead = pass_on(slabs, y_first, 0, -1)
    before_after = both_faces(x_faces, lambda a, by: pass_on(slabs, a, by, 0), lax.axis_size("gx"))
    return [main, behind, ahead, before_after]


class Node:
    def __init__(self, main, x_faces, behind, ahead, off=0):
        self.main, self.x_faces, self.behind, self.ahead, self.off = main, x_faces, behind, ahead, off


def packed_rows(width, length):
    return width * length + 2 * length + 2 * width


class Reader:
    def __init__(self, read):
        self.read = read

    def __getitem__(self, key):
        return self.read(*key)


def packed_node(ref, width, length):
    inner = width * length

    def main(c, x, rows=slice(0, length)):
        begin = pl.multiple_of(x * length + rows.start, 8)
        return ref[c, pl.ds(begin, rows.stop - rows.start)]

    def x_layer(c, k):
        return ref[c, inner + k * length : inner + (k + 1) * length]

    def y_layer(base):
        return Reader(lambda c, row: ref[c, pl.ds(base + row.start, 1)])

    base = inner + 2 * length
    return Node(Reader(main), Reader(x_layer), y_layer(base), y_layer(base + width))


def emit_packed(node, ref):
    width, length = node.main.shape[1:3]
    inner = width * length
    base = inner + 2 * length
    for c in range(3):
        ref[c, 0:inner] = node.main[c].reshape(inner, ref.shape[2])
        for k in range(2):
            ref[c, inner + k * length : inner + (k + 1) * length] = node.x_faces[c, k]
        ref[c, base : base + width] = node.behind[c]
        ref[c, base + width : base + 2 * width] = node.ahead[c]


class Mix:
    def __init__(self, *parts):
        self.parts, self.shape = parts, parts[0][1].shape

    def __getitem__(self, key):
        return total([w * field[key] for w, field in self.parts])


def scaled(weight, value):
    return value if isinstance(weight, float) and weight == 1.0 else weight * value


def total(terms):
    result = terms[0]
    for term in terms[1:]:
        result = result + term
    return result


def each(count, unrolled=False):
    def wrap(body):
        if unrolled:
            for i in range(count):
                body(i)
        else:
            pl.loop(0, count)(body)

    return wrap


def fill(ext, parts, spread=(), unrolled=False):
    width, length = ext.shape[1] - 2, ext.shape[2] - 2 * PAD
    inner = slice(PAD, PAD + length)
    for c in range(3):
        for k, at in ((0, 0), (1, width + 1)):
            terms = [scaled(w, n.x_faces[n.off + c, k]) for w, n in parts]
            terms += [w * p[c, k * (width // 2 + 1)] for w, p, _ in spread]
            ext[c, at, inner] = total(terms)

    @each(width // 2, unrolled)
    def _(i):
        for q in range(2):
            x = 2 * i + q
            for c in range(3):
                terms = [scaled(w, n.main[c, x]) for w, n in parts]
                terms += [w * p[c, i + 1] for w, p, _ in spread]
                ext[c, x + 1, inner] = total(terms)
                row = pl.ds(x, 1)
                for k, at in ((0, PAD - 1), (1, PAD + length)):
                    terms = [scaled(w, (n.ahead if k else n.behind)[n.off + c, row]) for w, n in parts]
                    terms += [w * e[k, c, pl.ds(i, 1)] for w, _, e in spread]
                    ext[c, x + 1, at : at + 1] = total(terms)


def turned(value, by):
    return pltpu.roll(value, by % value.shape[-1], value.ndim - 1)


def sides(ext, c, x, r, n):
    here = ext[c, x, r : r + n]
    return (
        here,
        (ext[c, x + 1, r : r + n], ext[c, x, r + 1 : r + 1 + n], turned(here, -1)),
        (ext[c, x - 1, r : r + n], ext[c, x, r - 1 : r - 1 + n], turned(here, 1)),
    )


def rates(ext, x, r, n, speeds, grads_of, strength):
    here = [ext[b, x, r : r + n] for b in range(3)]
    toward = [strength - speed for speed in speeds]
    away = [strength + speed for speed in speeds]
    outputs = []
    for a in range(3):
        _, ahead, behind = sides(ext, a, x, r, n)
        grads = grads_of(a)
        result = here[a] * (grads[a] - 6.0 * strength)
        for b in range(3):
            if b != a:
                result = result + here[b] * grads[b]
            result = result + toward[b] * ahead[b] + away[b] * behind[b]
        outputs.append(result)
    return outputs


def slopes(half, a, x, r, n):
    _, ahead, behind = sides(half, a, x, r, n)
    return [ahead[b] - behind[b] for b in range(3)]


def fine_rates(ext, v, grads, x, r, n):
    speeds = [0.5 * v[b, x, r : r + n] for b in range(3)]

    def grads_of(a):
        return [grads[3 * a + b, x, r : r + n] for b in range(3)]

    return rates(ext, x + 1, PAD + r, n, speeds, grads_of, VISCOSITY)


def split(value):
    high = value.astype(BF16)
    low = (value - high.astype(F32)).astype(BF16)
    return high, low


def pair_table(rows, columns, by_row, entry):
    i = lax.broadcasted_iota(jnp.int32, (rows, columns), 0)
    j = lax.broadcasted_iota(jnp.int32, (rows, columns), 1)
    same = (i >> 1) == j if by_row else i == (j >> 1)
    return jnp.where(same, entry, 0.0).astype(BF16)


def squeeze(summed, rows, store, count):
    cx, y, z = summed.shape[1:]
    table = pair_table(z, z // 2, True, 0.125)
    for c in range(count):
        high, low = split(summed[c].reshape(cx * y, z))
        rows[...] = jnp.dot(high, table, preferred_element_type=F32) + jnp.dot(
            low, table, preferred_element_type=F32
        )
        half = cx * y // 2
        value = rows[pl.ds(0, half, stride=2)] + rows[pl.ds(1, half, stride=2)]
        store(c, value.reshape(cx, y // 2, z // 2))


def spread_along(value):
    cz = value.shape[1]
    single = pair_table(cz, 2 * cz, False, 1.0)
    table = jnp.concatenate([single, single], axis=0)
    high, low = split(value)
    return jnp.dot(jnp.concatenate([high, low], axis=1), table, preferred_element_type=F32)


def doubled(value, rows):
    count = value.shape[0]
    rows[pl.ds(0, count, stride=2)] = value
    rows[pl.ds(1, count, stride=2)] = value
    return rows[...]


def prolong_own(main, wide, rows):
    cx, cy, cz = main.shape[1:]
    for c in range(3):
        value = doubled(main[c].reshape(cx * cy, cz), rows)
        wide[c] = spread_along(value).reshape(cx, 2 * cy, 2 * cz)


def prolong(field, wide, edge, rows):
    cx, cy, cz = field.main.shape[1:]
    edges = []
    for c in range(3):
        layers = [field.x_faces[c, 0:1], field.main[c], field.x_faces[c, 1:2]]
        value = doubled(jnp.concatenate(layers, axis=0).reshape((cx + 2) * cy, cz), rows)
        wide[c] = spread_along(value).reshape(cx + 2, 2 * cy, 2 * cz)
        edges += [field.behind[c], field.ahead[c]]
    value = spread_along(jnp.concatenate(edges, axis=0))
    for c in range(3):
        for k in range(2):
            at = (2 * c + k) * cx
            edge[k, c] = value[at : at + cx]


def emit_faces(main, outs, off=0):
    x_faces, y_last, y_first = outs
    width, length = main.shape[1:3]
    for c in range(3):
        x_faces[off + c, 0] = main[c, width - 1]
        x_faces[off + c, 1] = main[c, 0]
        for x in range(width):
            y_last[off + c, x : x + 1] = main[c, x, length - 1 : length]
            y_first[off + c, x : x + 1] = main[c, x, 0:1]


def quadrant(c, rows, columns):
    up, along = c // 2, c % 2
    return slice(up * rows, (up + 1) * rows), slice(along * columns, (along + 1) * columns)


def emit_coarse_faces(main, outs, comp):
    x_faces, y_last, y_first = outs
    cx, cy, cz = main.shape[1:]
    for c in range(3):
        x_faces[(comp, 0) + quadrant(c, cy, cz)] = main[c, cx - 1]
        x_faces[(comp, 1) + quadrant(c, cy, cz)] = main[c, 0]
        rows, columns = quadrant(c, cx, cz)
        for i in range(cx):
            at = slice(rows.start + i, rows.start + i + 1)
            y_last[comp, at, columns] = main[c, i, cy - 1 : cy]
            y_first[comp, at, columns] = main[c, i, 0:1]


def take_coarse_faces(x_faces, behind, ahead, comp, outs):
    out_x, out_b, out_a = outs
    cy, cz = out_x.shape[2:]
    cx = out_b.shape[1]
    for c in range(3):
        for k in range(2):
            out_x[c, k] = x_faces[(comp, k) + quadrant(c, cy, cz)]
        out_b[c] = behind[(comp,) + quadrant(c, cx, cz)]
        out_a[c] = ahead[(comp,) + quadrant(c, cx, cz)]


def coarsen(field, summed, rows, store):
    @pl.loop(0, field.shape[1] // 2)
    def _(i):
        for c in range(3):
            summed[c, i] = field[c, 2 * i] + field[c, 2 * i + 1]

    squeeze(summed, rows, store, 3)


def offset_mix(f, s, g):
    return Mix((f / 6.0, s), (1.0 - f / 6.0, g))


def pack_kernel(first, v, s, g, end, x_faces, y_last, y_first, summed, rows):
    outs = (x_faces, y_last, y_first)
    emit_faces(v, outs, 0)
    emit_faces(offset_mix(first[0], s, g), outs, 3)

    def store(c, value):
        end[c] = value

    coarsen(g, summed, rows, store)
    emit_coarse_faces(end, outs, 6)


def coarsen_kernel(first, v, s, end, speed, zero, summed, rows):
    f = first[0]

    def store_zero(c, value):
        zero[c] = f * value + (1.0 - f) * end[c]

    def store_speed(c, value):
        speed[c] = value * 0.25

    coarsen(s, summed, rows, store_zero)
    coarsen(v, summed, rows, store_speed)


def offset_start_kernel(
    first, v, s, g, x_faces, behind, ahead, zero,
    grads, integral, coarse_grads, zero_x, zero_b, zero_a, end, end_x, end_l, end_f,
    ext, half, summed, grads_summed, rows,
):
    f = first[0]
    fill(half, [(0.5, Node(v, x_faces, behind, ahead))])
    fill(ext, [(TIME_STEP, Node(offset_mix(f, s, g), x_faces, behind, ahead, 3))])
    width, length = v.shape[1:3]
    n = min(CHUNK, length)

    @pl.loop(0, width // 2)
    def _(i):
        for r in range(0, length, n):
            at = slice(r, r + n)
            for q in range(2):
                x = 2 * i + q
                for a in range(3):
                    row = slopes(half, a, x + 1, PAD + r, n)
                    for b in range(3):
                        grads[3 * a + b, x, at] = row[b]
                        if q:
                            row[b] = row[b] + grads_summed[3 * a + b, i, at]
                        grads_summed[3 * a + b, i, at] = row[b]
            pair = [fine_rates(ext, v, grads, 2 * i + q, r, n) for q in range(2)]
            for a in range(3):
                summed[a, i, at] = pair[0][a] + pair[1][a]

    def store(c, value):
        integral[c] = value
        end[c] = zero[c] + value

    squeeze(summed, rows, store, 3)
    emit_faces(end, (end_x, end_l, end_f))
    take_coarse_faces(x_faces, behind, ahead, 6, (zero_x, zero_b, zero_a))

    def store_grads(c, value):
        coarse_grads[c] = value

    squeeze(grads_summed, rows, store_grads, 9)


def offset_later_kernel(
    first, v, grads, s, x_faces, behind, ahead,
    u1, u1_x, u1_b, u1_a, u2, u2_x, u2_b, u2_a, zero, end_two,
    own, following, sent, sent_x, sent_l, sent_f, bulk,
    ext, ext_two, summed, summed_two, rows,
):
    f = first[0]
    sixth = TIME_STEP / 6.0
    last = Node(u2, u2_x, u2_b, u2_a)
    emit_packed(last, bulk)
    fill(ext_two, [(sixth, last)])
    fill(
        ext,
        [
            (f * sixth, Node(s, x_faces, behind, ahead)),
            (TIME_STEP * 2.0 / 3.0, Node(u1, u1_x, u1_b, u1_a)),
            (sixth, last),
        ],
    )
    width, length = v.shape[1:3]
    n = min(CHUNK, length)

    @pl.loop(0, width // 2)
    def _(i):
        for r in range(0, length, n):
            at = slice(r, r + n)
            pair = [fine_rates(ext, v, grads, 2 * i + q, r, n) for q in range(2)]
            for a in range(3):
                summed[a, i, at] = pair[0][a] + pair[1][a]
            pair = [fine_rates(ext_two, v, grads, 2 * i + q, r, n) for q in range(2)]
            for a in range(3):
                summed_two[a, i, at] = (pair[0][a] + u2[a, 2 * i, at]) + (pair[1][a] + u2[a, 2 * i + 1, at])

    def store(c, value):
        own[c] = value + (f * zero[c] - end_two[c])
        sent[c] = own[c]

    squeeze(summed, rows, store, 3)
    emit_faces(own, (sent_x, sent_l, sent_f))

    def store_following(c, value):
        following[c] = value
        sent[3 + c] = value

    squeeze(summed_two, rows, store_following, 3)


def chain_step(base, speed, coarse_grads, d0, ext, store):
    fill(ext, [(TIME_STEP, Node(*d0))], unrolled=True)
    width, length = speed.shape[1:3]
    for x in range(width):
        speeds = [speed[b, x] for b in range(3)]

        def grads_of(a):
            return [coarse_grads[3 * a + b, x] for b in range(3)]

        changes = rates(ext, x + 1, PAD, length, speeds, grads_of, VISCOSITY / 4.0)
        for a in range(3):
            store(a, x, base(a, x) + d0[0][a, x] + changes[a])


def arrival(refs):
    main, behind, ahead, x_faces = refs
    return main, x_faces, behind, ahead


def pass_start_kernel(turn, first, *refs):
    arrived, zero = arrival(refs[:4]), refs[4:8]
    integral, speed, coarse_grads, end, end_x, end_l, end_f = refs[8:15]
    d0, ext = refs[15:19], refs[19]

    @pl.when(first[1] == float(turn))
    def _():
        def base(a, x):
            return zero[0][a, x] + integral[a, x]

        def store(a, x, value):
            end[a, x] = value

        for k in range(4):
            d0[k][...] = arrived[k][...] - zero[k][...]
        chain_step(base, speed, coarse_grads, d0, ext, store)
        emit_faces(end, (end_x, end_l, end_f))


def settle_start_kernel(count, first, *refs):
    arrived = [arrival(refs[4 * k : 4 * k + 4]) for k in range(count)]
    refs = refs[4 * count :]
    zero, (integral, speed, coarse_grads, end_two, s) = refs[:4], refs[4:9]
    d0, d2, outs, ext = refs[9:13], refs[13], refs[14:17], refs[17]
    rest = 1.0 - first[0]

    def base(a, x):
        return zero[0][a, x] + integral[a, x] - end_two[a, x]

    def store(a, x, value):
        d2[a, x] = value

    for k in range(4):
        d0[k][...] = rest * (total([group[k][...] for group in arrived]) - zero[k][...])
    chain_step(base, speed, coarse_grads, d0, ext, store)
    emit_faces(s, outs, 0)
    emit_coarse_faces(d2, outs, 3)


def pass_later_kernel(turn, first, *refs):
    arrived, (own, following, speed, coarse_grads) = arrival(refs[:4]), refs[4:8]
    sent, sent_x, sent_l, sent_f, ext = refs[8:13]

    @pl.when(first[1] == float(turn))
    def _():
        def base(a, x):
            return own[a, x] + arrived[0][3 + a, x]

        def store(a, x, value):
            sent[a, x] = value
            sent[3 + a, x] = following[a, x]

        chain_step(base, speed, coarse_grads, arrived, ext, store)
        emit_faces(sent, (sent_x, sent_l, sent_f))


def settle_later_kernel(count, first, *refs):
    arrived = [arrival(refs[4 * k : 4 * k + 4]) for k in range(count)]
    own, speed, coarse_grads, s, u1, u2, stage, stage_x, stage_l, stage_f, begin, rest = refs[4 * count : 4 * count + 12]
    d0, (d2, ext, wide0, wide2, rows) = refs[4 * count + 12 : 4 * count + 16], refs[4 * count + 16 :]
    f = first[0]

    def base(a, x):
        return own[a, x] + total([group[0][3 + a, x] for group in arrived])

    def store(a, x, value):
        d2[a, x] = value

    d0[0][...] = total([group[0][0:3] for group in arrived])
    for k in range(1, 4):
        d0[k][...] = total([group[k][...] for group in arrived])
    chain_step(base, speed, coarse_grads, d0, ext, store)
    prolong_own(d0[0], wide0, rows)
    prolong_own(d2, wide2, rows)

    @pl.loop(0, u1.shape[1] // 2)
    def _(i):
        for c in range(3):
            p0, p2 = wide0[c, i], wide2[c, i]
            toward_stage = TIME_STEP * (0.375 * p0 + 0.125 * p2)
            toward_rest = 0.125 * (p2 - p0)
            for q in range(2):
                x = 2 * i + q
                start, one, two = f * s[c, x], u1[c, x], u2[c, x]
                stage[c, x] = toward_stage + TIME_STEP * (start * (5.0 / 24.0) + one / 3.0 - two / 24.0)
                begin[c, x] = start + p0
                rest[c, x] = toward_rest + (two * (5.0 / 24.0) - one / 6.0 - start / 24.0)

    emit_faces(stage, (stage_x, stage_l, stage_f))


def first_stage_kernel(first, v, grads, y, y_x, y_b, y_a, begin, rest, bulk, out, stage, stage_x, stage_l, stage_f, ext):
    width, length = v.shape[1:3]
    arrived = packed_node(bulk, width, length)
    fill(ext, [(1.0, Node(y, y_x, y_b, y_a)), (TIME_STEP * 5.0 / 24.0, arrived)])
    n = min(CHUNK, length)

    @pl.loop(0, width)
    def _(x):
        for r in range(0, length, n):
            at = slice(r, r + n)
            changes = fine_rates(ext, v, grads, x, r, n)
            for a in range(3):
                start = arrived.main[a, x, at]
                value = begin[a, x, at] + start + changes[a]
                out[a, x, at] = value
                stage[a, x, at] = TIME_STEP * (0.5 * value + (rest[a, x, at] - start / 24.0))

    emit_faces(stage, (stage_x, stage_l, stage_f))


def last_stage_kernel(first, v, grads, y, y_x, y_b, y_a, begin, out, ext):
    fill(ext, [(1.0, Node(y, y_x, y_b, y_a))])
    width, length = v.shape[1:3]
    n = min(CHUNK, length)

    @pl.loop(0, width)
    def _(x):
        for r in range(0, length, n):
            changes = fine_rates(ext, v, grads, x, r, n)
            for a in range(3):
                out[a, x, r : r + n] = begin[a, x, r : r + n] + changes[a]


def middle_kernel(
    first, v, grads, s, g, w_x, w_b, w_a, d0, d0_x, d0_b, d0_a, d2, m_x, m_b, m_a,
    a1, a1_x, a1_l, a1_f, rest, rest_x, rest_b, rest_a,
    ext, wide0, edge0, wide2, edge2, rows, d2_x, d2_b, d2_a, g_x, g_b, g_a,
):
    f = first[0]
    take_coarse_faces(m_x, m_b, m_a, 3, (d2_x, d2_b, d2_a))
    for out, mixed, start, off in ((g_x, w_x, m_x, 3), (g_b, w_b, m_b, 3), (g_a, w_a, m_a, 3)):
        for c in range(3):
            out[c] = (1.0 + 0.2 * f) * mixed[off + c] - (0.2 * f) * start[c]
    parts = [Node(s, m_x, m_b, m_a), Node(g, g_x, g_b, g_a)]
    begin = list(zip((f, 1.0 - f), parts))
    first_stage = list(zip((5.0 / 24.0 * f, 0.5 - 5.0 / 24.0 * f), parts))
    second_stage = list(zip((f / -24.0, f / 24.0), parts))
    prolong(Node(d0, d0_x, d0_b, d0_a), wide0, edge0, rows)
    prolong(Node(d2, d2_x, d2_b, d2_a), wide2, edge2, rows)
    fill(
        ext,
        [(TIME_STEP * w, node) for w, node in first_stage],
        [(TIME_STEP * 0.375, wide0, edge0), (TIME_STEP * 0.125, wide2, edge2)],
    )
    width, length = a1.shape[1:3]
    n = min(CHUNK, length)
    last_cx = width // 2 + 1

    def rest_of(get, p0, p2):
        return total([w * get(node) for w, node in second_stage]) + 0.125 * (p2 - p0)

    for c in range(3):
        for k in range(2):
            rest_x[c, k] = rest_of(
                lambda nd: nd.x_faces[nd.off + c, k], wide0[c, k * last_cx], wide2[c, k * last_cx]
            )

    @pl.loop(0, width // 2)
    def _(i):
        for q in range(2):
            x = 2 * i + q
            row = pl.ds(x, 1)
            for r in range(0, length, n):
                changes = fine_rates(ext, v, grads, x, r, n)
                for a in range(3):
                    p0, p2 = wide0[a, i + 1, r : r + n], wide2[a, i + 1, r : r + n]
                    start = total([w * nd.main[a, x, r : r + n] for w, nd in begin])
                    a1[a, x, r : r + n] = start + p0 + changes[a]
                    rest[a, x, r : r + n] = rest_of(lambda nd: nd.main[a, x, r : r + n], p0, p2)
            for c in range(3):
                p0, p2 = edge0[0, c, pl.ds(i, 1)], edge2[0, c, pl.ds(i, 1)]
                rest_b[c, row] = rest_of(lambda nd: nd.behind[nd.off + c, row], p0, p2)
                p0, p2 = edge0[1, c, pl.ds(i, 1)], edge2[1, c, pl.ds(i, 1)]
                rest_a[c, row] = rest_of(lambda nd: nd.ahead[nd.off + c, row], p0, p2)

    emit_faces(a1, (a1_x, a1_l, a1_f))


def finish_kernel(
    first, v, grads, a1, a1_x, a1_b, a1_a, rest, rest_x, rest_b, rest_a,
    a2, a2_x, a2_l, a2_f, end, ext, summed, rows,
):
    fill(
        ext,
        [
            (TIME_STEP * 0.5, Node(a1, a1_x, a1_b, a1_a)),
            (TIME_STEP, Node(rest, rest_x, rest_b, rest_a)),
        ],
    )
    width, length = a1.shape[1:3]
    n = min(CHUNK, length)

    @pl.loop(0, width // 2)
    def _(i):
        for r in range(0, length, n):
            pair = []
            for q in range(2):
                x = 2 * i + q
                changes = fine_rates(ext, v, grads, x, r, n)
                pair.append([a1[a, x, r : r + n] + changes[a] for a in range(3)])
                for a in range(3):
                    a2[a, x, r : r + n] = pair[q][a]
            for a in range(3):
                summed[a, i, r : r + n] = pair[0][a] + pair[1][a]

    emit_faces(a2, (a2_x, a2_l, a2_f))

    def store(c, value):
        end[c] = value

    squeeze(summed, rows, store, 3)


def call(kernel, name, first, args, outs, scratch, flops=0, least=0):
    moved = sum(4 * a.size for a in args)
    room = moved + sum(4 * math.prod(dims) for dims in outs + scratch)
    return pl.pallas_call(
        kernel,
        name=name,
        out_shape=[jax.ShapeDtypeStruct(dims, F32) for dims in outs],
        in_specs=[pl.BlockSpec(memory_space=pltpu.SMEM)] + [pl.BlockSpec(memory_space=pltpu.VMEM)] * len(args),
        out_specs=[pl.BlockSpec(memory_space=pltpu.VMEM)] * len(outs),
        scratch_shapes=[pltpu.VMEM(dims, F32) for dims in scratch],
        compiler_params=pltpu.CompilerParams(vmem_limit_bytes=min(max(room + ROOM, least), 56 << 20)),
        cost_estimate=pl.CostEstimate(flops=flops, bytes_accessed=moved, transcendentals=0),
    )(first, *args)


def shards(velocity, start_field, guess):
    own = guess[0]
    _, nx, ny, nz = own.shape
    cx, cy, cz = nx // 2, ny // 2, nz // 2
    slabs = lax.axis_size("tm")
    number = lax.axis_index("tm")
    first = jnp.stack([number == 0, number]).astype(F32)

    def layers_of(count):
        return [(count, 2, ny, nz), (count, nx, nz), (count, nx, nz)]

    fine, coarse = (3, nx, ny, nz), (3, cx, cy, cz)
    fine_faces, coarse_faces = layers_of(3), [(3, 2, cy, cz), (3, cx, cz), (3, cx, cz)]
    ext = (3, nx + 2, ny + 2 * PAD, nz)
    coarse_ext = (3, cx + 2, cy + 2 * PAD, cz)
    summed, rows = (3, cx, ny, nz), (cx * ny, cz)
    wide, edge, wide_rows = (3, cx + 2, ny, nz), (2, 3, cx, nz), ((cx + 2) * ny, cz)

    end_two, *packed = call(
        pack_kernel, "pack", first, [velocity, start_field, own],
        [coarse] + layers_of(7), [summed, rows], 5_000_000, 56 << 20,
    )
    layers = swap_faces(packed)
    speed, zero = call(
        coarsen_kernel, "coarsen", first, [velocity, start_field, end_two],
        [coarse, coarse], [summed, rows], 10_000_000,
    )
    grads, integral, coarse_grads, *results = call(
        offset_start_kernel, "offset_start", first, [velocity, start_field, own, *layers, zero],
        [(9, nx, ny, nz), coarse, (9, cx, cy, cz)] + coarse_faces + [coarse] + coarse_faces,
        [ext, ext, summed, (9, cx, ny, nz), rows], 40_000_000,
    )
    zero_faces, sent = results[:3], results[3:]

    def chain(step, sent, outs, scratch, own_terms, bulk=None):
        arrivals = []
        for turn in range(1, slabs):
            arrivals += hand_on([turn - 1], sent[0], sent[1:])
            if turn + 1 < slabs:
                sent = call(
                    lambda *refs, turn=turn: step(turn, *refs), "chain", first,
                    [*arrivals[-4:], *own_terms, speed, coarse_grads],
                    [outs] + coarse_faces, scratch + [coarse_ext], 2_000_000,
                )
            if turn == 1 and bulk is not None:
                *sent, bulk = lax.optimization_barrier([*sent, bulk])
                bulk = pass_on(range(slabs - 1), bulk)
        return arrivals, bulk

    terms = [zero, *zero_faces, integral]
    arrivals, _ = chain(pass_start_kernel, sent, coarse, [coarse] + coarse_faces, terms)
    results = call(
        lambda *refs: settle_start_kernel(slabs - 1, *refs), "settle", first,
        [*arrivals, *terms, speed, coarse_grads, end_two, start_field],
        [coarse] + coarse_faces + [coarse] + layers_of(4), [coarse_ext], 2_000_000,
    )
    start_layers = swap_faces(results[5:])
    middle, m_x, m_l, m_f, *rest = call(
        middle_kernel, "middle", first,
        [velocity, grads, start_field, own, *layers, *results[:5], *start_layers],
        [fine] + fine_faces + [fine] + fine_faces,
        [ext, wide, edge, wide, edge, wide_rows] + coarse_faces + fine_faces, 60_000_000,
    )
    u1 = [middle, *swap_faces((m_x, m_l, m_f))]
    value, *results = call(
        finish_kernel, "finish", first, [velocity, grads, *u1, *rest],
        [fine] + fine_faces + [coarse], [ext, summed, rows], 40_000_000,
    )
    faces, end_two = results[:3], results[3]
    u2 = [value, *swap_faces(faces)]

    own_part, following, *sent, bulk = call(
        offset_later_kernel, "offset_later", first,
        [velocity, grads, start_field, *start_layers, *u1, *u2, zero, end_two],
        [coarse, coarse, (6, cx, cy, cz)] + coarse_faces + [(3, packed_rows(nx, ny), nz)],
        [ext, ext, summed, summed, rows], 60_000_000,
    )
    arrivals, bulk = chain(pass_later_kernel, sent, (6, cx, cy, cz), [], [own_part, following], bulk)
    stage, *faces, begin, rest = call(
        lambda *refs: settle_later_kernel(slabs - 1, *refs), "settle", first,
        [*arrivals, own_part, speed, coarse_grads, start_field, middle, value],
        [fine] + fine_faces + [fine, fine],
        [coarse, *coarse_faces, coarse, coarse_ext, summed, summed, rows], 10_000_000,
    )
    middle, stage, *faces = call(
        first_stage_kernel, "stage", first, [velocity, grads, stage, *swap_faces(faces), begin, rest, bulk],
        [fine, fine] + fine_faces, [ext], 40_000_000,
    )
    result, = call(
        last_stage_kernel, "stage", first, [velocity, grads, stage, *swap_faces(faces), middle],
        [fine], [ext], 40_000_000,
    )
    return result[None]


def solution(mesh):
    in_specs = (
        P(None, "gx", "gy", None),
        P(None, "gx", "gy", None),
        P("tm", None, "gx", "gy", None),
    )
    out_specs = P("tm", None, "gx", "gy", None)
    return jax.shard_map(shards, mesh=mesh, in_specs=in_specs, out_specs=out_specs, check_vma=False)
```

```python
import math

import jax
import jax.numpy as jnp
from jax import lax
from jax.experimental import pallas as pl
from jax.experimental.pallas import tpu as pltpu
from jax.sharding import PartitionSpec as P

VISCOSITY = 0.25
TIME_STEP = 0.5
PAD = 8
CHUNK = 16
ROOM = 4 << 20
F32 = jnp.float32
BF16 = jnp.bfloat16


def ring(size, by):
    return [(i, (i + by) % size) for i in range(size)]


def both_faces(faces, permute, size):
    if size == 2:
        return permute(faces, 1)
    before = permute(faces[:, 0:1], 1)
    after = permute(faces[:, 1:2], -1)
    return jnp.concatenate([before, after], axis=1)


def swap_faces(faces):
    x_faces, y_last, y_first = faces
    gx, gy = lax.axis_size("gx"), lax.axis_size("gy")
    before_after = both_faces(x_faces, lambda a, by: lax.ppermute(a, "gx", ring(gx, by)), gx)
    behind = lax.ppermute(y_last, "gy", ring(gy, 1))
    ahead = lax.ppermute(y_first, "gy", ring(gy, -1))
    return before_after, behind, ahead


def pass_on(slabs, array, dx=0, dy=0):
    gx, gy = lax.axis_size("gx"), lax.axis_size("gy")
    pairs = []
    for t in slabs:
        for x in range(gx):
            for y in range(gy):
                source = (t * gx + x) * gy + y
                target = ((t + 1) * gx + (x + dx) % gx) * gy + (y + dy) % gy
                pairs.append((source, target))
    return lax.ppermute(array, ("tm", "gx", "gy"), pairs)


def hand_on(slabs, value, faces):
    x_faces, y_last, y_first = faces
    main = pass_on(slabs, value)
    behind = pass_on(slabs, y_last, 0, 1)
    ahead = pass_on(slabs, y_first, 0, -1)
    before_after = both_faces(x_faces, lambda a, by: pass_on(slabs, a, by, 0), lax.axis_size("gx"))
    return [main, behind, ahead, before_after]


class Node:
    def __init__(self, main, x_faces, behind, ahead, off=0):
        self.main, self.x_faces, self.behind, self.ahead, self.off = main, x_faces, behind, ahead, off


class Mix:
    def __init__(self, *parts):
        self.parts, self.shape = parts, parts[0][1].shape

    def __getitem__(self, key):
        return total([w * field[key] for w, field in self.parts])


def scaled(weight, value):
    return value if isinstance(weight, float) and weight == 1.0 else weight * value


def total(terms):
    result = terms[0]
    for term in terms[1:]:
        result = result + term
    return result


def each(count, unrolled=False):
    def wrap(body):
        if unrolled:
            for i in range(count):
                body(i)
        else:
            pl.loop(0, count)(body)

    return wrap


def fill(ext, parts, spread=(), unrolled=False):
    width, length = ext.shape[1] - 2, ext.shape[2] - 2 * PAD
    inner = slice(PAD, PAD + length)
    for c in range(3):
        for k, at in ((0, 0), (1, width + 1)):
            terms = [scaled(w, n.x_faces[n.off + c, k]) for w, n in parts]
            terms += [w * p[c, k * (width // 2 + 1)] for w, p, _ in spread]
            ext[c, at, inner] = total(terms)

    @each(width // 2, unrolled)
    def _(i):
        for q in range(2):
            x = 2 * i + q
            for c in range(3):
                terms = [scaled(w, n.main[c, x]) for w, n in parts]
                terms += [w * p[c, i + 1] for w, p, _ in spread]
                ext[c, x + 1, inner] = total(terms)
                row = pl.ds(x, 1)
                for k, at in ((0, PAD - 1), (1, PAD + length)):
                    terms = [scaled(w, (n.ahead if k else n.behind)[n.off + c, row]) for w, n in parts]
                    terms += [w * e[k, c, pl.ds(i, 1)] for w, _, e in spread]
                    ext[c, x + 1, at : at + 1] = total(terms)


def turned(value, by):
    return pltpu.roll(value, by % value.shape[-1], value.ndim - 1)


def sides(ext, c, x, r, n):
    here = ext[c, x, r : r + n]
    return (
        here,
        (ext[c, x + 1, r : r + n], ext[c, x, r + 1 : r + 1 + n], turned(here, -1)),
        (ext[c, x - 1, r : r + n], ext[c, x, r - 1 : r - 1 + n], turned(here, 1)),
    )


def rates(ext, x, r, n, speeds, grads_of, strength):
    here = [ext[b, x, r : r + n] for b in range(3)]
    toward = [strength - speed for speed in speeds]
    away = [strength + speed for speed in speeds]
    outputs = []
    for a in range(3):
        _, ahead, behind = sides(ext, a, x, r, n)
        grads = grads_of(a)
        result = here[a] * (grads[a] - 6.0 * strength)
        for b in range(3):
            if b != a:
                result = result + here[b] * grads[b]
            result = result + toward[b] * ahead[b] + away[b] * behind[b]
        outputs.append(result)
    return outputs


def slopes(half, a, x, r, n):
    _, ahead, behind = sides(half, a, x, r, n)
    return [ahead[b] - behind[b] for b in range(3)]


def fine_rates(ext, v, grads, x, r, n):
    speeds = [0.5 * v[b, x, r : r + n] for b in range(3)]

    def grads_of(a):
        return [grads[3 * a + b, x, r : r + n] for b in range(3)]

    return rates(ext, x + 1, PAD + r, n, speeds, grads_of, VISCOSITY)


def split(value):
    high = value.astype(BF16)
    low = (value - high.astype(F32)).astype(BF16)
    return high, low


def pair_table(rows, columns, by_row, entry):
    i = lax.broadcasted_iota(jnp.int32, (rows, columns), 0)
    j = lax.broadcasted_iota(jnp.int32, (rows, columns), 1)
    same = (i >> 1) == j if by_row else i == (j >> 1)
    return jnp.where(same, entry, 0.0).astype(BF16)


def squeeze(summed, rows, store, count):
    cx, y, z = summed.shape[1:]
    table = pair_table(z, z // 2, True, 0.125)
    for c in range(count):
        high, low = split(summed[c].reshape(cx * y, z))
        rows[...] = jnp.dot(high, table, preferred_element_type=F32) + jnp.dot(
            low, table, preferred_element_type=F32
        )
        half = cx * y // 2
        value = rows[pl.ds(0, half, stride=2)] + rows[pl.ds(1, half, stride=2)]
        store(c, value.reshape(cx, y // 2, z // 2))


def spread_along(value):
    cz = value.shape[1]
    single = pair_table(cz, 2 * cz, False, 1.0)
    table = jnp.concatenate([single, single], axis=0)
    high, low = split(value)
    return jnp.dot(jnp.concatenate([high, low], axis=1), table, preferred_element_type=F32)


def doubled(value, rows):
    count = value.shape[0]
    rows[pl.ds(0, count, stride=2)] = value
    rows[pl.ds(1, count, stride=2)] = value
    return rows[...]


def prolong_own(main, wide, rows):
    cx, cy, cz = main.shape[1:]
    for c in range(3):
        value = doubled(main[c].reshape(cx * cy, cz), rows)
        wide[c] = spread_along(value).reshape(cx, 2 * cy, 2 * cz)


def prolong(field, wide, edge, rows):
    cx, cy, cz = field.main.shape[1:]
    edges = []
    for c in range(3):
        layers = [field.x_faces[c, 0:1], field.main[c], field.x_faces[c, 1:2]]
        value = doubled(jnp.concatenate(layers, axis=0).reshape((cx + 2) * cy, cz), rows)
        wide[c] = spread_along(value).reshape(cx + 2, 2 * cy, 2 * cz)
        edges += [field.behind[c], field.ahead[c]]
    value = spread_along(jnp.concatenate(edges, axis=0))
    for c in range(3):
        for k in range(2):
            at = (2 * c + k) * cx
            edge[k, c] = value[at : at + cx]


def emit_faces(main, outs, off=0):
    x_faces, y_last, y_first = outs
    width, length = main.shape[1:3]
    for c in range(3):
        x_faces[off + c, 0] = main[c, width - 1]
        x_faces[off + c, 1] = main[c, 0]
        for x in range(width):
            y_last[off + c, x : x + 1] = main[c, x, length - 1 : length]
            y_first[off + c, x : x + 1] = main[c, x, 0:1]


def quadrant(c, rows, columns):
    up, along = c // 2, c % 2
    return slice(up * rows, (up + 1) * rows), slice(along * columns, (along + 1) * columns)


def emit_coarse_faces(main, outs, comp):
    x_faces, y_last, y_first = outs
    cx, cy, cz = main.shape[1:]
    for c in range(3):
        x_faces[(comp, 0) + quadrant(c, cy, cz)] = main[c, cx - 1]
        x_faces[(comp, 1) + quadrant(c, cy, cz)] = main[c, 0]
        rows, columns = quadrant(c, cx, cz)
        for i in range(cx):
            at = slice(rows.start + i, rows.start + i + 1)
            y_last[comp, at, columns] = main[c, i, cy - 1 : cy]
            y_first[comp, at, columns] = main[c, i, 0:1]


def take_coarse_faces(x_faces, behind, ahead, comp, outs):
    out_x, out_b, out_a = outs
    cy, cz = out_x.shape[2:]
    cx = out_b.shape[1]
    for c in range(3):
        for k in range(2):
            out_x[c, k] = x_faces[(comp, k) + quadrant(c, cy, cz)]
        out_b[c] = behind[(comp,) + quadrant(c, cx, cz)]
        out_a[c] = ahead[(comp,) + quadrant(c, cx, cz)]


def coarsen(field, summed, rows, store):
    @pl.loop(0, field.shape[1] // 2)
    def _(i):
        for c in range(3):
            summed[c, i] = field[c, 2 * i] + field[c, 2 * i + 1]

    squeeze(summed, rows, store, 3)


def offset_mix(f, s, g):
    return Mix((f / 6.0, s), (1.0 - f / 6.0, g))


def pack_kernel(v, s, g, end, x_faces, y_last, y_first, summed, rows):
    outs = (x_faces, y_last, y_first)
    emit_faces(v, outs, 0)
    f = jnp.where(lax.axis_index("tm") == 0, 1.0, 0.0)
    emit_faces(offset_mix(f, s, g), outs, 3)

    def store(c, value):
        end[c] = value

    coarsen(g, summed, rows, store)
    emit_coarse_faces(end, outs, 6)


def coarsen_kernel(first, v, s, end, speed, zero, summed, rows):
    f = first[0]

    def store_zero(c, value):
        zero[c] = f * value + (1.0 - f) * end[c]

    def store_speed(c, value):
        speed[c] = value * 0.25

    coarsen(s, summed, rows, store_zero)
    coarsen(v, summed, rows, store_speed)


def offset_start_kernel(
    first, v, s, g, x_faces, behind, ahead, zero,
    grads, integral, coarse_grads, zero_x, zero_b, zero_a, end, end_x, end_l, end_f,
    ext, half, summed, grads_summed, rows,
):
    f = first[0]
    fill(half, [(0.5, Node(v, x_faces, behind, ahead))])
    fill(ext, [(TIME_STEP, Node(offset_mix(f, s, g), x_faces, behind, ahead, 3))])
    width, length = v.shape[1:3]
    n = min(CHUNK, length)

    @pl.loop(0, width // 2)
    def _(i):
        for r in range(0, length, n):
            at = slice(r, r + n)
            for q in range(2):
                x = 2 * i + q
                for a in range(3):
                    row = slopes(half, a, x + 1, PAD + r, n)
                    for b in range(3):
                        grads[3 * a + b, x, at] = row[b]
                        if q:
                            row[b] = row[b] + grads_summed[3 * a + b, i, at]
                        grads_summed[3 * a + b, i, at] = row[b]
            pair = [fine_rates(ext, v, grads, 2 * i + q, r, n) for q in range(2)]
            for a in range(3):
                summed[a, i, at] = pair[0][a] + pair[1][a]

    def store(c, value):
        integral[c] = value
        end[c] = zero[c] + value

    squeeze(summed, rows, store, 3)
    emit_faces(end, (end_x, end_l, end_f))
    take_coarse_faces(x_faces, behind, ahead, 6, (zero_x, zero_b, zero_a))

    def store_grads(c, value):
        coarse_grads[c] = value

    squeeze(grads_summed, rows, store_grads, 9)


def offset_later_kernel(
    first, v, grads, s, x_faces, behind, ahead,
    u1, u1_x, u1_b, u1_a, u2, u2_x, u2_b, u2_a, zero, end_two,
    own, following, sent, sent_x, sent_l, sent_f,
    ext, ext_two, summed, summed_two, rows,
):
    f = first[0]
    sixth = TIME_STEP / 6.0
    last = Node(u2, u2_x, u2_b, u2_a)
    fill(ext_two, [(sixth, last)])
    fill(
        ext,
        [
            (f * sixth, Node(s, x_faces, behind, ahead)),
            (TIME_STEP * 2.0 / 3.0, Node(u1, u1_x, u1_b, u1_a)),
            (sixth, last),
        ],
    )
    width, length = v.shape[1:3]
    n = min(CHUNK, length)

    @pl.loop(0, width // 2)
    def _(i):
        for r in range(0, length, n):
            at = slice(r, r + n)
            pair = [fine_rates(ext, v, grads, 2 * i + q, r, n) for q in range(2)]
            for a in range(3):
                summed[a, i, at] = pair[0][a] + pair[1][a]
            pair = [fine_rates(ext_two, v, grads, 2 * i + q, r, n) for q in range(2)]
            for a in range(3):
                summed_two[a, i, at] = (pair[0][a] + u2[a, 2 * i, at]) + (pair[1][a] + u2[a, 2 * i + 1, at])

    def store(c, value):
        own[c] = value + (f * zero[c] - end_two[c])
        sent[c] = own[c]

    squeeze(summed, rows, store, 3)
    emit_faces(own, (sent_x, sent_l, sent_f))

    def store_following(c, value):
        following[c] = value
        sent[3 + c] = value

    squeeze(summed_two, rows, store_following, 3)


def chain_step(base, speed, coarse_grads, d0, ext, store):
    fill(ext, [(TIME_STEP, Node(*d0))], unrolled=True)
    width, length = speed.shape[1:3]
    for x in range(width):
        speeds = [speed[b, x] for b in range(3)]

        def grads_of(a):
            return [coarse_grads[3 * a + b, x] for b in range(3)]

        changes = rates(ext, x + 1, PAD, length, speeds, grads_of, VISCOSITY / 4.0)
        for a in range(3):
            store(a, x, base(a, x) + d0[0][a, x] + changes[a])


def arrival(refs):
    main, behind, ahead, x_faces = refs
    return main, x_faces, behind, ahead


def pass_start_kernel(turn, first, *refs):
    arrived, zero = arrival(refs[:4]), refs[4:8]
    integral, speed, coarse_grads, end, end_x, end_l, end_f = refs[8:15]
    d0, ext = refs[15:19], refs[19]

    @pl.when(first[1] == float(turn))
    def _():
        def base(a, x):
            return zero[0][a, x] + integral[a, x]

        def store(a, x, value):
            end[a, x] = value

        for k in range(4):
            d0[k][...] = arrived[k][...] - zero[k][...]
        chain_step(base, speed, coarse_grads, d0, ext, store)
        emit_faces(end, (end_x, end_l, end_f))


def settle_start_kernel(count, first, *refs):
    arrived = [arrival(refs[4 * k : 4 * k + 4]) for k in range(count)]
    refs = refs[4 * count :]
    zero, (integral, speed, coarse_grads, end_two, s) = refs[:4], refs[4:9]
    d0, d2, outs, ext = refs[9:13], refs[13], refs[14:17], refs[17]
    rest = 1.0 - first[0]

    def base(a, x):
        return zero[0][a, x] + integral[a, x] - end_two[a, x]

    def store(a, x, value):
        d2[a, x] = value

    for k in range(4):
        d0[k][...] = rest * (total([group[k][...] for group in arrived]) - zero[k][...])
    chain_step(base, speed, coarse_grads, d0, ext, store)
    emit_faces(s, outs, 0)
    emit_coarse_faces(d2, outs, 3)


def pass_later_kernel(turn, first, *refs):
    arrived, (own, following, speed, coarse_grads) = arrival(refs[:4]), refs[4:8]
    sent, sent_x, sent_l, sent_f, ext = refs[8:13]

    @pl.when(first[1] == float(turn))
    def _():
        def base(a, x):
            return own[a, x] + arrived[0][3 + a, x]

        def store(a, x, value):
            sent[a, x] = value
            sent[3 + a, x] = following[a, x]

        chain_step(base, speed, coarse_grads, arrived, ext, store)
        emit_faces(sent, (sent_x, sent_l, sent_f))


def settle_later_kernel(count, first, *refs):
    arrived = [arrival(refs[4 * k : 4 * k + 4]) for k in range(count)]
    own, speed, coarse_grads, s, u0, u1, u2, stage, stage_x, stage_l, stage_f, begin, rest = refs[4 * count : 4 * count + 13]
    d0, (d2, ext, wide0, wide2, rows) = refs[4 * count + 13 : 4 * count + 17], refs[4 * count + 17 :]
    f = first[0]

    def base(a, x):
        return own[a, x] + total([group[0][3 + a, x] for group in arrived])

    def store(a, x, value):
        d2[a, x] = value

    d0[0][...] = total([group[0][0:3] for group in arrived])
    for k in range(1, 4):
        d0[k][...] = total([group[k][...] for group in arrived])
    chain_step(base, speed, coarse_grads, d0, ext, store)
    prolong_own(d0[0], wide0, rows)
    prolong_own(d2, wide2, rows)

    @pl.loop(0, u0.shape[1] // 2)
    def _(i):
        for c in range(3):
            p0, p2 = wide0[c, i], wide2[c, i]
            toward_stage = TIME_STEP * (0.375 * p0 + 0.125 * p2)
            toward_rest = 0.125 * (p2 - p0)
            for q in range(2):
                x = 2 * i + q
                start, one, two = f * s[c, x] + u0[c, x], u1[c, x], u2[c, x]
                stage[c, x] = toward_stage + TIME_STEP * (start * (5.0 / 24.0) + one / 3.0 - two / 24.0)
                begin[c, x] = start + p0
                rest[c, x] = toward_rest + (two * (5.0 / 24.0) - one / 6.0 - start / 24.0)

    emit_faces(stage, (stage_x, stage_l, stage_f))


def first_stage_kernel(first, v, grads, y, y_x, y_b, y_a, begin, rest, out, stage, stage_x, stage_l, stage_f, ext):
    fill(ext, [(1.0, Node(y, y_x, y_b, y_a))])
    width, length = v.shape[1:3]
    n = min(CHUNK, length)

    @pl.loop(0, width)
    def _(x):
        for r in range(0, length, n):
            at = slice(r, r + n)
            changes = fine_rates(ext, v, grads, x, r, n)
            for a in range(3):
                value = begin[a, x, at] + changes[a]
                out[a, x, at] = value
                stage[a, x, at] = TIME_STEP * (0.5 * value + rest[a, x, at])

    emit_faces(stage, (stage_x, stage_l, stage_f))


def last_stage_kernel(v, grads, y, y_x, y_b, y_a, begin, out, ext, made, sent):
    fill(ext, [(1.0, Node(y, y_x, y_b, y_a))])
    width, length = v.shape[1:3]
    n = min(CHUNK, length)

    @pl.loop(0, width)
    def _(x):
        for r in range(0, length, n):
            changes = fine_rates(ext, v, grads, x, r, n)
            for a in range(3):
                made[a, x, r : r + n] = begin[a, x, r : r + n] + changes[a]
        plane = pl.ds(x, 1)
        pltpu.make_async_copy(made.at[:, plane], out.at[:, plane], sent).start()

    pltpu.make_async_copy(made, out, sent).wait()


def middle_kernel(
    first, v, grads, s, g, w_x, w_b, w_a, d0, d0_x, d0_b, d0_a, d2, m_x, m_b, m_a,
    a1, a1_x, a1_l, a1_f, rest, rest_x, rest_b, rest_a,
    ext, wide0, edge0, wide2, edge2, rows, d2_x, d2_b, d2_a, g_x, g_b, g_a,
):
    f = first[0]
    take_coarse_faces(m_x, m_b, m_a, 3, (d2_x, d2_b, d2_a))
    for out, mixed, start, off in ((g_x, w_x, m_x, 3), (g_b, w_b, m_b, 3), (g_a, w_a, m_a, 3)):
        for c in range(3):
            out[c] = (1.0 + 0.2 * f) * mixed[off + c] - (0.2 * f) * start[c]
    parts = [Node(s, m_x, m_b, m_a), Node(g, g_x, g_b, g_a)]
    begin = list(zip((f, 1.0 - f), parts))
    first_stage = list(zip((5.0 / 24.0 * f, 0.5 - 5.0 / 24.0 * f), parts))
    second_stage = list(zip((f / -24.0, f / 24.0), parts))
    prolong(Node(d0, d0_x, d0_b, d0_a), wide0, edge0, rows)
    prolong(Node(d2, d2_x, d2_b, d2_a), wide2, edge2, rows)
    fill(
        ext,
        [(TIME_STEP * w, node) for w, node in first_stage],
        [(TIME_STEP * 0.375, wide0, edge0), (TIME_STEP * 0.125, wide2, edge2)],
    )
    width, length = a1.shape[1:3]
    n = min(CHUNK, length)
    last_cx = width // 2 + 1

    def rest_of(get, p0, p2):
        return total([w * get(node) for w, node in second_stage]) + 0.125 * (p2 - p0)

    for c in range(3):
        for k in range(2):
            rest_x[c, k] = rest_of(
                lambda nd: nd.x_faces[nd.off + c, k], wide0[c, k * last_cx], wide2[c, k * last_cx]
            )

    @pl.loop(0, width // 2)
    def _(i):
        for q in range(2):
            x = 2 * i + q
            row = pl.ds(x, 1)
            for r in range(0, length, n):
                changes = fine_rates(ext, v, grads, x, r, n)
                for a in range(3):
                    p0, p2 = wide0[a, i + 1, r : r + n], wide2[a, i + 1, r : r + n]
                    start = total([w * nd.main[a, x, r : r + n] for w, nd in begin])
                    a1[a, x, r : r + n] = start + p0 + changes[a]
                    rest[a, x, r : r + n] = rest_of(lambda nd: nd.main[a, x, r : r + n], p0, p2)
            for c in range(3):
                p0, p2 = edge0[0, c, pl.ds(i, 1)], edge2[0, c, pl.ds(i, 1)]
                rest_b[c, row] = rest_of(lambda nd: nd.behind[nd.off + c, row], p0, p2)
                p0, p2 = edge0[1, c, pl.ds(i, 1)], edge2[1, c, pl.ds(i, 1)]
                rest_a[c, row] = rest_of(lambda nd: nd.ahead[nd.off + c, row], p0, p2)

    emit_faces(a1, (a1_x, a1_l, a1_f))


def finish_kernel(
    first, v, grads, a1, a1_x, a1_b, a1_a, rest, rest_x, rest_b, rest_a,
    a2, a2_x, a2_l, a2_f, end, ext, summed, rows,
):
    fill(
        ext,
        [
            (TIME_STEP * 0.5, Node(a1, a1_x, a1_b, a1_a)),
            (TIME_STEP, Node(rest, rest_x, rest_b, rest_a)),
        ],
    )
    width, length = a1.shape[1:3]
    n = min(CHUNK, length)

    @pl.loop(0, width // 2)
    def _(i):
        for r in range(0, length, n):
            pair = []
            for q in range(2):
                x = 2 * i + q
                changes = fine_rates(ext, v, grads, x, r, n)
                pair.append([a1[a, x, r : r + n] + changes[a] for a in range(3)])
                for a in range(3):
                    a2[a, x, r : r + n] = pair[q][a]
            for a in range(3):
                summed[a, i, r : r + n] = pair[0][a] + pair[1][a]

    emit_faces(a2, (a2_x, a2_l, a2_f))

    def store(c, value):
        end[c] = value

    squeeze(summed, rows, store, 3)


def call(kernel, name, first, args, outs, scratch, flops=0, least=0, streamed=False):
    moved = sum(4 * a.size for a in args)
    room = moved + sum(4 * math.prod(dims) for dims in outs + scratch)
    values = pl.BlockSpec(memory_space=pltpu.VMEM)
    buffers = [pltpu.VMEM(dims, F32) for dims in scratch]
    if streamed:
        buffers += [pltpu.VMEM(dims, F32) for dims in outs] + [pltpu.SemaphoreType.DMA]
    return pl.pallas_call(
        kernel,
        name=name,
        out_shape=[jax.ShapeDtypeStruct(dims, F32) for dims in outs],
        in_specs=[pl.BlockSpec(memory_space=pltpu.SMEM)] * (first is not None) + [values] * len(args),
        out_specs=[pl.BlockSpec(memory_space=pl.ANY) if streamed else values] * len(outs),
        scratch_shapes=buffers,
        compiler_params=pltpu.CompilerParams(vmem_limit_bytes=min(max(room + ROOM, least), 56 << 20)),
        cost_estimate=pl.CostEstimate(flops=flops, bytes_accessed=moved, transcendentals=0),
    )(*([] if first is None else [first]), *args)


def shards(velocity, start_field, guess):
    own = guess[0]
    _, nx, ny, nz = own.shape
    cx, cy, cz = nx // 2, ny // 2, nz // 2
    slabs = lax.axis_size("tm")
    number = lax.axis_index("tm")
    first = jnp.stack([number == 0, number]).astype(F32)

    def layers_of(count):
        return [(count, 2, ny, nz), (count, nx, nz), (count, nx, nz)]

    fine, coarse = (3, nx, ny, nz), (3, cx, cy, cz)
    fine_faces, coarse_faces = layers_of(3), [(3, 2, cy, cz), (3, cx, cz), (3, cx, cz)]
    ext = (3, nx + 2, ny + 2 * PAD, nz)
    coarse_ext = (3, cx + 2, cy + 2 * PAD, cz)
    summed, rows = (3, cx, ny, nz), (cx * ny, cz)
    wide, edge, wide_rows = (3, cx + 2, ny, nz), (2, 3, cx, nz), ((cx + 2) * ny, cz)

    end_two, *packed = call(
        pack_kernel, "pack", None, [velocity, start_field, own],
        [coarse] + layers_of(7), [summed, rows], 5_000_000, 56 << 20,
    )
    layers = swap_faces(packed)
    speed, zero = call(
        coarsen_kernel, "coarsen", first, [velocity, start_field, end_two],
        [coarse, coarse], [summed, rows], 10_000_000,
    )
    grads, integral, coarse_grads, *results = call(
        offset_start_kernel, "offset_start", first, [velocity, start_field, own, *layers, zero],
        [(9, nx, ny, nz), coarse, (9, cx, cy, cz)] + coarse_faces + [coarse] + coarse_faces,
        [ext, ext, summed, (9, cx, ny, nz), rows], 40_000_000,
    )
    zero_faces, sent = results[:3], results[3:]

    def chain(step, sent, outs, scratch, own_terms):
        arrivals = []
        for turn in range(1, slabs):
            arrivals += hand_on([turn - 1], sent[0], sent[1:])
            if turn + 1 < slabs:
                sent = call(
                    lambda *refs, turn=turn: step(turn, *refs), "chain", first,
                    [*arrivals[-4:], *own_terms, speed, coarse_grads],
                    [outs] + coarse_faces, scratch + [coarse_ext], 2_000_000,
                )
        return arrivals

    terms = [zero, *zero_faces, integral]
    arrivals = chain(pass_start_kernel, sent, coarse, [coarse] + coarse_faces, terms)
    results = call(
        lambda *refs: settle_start_kernel(slabs - 1, *refs), "settle", first,
        [*arrivals, *terms, speed, coarse_grads, end_two, start_field],
        [coarse] + coarse_faces + [coarse] + layers_of(4), [coarse_ext], 2_000_000,
    )
    start_layers = swap_faces(results[5:])
    middle, m_x, m_l, m_f, *rest = call(
        middle_kernel, "middle", first,
        [velocity, grads, start_field, own, *layers, *results[:5], *start_layers],
        [fine] + fine_faces + [fine] + fine_faces,
        [ext, wide, edge, wide, edge, wide_rows] + coarse_faces + fine_faces, 60_000_000,
    )
    u1 = [middle, *swap_faces((m_x, m_l, m_f))]
    value, *results = call(
        finish_kernel, "finish", first, [velocity, grads, *u1, *rest],
        [fine] + fine_faces + [coarse], [ext, summed, rows], 40_000_000,
    )
    faces, end_two = results[:3], results[3]
    u0 = pass_on(range(slabs - 1), value)
    u2 = [value, *swap_faces(faces)]

    own_part, following, *sent = call(
        offset_later_kernel, "offset_later", first,
        [velocity, grads, start_field, *start_layers, *u1, *u2, zero, end_two],
        [coarse, coarse, (6, cx, cy, cz)] + coarse_faces,
        [ext, ext, summed, summed, rows], 60_000_000,
    )
    arrivals = chain(pass_later_kernel, sent, (6, cx, cy, cz), [], [own_part, following])
    stage, *faces, begin, rest = call(
        lambda *refs: settle_later_kernel(slabs - 1, *refs), "settle", first,
        [*arrivals, own_part, speed, coarse_grads, start_field, u0, middle, value],
        [fine] + fine_faces + [fine, fine],
        [coarse, *coarse_faces, coarse, coarse_ext, summed, summed, rows], 10_000_000,
    )
    middle, stage, *faces = call(
        first_stage_kernel, "stage", first, [velocity, grads, stage, *swap_faces(faces), begin, rest],
        [fine, fine] + fine_faces, [ext], 40_000_000,
    )
    result, = call(
        last_stage_kernel, "last_stage", None, [velocity, grads, stage, *swap_faces(faces), middle],
        [fine], [ext], 40_000_000, streamed=True,
    )
    return result[None]


def solution(mesh):
    in_specs = (
        P(None, "gx", "gy", None),
        P(None, "gx", "gy", None),
        P("tm", None, "gx", "gy", None),
    )
    out_specs = P("tm", None, "gx", "gy", None)
    return jax.shard_map(shards, mesh=mesh, in_specs=in_specs, out_specs=out_specs, check_vma=False)
```

```python
import math

import jax
import jax.numpy as jnp
from jax import lax
from jax.experimental import pallas as pl
from jax.experimental.pallas import tpu as pltpu
from jax.sharding import PartitionSpec as P

VISCOSITY = 0.25
TIME_STEP = 0.5
PAD = 8
CHUNK = 8
ROOM = 4 << 20
F32 = jnp.float32
BF16 = jnp.bfloat16


def ring(size, by):
    return [(i, (i + by) % size) for i in range(size)]


def both_faces(faces, permute, size):
    if size == 2:
        return permute(faces, 1)
    before = permute(faces[:, 0:1], 1)
    after = permute(faces[:, 1:2], -1)
    return jnp.concatenate([before, after], axis=1)


def swap_faces(faces):
    x_faces, y_last, y_first = faces
    gx, gy = lax.axis_size("gx"), lax.axis_size("gy")
    before_after = both_faces(x_faces, lambda a, by: lax.ppermute(a, "gx", ring(gx, by)), gx)
    behind = lax.ppermute(y_last, "gy", ring(gy, 1))
    ahead = lax.ppermute(y_first, "gy", ring(gy, -1))
    return before_after, behind, ahead


def pass_on(slabs, array, dx=0, dy=0, dt=1):
    gx, gy = lax.axis_size("gx"), lax.axis_size("gy")
    pairs = []
    for t in slabs:
        for x in range(gx):
            for y in range(gy):
                source = (t * gx + x) * gy + y
                target = ((t + dt) * gx + (x + dx) % gx) * gy + (y + dy) % gy
                pairs.append((source, target))
    return lax.ppermute(array, ("tm", "gx", "gy"), pairs)


def swap_within(slabs, faces):
    x_faces, y_last, y_first = faces
    before_after = both_faces(x_faces, lambda a, by: pass_on(slabs, a, by, 0, 0), lax.axis_size("gx"))
    return before_after, pass_on(slabs, y_last, 0, 1, 0), pass_on(slabs, y_first, 0, -1, 0)


def hand_on(slabs, value, faces):
    x_faces, y_last, y_first = faces
    main = pass_on(slabs, value)
    behind = pass_on(slabs, y_last, 0, 1)
    ahead = pass_on(slabs, y_first, 0, -1)
    before_after = both_faces(x_faces, lambda a, by: pass_on(slabs, a, by, 0), lax.axis_size("gx"))
    return [main, behind, ahead, before_after]


class Node:
    def __init__(self, main, x_faces, behind, ahead, off=0):
        self.main, self.x_faces, self.behind, self.ahead, self.off = main, x_faces, behind, ahead, off


class Mix:
    def __init__(self, *parts):
        self.parts, self.shape = parts, parts[0][1].shape

    def __getitem__(self, key):
        return total([w * field[key] for w, field in self.parts])


def scaled(weight, value):
    return value if isinstance(weight, float) and weight == 1.0 else weight * value


def total(terms):
    result = terms[0]
    for term in terms[1:]:
        result = result + term
    return result


def each(count, unrolled=False):
    def wrap(body):
        if unrolled:
            for i in range(count):
                body(i)
        else:
            pl.loop(0, count)(body)

    return wrap


def fill(ext, parts, spread=(), unrolled=False):
    width, length = ext.shape[1] - 2, ext.shape[2] - 2 * PAD
    inner = slice(PAD, PAD + length)
    for c in range(3):
        for k, at in ((0, 0), (1, width + 1)):
            terms = [scaled(w, n.x_faces[n.off + c, k]) for w, n in parts]
            terms += [w * p[c, k * (width // 2 + 1)] for w, p, _ in spread]
            ext[c, at, inner] = total(terms)

    @each(width // 2, unrolled)
    def _(i):
        for q in range(2):
            x = 2 * i + q
            for c in range(3):
                terms = [scaled(w, n.main[c, x]) for w, n in parts]
                terms += [w * p[c, i + 1] for w, p, _ in spread]
                ext[c, x + 1, inner] = total(terms)
                row = pl.ds(x, 1)
                for k, at in ((0, PAD - 1), (1, PAD + length)):
                    terms = [scaled(w, (n.ahead if k else n.behind)[n.off + c, row]) for w, n in parts]
                    terms += [w * e[k, c, pl.ds(i, 1)] for w, _, e in spread]
                    ext[c, x + 1, at : at + 1] = total(terms)


def turned(value, by):
    return pltpu.roll(value, by % value.shape[-1], value.ndim - 1)


def sides(ext, c, x, r, n):
    here = ext[c, x, r : r + n]
    return (
        here,
        (ext[c, x + 1, r : r + n], ext[c, x, r + 1 : r + 1 + n], turned(here, -1)),
        (ext[c, x - 1, r : r + n], ext[c, x, r - 1 : r - 1 + n], turned(here, 1)),
    )


def rates(ext, x, r, n, speeds, grads_of, strength):
    here = [ext[b, x, r : r + n] for b in range(3)]
    toward = [strength - speed for speed in speeds]
    away = [strength + speed for speed in speeds]
    outputs = []
    for a in range(3):
        _, ahead, behind = sides(ext, a, x, r, n)
        grads = grads_of(a)
        result = here[a] * (grads[a] - 6.0 * strength)
        for b in range(3):
            if b != a:
                result = result + here[b] * grads[b]
            result = result + toward[b] * ahead[b] + away[b] * behind[b]
        outputs.append(result)
    return outputs


def slopes(half, a, x, r, n):
    _, ahead, behind = sides(half, a, x, r, n)
    return [ahead[b] - behind[b] for b in range(3)]


def fine_rates(ext, v, grads, x, r, n):
    speeds = [0.5 * v[b, x, r : r + n] for b in range(3)]

    def grads_of(a):
        return [grads[3 * a + b, x, r : r + n] for b in range(3)]

    return rates(ext, x + 1, PAD + r, n, speeds, grads_of, VISCOSITY)


def split(value):
    high = value.astype(BF16)
    low = (value - high.astype(F32)).astype(BF16)
    return high, low


def pair_table(rows, columns, by_row, entry):
    i = lax.broadcasted_iota(jnp.int32, (rows, columns), 0)
    j = lax.broadcasted_iota(jnp.int32, (rows, columns), 1)
    same = (i >> 1) == j if by_row else i == (j >> 1)
    return jnp.where(same, entry, 0.0).astype(BF16)


def squeeze(summed, rows, store, count):
    cx, y, z = summed.shape[1:]
    table = pair_table(z, z // 2, True, 0.125)
    for c in range(count):
        high, low = split(summed[c].reshape(cx * y, z))
        rows[...] = jnp.dot(high, table, preferred_element_type=F32) + jnp.dot(
            low, table, preferred_element_type=F32
        )
        half = cx * y // 2
        value = rows[pl.ds(0, half, stride=2)] + rows[pl.ds(1, half, stride=2)]
        store(c, value.reshape(cx, y // 2, z // 2))


def spread_along(value):
    cz = value.shape[1]
    single = pair_table(cz, 2 * cz, False, 1.0)
    table = jnp.concatenate([single, single], axis=0)
    high, low = split(value)
    return jnp.dot(jnp.concatenate([high, low], axis=1), table, preferred_element_type=F32)


def doubled(value, rows):
    count = value.shape[0]
    rows[pl.ds(0, count, stride=2)] = value
    rows[pl.ds(1, count, stride=2)] = value
    return rows[...]


def prolong_own(main, wide, rows):
    cx, cy, cz = main.shape[1:]
    for c in range(3):
        value = doubled(main[c].reshape(cx * cy, cz), rows)
        wide[c] = spread_along(value).reshape(cx, 2 * cy, 2 * cz)


def prolong(field, wide, edge, rows):
    cx, cy, cz = field.main.shape[1:]
    edges = []
    for c in range(3):
        layers = [field.x_faces[c, 0:1], field.main[c], field.x_faces[c, 1:2]]
        value = doubled(jnp.concatenate(layers, axis=0).reshape((cx + 2) * cy, cz), rows)
        wide[c] = spread_along(value).reshape(cx + 2, 2 * cy, 2 * cz)
        edges += [field.behind[c], field.ahead[c]]
    value = spread_along(jnp.concatenate(edges, axis=0))
    for c in range(3):
        for k in range(2):
            at = (2 * c + k) * cx
            edge[k, c] = value[at : at + cx]


def emit_faces(main, outs, off=0):
    x_faces, y_last, y_first = outs
    width, length = main.shape[1:3]
    for c in range(3):
        x_faces[off + c, 0] = main[c, width - 1]
        x_faces[off + c, 1] = main[c, 0]
        for x in range(width):
            y_last[off + c, x : x + 1] = main[c, x, length - 1 : length]
            y_first[off + c, x : x + 1] = main[c, x, 0:1]


def quadrant(c, rows, columns):
    up, along = c // 2, c % 2
    return slice(up * rows, (up + 1) * rows), slice(along * columns, (along + 1) * columns)


def emit_coarse_faces(main, outs, comp):
    x_faces, y_last, y_first = outs
    cx, cy, cz = main.shape[1:]
    for c in range(3):
        x_faces[(comp, 0) + quadrant(c, cy, cz)] = main[c, cx - 1]
        x_faces[(comp, 1) + quadrant(c, cy, cz)] = main[c, 0]
        rows, columns = quadrant(c, cx, cz)
        for i in range(cx):
            at = slice(rows.start + i, rows.start + i + 1)
            y_last[comp, at, columns] = main[c, i, cy - 1 : cy]
            y_first[comp, at, columns] = main[c, i, 0:1]


def take_coarse_faces(x_faces, behind, ahead, comp, outs):
    out_x, out_b, out_a = outs
    cy, cz = out_x.shape[2:]
    cx = out_b.shape[1]
    for c in range(3):
        for k in range(2):
            out_x[c, k] = x_faces[(comp, k) + quadrant(c, cy, cz)]
        out_b[c] = behind[(comp,) + quadrant(c, cx, cz)]
        out_a[c] = ahead[(comp,) + quadrant(c, cx, cz)]


def coarsen(field, summed, rows, store):
    @pl.loop(0, field.shape[1] // 2)
    def _(i):
        for c in range(3):
            summed[c, i] = field[c, 2 * i] + field[c, 2 * i + 1]

    squeeze(summed, rows, store, 3)


def offset_mix(f, s, g):
    return Mix((f / 6.0, s), (1.0 - f / 6.0, g))


def pack_kernel(v, s, g, end, x_faces, y_last, y_first, summed, rows):
    outs = (x_faces, y_last, y_first)
    emit_faces(v, outs, 0)
    f = jnp.where(lax.axis_index("tm") == 0, 1.0, 0.0)
    emit_faces(offset_mix(f, s, g), outs, 3)

    def store(c, value):
        end[c] = value

    coarsen(g, summed, rows, store)
    emit_coarse_faces(end, outs, 6)


def coarsen_kernel(first, v, s, end, speed, zero, summed, rows):
    f = first[0]

    def store_zero(c, value):
        zero[c] = f * value + (1.0 - f) * end[c]

    def store_speed(c, value):
        speed[c] = value * 0.25

    coarsen(s, summed, rows, store_zero)
    coarsen(v, summed, rows, store_speed)


def offset_start_kernel(
    first, v, s, g, x_faces, behind, ahead, zero,
    grads, integral, coarse_grads, zero_x, zero_b, zero_a, end, end_x, end_l, end_f,
    ext, half, summed, grads_summed, rows,
):
    f = first[0]
    fill(half, [(0.5, Node(v, x_faces, behind, ahead))])
    fill(ext, [(TIME_STEP, Node(offset_mix(f, s, g), x_faces, behind, ahead, 3))])
    width, length = v.shape[1:3]
    n = min(CHUNK, length)

    @pl.loop(0, width // 2)
    def _(i):
        for r in range(0, length, n):
            at = slice(r, r + n)
            for q in range(2):
                x = 2 * i + q
                for a in range(3):
                    row = slopes(half, a, x + 1, PAD + r, n)
                    for b in range(3):
                        grads[3 * a + b, x, at] = row[b]
                        if q:
                            row[b] = row[b] + grads_summed[3 * a + b, i, at]
                        grads_summed[3 * a + b, i, at] = row[b]
            pair = [fine_rates(ext, v, grads, 2 * i + q, r, n) for q in range(2)]
            for a in range(3):
                summed[a, i, at] = pair[0][a] + pair[1][a]

    def store(c, value):
        integral[c] = value
        end[c] = zero[c] + value

    squeeze(summed, rows, store, 3)
    emit_faces(end, (end_x, end_l, end_f))
    take_coarse_faces(x_faces, behind, ahead, 6, (zero_x, zero_b, zero_a))

    def store_grads(c, value):
        coarse_grads[c] = value

    squeeze(grads_summed, rows, store_grads, 9)


def offset_later_kernel(
    first, v, grads, s, x_faces, behind, ahead,
    u1, u1_x, u1_b, u1_a, u2, u2_x, u2_b, u2_a, zero, end_two,
    own, following, sent, sent_x, sent_l, sent_f,
    ext, ext_two, summed, summed_two, rows,
):
    f = first[0]
    sixth = TIME_STEP / 6.0
    last = Node(u2, u2_x, u2_b, u2_a)
    fill(ext_two, [(sixth, last)])
    fill(
        ext,
        [
            (f * sixth, Node(s, x_faces, behind, ahead)),
            (TIME_STEP * 2.0 / 3.0, Node(u1, u1_x, u1_b, u1_a)),
            (sixth, last),
        ],
    )
    width, length = v.shape[1:3]
    n = min(CHUNK, length)

    @pl.loop(0, width // 2)
    def _(i):
        for r in range(0, length, n):
            at = slice(r, r + n)
            pair = [fine_rates(ext, v, grads, 2 * i + q, r, n) for q in range(2)]
            for a in range(3):
                summed[a, i, at] = pair[0][a] + pair[1][a]
            pair = [fine_rates(ext_two, v, grads, 2 * i + q, r, n) for q in range(2)]
            for a in range(3):
                summed_two[a, i, at] = (pair[0][a] + u2[a, 2 * i, at]) + (pair[1][a] + u2[a, 2 * i + 1, at])

    def store(c, value):
        own[c] = value + (f * zero[c] - end_two[c])
        sent[c] = own[c]

    squeeze(summed, rows, store, 3)
    emit_faces(own, (sent_x, sent_l, sent_f))

    def store_following(c, value):
        following[c] = value
        sent[3 + c] = value

    squeeze(summed_two, rows, store_following, 3)


def offset_early_kernel(count, first, *refs):
    @pl.when(first[1] < float(count))
    def _():
        offset_later_kernel(first, *refs)


def offset_late_kernel(count, first, *refs):
    args, early, outs, scratch = refs[:16], refs[16:22], refs[22:28], refs[28:]

    @pl.when(first[1] >= float(count))
    def _():
        offset_later_kernel(first, *args, *outs, *scratch)

    @pl.when(first[1] < float(count))
    def _():
        for out, made in zip(outs, early):
            out[...] = made[...]


def chain_step(base, speed, coarse_grads, d0, ext, store):
    fill(ext, [(TIME_STEP, Node(*d0))], unrolled=True)
    width, length = speed.shape[1:3]
    for x in range(width):
        speeds = [speed[b, x] for b in range(3)]

        def grads_of(a):
            return [coarse_grads[3 * a + b, x] for b in range(3)]

        changes = rates(ext, x + 1, PAD, length, speeds, grads_of, VISCOSITY / 4.0)
        for a in range(3):
            store(a, x, base(a, x) + d0[0][a, x] + changes[a])


def arrival(refs):
    main, behind, ahead, x_faces = refs
    return main, x_faces, behind, ahead


def pass_start_kernel(turn, first, *refs):
    arrived, zero = arrival(refs[:4]), refs[4:8]
    integral, speed, coarse_grads, end, end_x, end_l, end_f = refs[8:15]
    d0, ext = refs[15:19], refs[19]

    @pl.when(first[1] == float(turn))
    def _():
        def base(a, x):
            return zero[0][a, x] + integral[a, x]

        def store(a, x, value):
            end[a, x] = value

        for k in range(4):
            d0[k][...] = arrived[k][...] - zero[k][...]
        chain_step(base, speed, coarse_grads, d0, ext, store)
        emit_faces(end, (end_x, end_l, end_f))


def settle_start_kernel(count, first, *refs):
    arrived = [arrival(refs[4 * k : 4 * k + 4]) for k in range(count)]
    refs = refs[4 * count :]
    zero, (integral, speed, coarse_grads, end_two, s) = refs[:4], refs[4:9]
    d0, d2, outs, ext = refs[9:13], refs[13], refs[14:17], refs[17]
    rest = 1.0 - first[0]

    def base(a, x):
        return zero[0][a, x] + integral[a, x] - end_two[a, x]

    def store(a, x, value):
        d2[a, x] = value

    for k in range(4):
        d0[k][...] = rest * (total([group[k][...] for group in arrived]) - zero[k][...])
    chain_step(base, speed, coarse_grads, d0, ext, store)
    emit_faces(s, outs, 0)
    emit_coarse_faces(d2, outs, 3)


def pass_later_kernel(turn, first, *refs):
    arrived, (own, following, speed, coarse_grads) = arrival(refs[:4]), refs[4:8]
    sent, sent_x, sent_l, sent_f, ext = refs[8:13]

    @pl.when(first[1] == float(turn))
    def _():
        def base(a, x):
            return own[a, x] + arrived[0][3 + a, x]

        def store(a, x, value):
            sent[a, x] = value
            sent[3 + a, x] = following[a, x]

        chain_step(base, speed, coarse_grads, arrived, ext, store)
        emit_faces(sent, (sent_x, sent_l, sent_f))


def settle_later_kernel(count, first, *refs):
    arrived = [arrival(refs[4 * k : 4 * k + 4]) for k in range(count)]
    own, speed, coarse_grads, s, u0, u1, u2, stage, stage_x, stage_l, stage_f, begin, rest = refs[4 * count : 4 * count + 13]
    d0, (d2, ext, wide0, wide2, rows) = refs[4 * count + 13 : 4 * count + 17], refs[4 * count + 17 :]
    f = first[0]

    def base(a, x):
        return own[a, x] + total([group[0][3 + a, x] for group in arrived])

    def store(a, x, value):
        d2[a, x] = value

    d0[0][...] = total([group[0][0:3] for group in arrived])
    for k in range(1, 4):
        d0[k][...] = total([group[k][...] for group in arrived])
    chain_step(base, speed, coarse_grads, d0, ext, store)
    prolong_own(d0[0], wide0, rows)
    prolong_own(d2, wide2, rows)

    @pl.loop(0, u0.shape[1] // 2)
    def _(i):
        for c in range(3):
            p0, p2 = wide0[c, i], wide2[c, i]
            toward_stage = TIME_STEP * (0.375 * p0 + 0.125 * p2)
            toward_rest = 0.125 * (p2 - p0)
            for q in range(2):
                x = 2 * i + q
                start, one, two = f * s[c, x] + u0[c, x], u1[c, x], u2[c, x]
                stage[c, x] = toward_stage + TIME_STEP * (start * (5.0 / 24.0) + one / 3.0 - two / 24.0)
                begin[c, x] = start + p0
                rest[c, x] = toward_rest + (two * (5.0 / 24.0) - one / 6.0 - start / 24.0)

    emit_faces(stage, (stage_x, stage_l, stage_f))


def first_stage_kernel(first, v, grads, y, y_x, y_b, y_a, begin, rest, out, stage, stage_x, stage_l, stage_f, ext):
    fill(ext, [(1.0, Node(y, y_x, y_b, y_a))])
    width, length = v.shape[1:3]
    n = min(CHUNK, length)

    @pl.loop(0, width)
    def _(x):
        for r in range(0, length, n):
            at = slice(r, r + n)
            changes = fine_rates(ext, v, grads, x, r, n)
            for a in range(3):
                value = begin[a, x, at] + changes[a]
                out[a, x, at] = value
                stage[a, x, at] = TIME_STEP * (0.5 * value + rest[a, x, at])

    emit_faces(stage, (stage_x, stage_l, stage_f))


def last_stage_kernel(v, grads, y, y_x, y_b, y_a, begin, out, ext, made, sent):
    fill(ext, [(1.0, Node(y, y_x, y_b, y_a))])
    width, length = v.shape[1:3]
    n = min(CHUNK, length)

    @pl.loop(0, width)
    def _(x):
        for r in range(0, length, n):
            changes = fine_rates(ext, v, grads, x, r, n)
            for a in range(3):
                made[a, x, r : r + n] = begin[a, x, r : r + n] + changes[a]
        plane = pl.ds(x, 1)
        pltpu.make_async_copy(made.at[:, plane], out.at[:, plane], sent).start()

    pltpu.make_async_copy(made, out, sent).wait()


def middle_kernel(
    first, v, grads, s, g, w_x, w_b, w_a, d0, d0_x, d0_b, d0_a, d2, m_x, m_b, m_a,
    a1, a1_x, a1_l, a1_f, rest, rest_x, rest_b, rest_a,
    ext, wide0, edge0, wide2, edge2, rows, d2_x, d2_b, d2_a, g_x, g_b, g_a,
):
    f = first[0]
    take_coarse_faces(m_x, m_b, m_a, 3, (d2_x, d2_b, d2_a))
    for out, mixed, start, off in ((g_x, w_x, m_x, 3), (g_b, w_b, m_b, 3), (g_a, w_a, m_a, 3)):
        for c in range(3):
            out[c] = (1.0 + 0.2 * f) * mixed[off + c] - (0.2 * f) * start[c]
    parts = [Node(s, m_x, m_b, m_a), Node(g, g_x, g_b, g_a)]
    begin = list(zip((f, 1.0 - f), parts))
    first_stage = list(zip((5.0 / 24.0 * f, 0.5 - 5.0 / 24.0 * f), parts))
    second_stage = list(zip((f / -24.0, f / 24.0), parts))
    prolong(Node(d0, d0_x, d0_b, d0_a), wide0, edge0, rows)
    prolong(Node(d2, d2_x, d2_b, d2_a), wide2, edge2, rows)
    fill(
        ext,
        [(TIME_STEP * w, node) for w, node in first_stage],
        [(TIME_STEP * 0.375, wide0, edge0), (TIME_STEP * 0.125, wide2, edge2)],
    )
    width, length = a1.shape[1:3]
    n = min(CHUNK, length)
    last_cx = width // 2 + 1

    def rest_of(get, p0, p2):
        return total([w * get(node) for w, node in second_stage]) + 0.125 * (p2 - p0)

    for c in range(3):
        for k in range(2):
            rest_x[c, k] = rest_of(
                lambda nd: nd.x_faces[nd.off + c, k], wide0[c, k * last_cx], wide2[c, k * last_cx]
            )

    @pl.loop(0, width // 2)
    def _(i):
        for q in range(2):
            x = 2 * i + q
            row = pl.ds(x, 1)
            for r in range(0, length, n):
                changes = fine_rates(ext, v, grads, x, r, n)
                for a in range(3):
                    p0, p2 = wide0[a, i + 1, r : r + n], wide2[a, i + 1, r : r + n]
                    start = total([w * nd.main[a, x, r : r + n] for w, nd in begin])
                    a1[a, x, r : r + n] = start + p0 + changes[a]
                    rest[a, x, r : r + n] = rest_of(lambda nd: nd.main[a, x, r : r + n], p0, p2)
            for c in range(3):
                p0, p2 = edge0[0, c, pl.ds(i, 1)], edge2[0, c, pl.ds(i, 1)]
                rest_b[c, row] = rest_of(lambda nd: nd.behind[nd.off + c, row], p0, p2)
                p0, p2 = edge0[1, c, pl.ds(i, 1)], edge2[1, c, pl.ds(i, 1)]
                rest_a[c, row] = rest_of(lambda nd: nd.ahead[nd.off + c, row], p0, p2)

    emit_faces(a1, (a1_x, a1_l, a1_f))


def finish_kernel(
    first, v, grads, a1, a1_x, a1_b, a1_a, rest, rest_x, rest_b, rest_a,
    a2, a2_x, a2_l, a2_f, end, ext, summed, rows,
):
    fill(
        ext,
        [
            (TIME_STEP * 0.5, Node(a1, a1_x, a1_b, a1_a)),
            (TIME_STEP, Node(rest, rest_x, rest_b, rest_a)),
        ],
    )
    width, length = a1.shape[1:3]
    n = min(CHUNK, length)

    @pl.loop(0, width // 2)
    def _(i):
        for r in range(0, length, n):
            pair = []
            for q in range(2):
                x = 2 * i + q
                changes = fine_rates(ext, v, grads, x, r, n)
                pair.append([a1[a, x, r : r + n] + changes[a] for a in range(3)])
                for a in range(3):
                    a2[a, x, r : r + n] = pair[q][a]
            for a in range(3):
                summed[a, i, r : r + n] = pair[0][a] + pair[1][a]

    emit_faces(a2, (a2_x, a2_l, a2_f))

    def store(c, value):
        end[c] = value

    squeeze(summed, rows, store, 3)


def call(kernel, name, first, args, outs, scratch, flops=0, least=0, streamed=False):
    moved = sum(4 * a.size for a in args)
    room = moved + sum(4 * math.prod(dims) for dims in outs + scratch)
    values = pl.BlockSpec(memory_space=pltpu.VMEM)
    buffers = [pltpu.VMEM(dims, F32) for dims in scratch]
    if streamed:
        buffers += [pltpu.VMEM(dims, F32) for dims in outs] + [pltpu.SemaphoreType.DMA]
    return pl.pallas_call(
        kernel,
        name=name,
        out_shape=[jax.ShapeDtypeStruct(dims, F32) for dims in outs],
        in_specs=[pl.BlockSpec(memory_space=pltpu.SMEM)] * (first is not None) + [values] * len(args),
        out_specs=[pl.BlockSpec(memory_space=pl.ANY) if streamed else values] * len(outs),
        scratch_shapes=buffers,
        compiler_params=pltpu.CompilerParams(vmem_limit_bytes=min(max(room + ROOM, least), 56 << 20)),
        cost_estimate=pl.CostEstimate(flops=flops, bytes_accessed=moved, transcendentals=0),
    )(*([] if first is None else [first]), *args)


def shards(velocity, start_field, guess):
    own = guess[0]
    _, nx, ny, nz = own.shape
    cx, cy, cz = nx // 2, ny // 2, nz // 2
    slabs = lax.axis_size("tm")
    number = lax.axis_index("tm")
    first = jnp.stack([number == 0, number]).astype(F32)

    def layers_of(count):
        return [(count, 2, ny, nz), (count, nx, nz), (count, nx, nz)]

    fine, coarse = (3, nx, ny, nz), (3, cx, cy, cz)
    fine_faces, coarse_faces = layers_of(3), [(3, 2, cy, cz), (3, cx, cz), (3, cx, cz)]
    ext = (3, nx + 2, ny + 2 * PAD, nz)
    coarse_ext = (3, cx + 2, cy + 2 * PAD, cz)
    summed, rows = (3, cx, ny, nz), (cx * ny, cz)
    wide, edge, wide_rows = (3, cx + 2, ny, nz), (2, 3, cx, nz), ((cx + 2) * ny, cz)

    end_two, *packed = call(
        pack_kernel, "pack", None, [velocity, start_field, own],
        [coarse] + layers_of(7), [summed, rows], 5_000_000, 56 << 20,
    )
    layers = swap_faces(packed)
    speed, zero = call(
        coarsen_kernel, "coarsen", first, [velocity, start_field, end_two],
        [coarse, coarse], [summed, rows], 10_000_000,
    )
    grads, integral, coarse_grads, *results = call(
        offset_start_kernel, "offset_start", first, [velocity, start_field, own, *layers, zero],
        [(9, nx, ny, nz), coarse, (9, cx, cy, cz)] + coarse_faces + [coarse] + coarse_faces,
        [ext, ext, summed, (9, cx, ny, nz), rows], 40_000_000,
    )
    zero_faces, sent = results[:3], results[3:]

    def chain(step, sent, outs, scratch, own_terms):
        arrivals = []
        for turn in range(1, slabs):
            arrivals += hand_on([turn - 1], sent[0], sent[1:])
            if turn + 1 < slabs:
                sent = call(
                    lambda *refs, turn=turn: step(turn, *refs), "chain", first,
                    [*arrivals[-4:], *own_terms, speed, coarse_grads],
                    [outs] + coarse_faces, scratch + [coarse_ext], 2_000_000,
                )
        return arrivals

    terms = [zero, *zero_faces, integral]
    arrivals = chain(pass_start_kernel, sent, coarse, [coarse] + coarse_faces, terms)
    results = call(
        lambda *refs: settle_start_kernel(slabs - 1, *refs), "settle", first,
        [*arrivals, *terms, speed, coarse_grads, end_two, start_field],
        [coarse] + coarse_faces + [coarse] + layers_of(4), [coarse_ext], 2_000_000,
    )
    start_layers = swap_faces(results[5:])
    middle, m_x, m_l, m_f, *rest = call(
        middle_kernel, "middle", first,
        [velocity, grads, start_field, own, *layers, *results[:5], *start_layers],
        [fine] + fine_faces + [fine] + fine_faces,
        [ext, wide, edge, wide, edge, wide_rows] + coarse_faces + fine_faces, 60_000_000,
    )
    u1 = [middle, *swap_faces((m_x, m_l, m_f))]
    value, *results = call(
        finish_kernel, "finish", first, [velocity, grads, *u1, *rest],
        [fine] + fine_faces + [coarse], [ext, summed, rows], 40_000_000,
    )
    faces, end_two = results[:3], results[3]
    half = (slabs + 1) // 2
    shared = [velocity, grads, start_field, *start_layers, *u1]
    outs = [coarse, coarse, (6, cx, cy, cz)] + coarse_faces
    scratch = [ext, ext, summed, summed, rows]
    early = call(
        lambda *refs: offset_early_kernel(half, *refs), "offset_early", first,
        [*shared, value, *swap_within(range(half), faces), zero, end_two], outs, scratch, 60_000_000,
    )
    tied, moving, *faces = lax.optimization_barrier([early[0], value, *faces])
    early = [tied, *early[1:]]
    u0 = pass_on(range(slabs - 1), moving)
    own_part, following, *sent = call(
        lambda *refs: offset_late_kernel(half, *refs), "offset_late", first,
        [*shared, value, *swap_within(range(half, slabs), faces), zero, end_two, *early], outs, scratch, 60_000_000,
    )
    arrivals = chain(pass_later_kernel, sent, (6, cx, cy, cz), [], [own_part, following])
    stage, *faces, begin, rest = call(
        lambda *refs: settle_later_kernel(slabs - 1, *refs), "settle", first,
        [*arrivals, own_part, speed, coarse_grads, start_field, u0, middle, value],
        [fine] + fine_faces + [fine, fine],
        [coarse, *coarse_faces, coarse, coarse_ext, summed, summed, rows], 10_000_000,
    )
    middle, stage, *faces = call(
        first_stage_kernel, "stage", first, [velocity, grads, stage, *swap_faces(faces), begin, rest],
        [fine, fine] + fine_faces, [ext], 40_000_000,
    )
    result, = call(
        last_stage_kernel, "last_stage", None, [velocity, grads, stage, *swap_faces(faces), middle],
        [fine], [ext], 40_000_000, streamed=True,
    )
    return result[None]


def solution(mesh):
    in_specs = (
        P(None, "gx", "gy", None),
        P(None, "gx", "gy", None),
        P("tm", None, "gx", "gy", None),
    )
    out_specs = P("tm", None, "gx", "gy", None)
    return jax.shard_map(shards, mesh=mesh, in_specs=in_specs, out_specs=out_specs, check_vma=False)
```

```python
import math

import jax
import jax.numpy as jnp
from jax import lax
from jax.experimental import pallas as pl
from jax.experimental.pallas import tpu as pltpu
from jax.sharding import PartitionSpec as P

VISCOSITY = 0.25
TIME_STEP = 0.5
PAD = 8
CHUNK = 8
ROOM = 4 << 20
F32 = jnp.float32
BF16 = jnp.bfloat16


def ring(size, by):
    return [(i, (i + by) % size) for i in range(size)]


def both_faces(faces, permute, size):
    if size == 2:
        return permute(faces, 1)
    before = permute(faces[:, 0:1], 1)
    after = permute(faces[:, 1:2], -1)
    return jnp.concatenate([before, after], axis=1)


def swap_faces(faces):
    x_faces, y_last, y_first = faces
    gx, gy = lax.axis_size("gx"), lax.axis_size("gy")
    before_after = both_faces(x_faces, lambda a, by: lax.ppermute(a, "gx", ring(gx, by)), gx)
    behind = lax.ppermute(y_last, "gy", ring(gy, 1))
    ahead = lax.ppermute(y_first, "gy", ring(gy, -1))
    return before_after, behind, ahead


def pass_on(array, dx=0, dy=0):
    slabs, gx, gy = lax.axis_size("tm"), lax.axis_size("gx"), lax.axis_size("gy")
    pairs = []
    for t in range(slabs):
        for x in range(gx):
            for y in range(gy):
                source = (t * gx + x) * gy + y
                target = ((t + 1) % slabs * gx + (x + dx) % gx) * gy + (y + dy) % gy
                pairs.append((source, target))
    return lax.ppermute(array, ("tm", "gx", "gy"), pairs)


def hand_on(value, faces):
    x_faces, y_last, y_first = faces
    main = pass_on(value)
    behind = pass_on(y_last, 0, 1)
    ahead = pass_on(y_first, 0, -1)
    before_after = both_faces(x_faces, lambda a, by: pass_on(a, by, 0), lax.axis_size("gx"))
    return [main, behind, ahead, before_after]


class Node:
    def __init__(self, main, x_faces, behind, ahead, off=0):
        self.main, self.x_faces, self.behind, self.ahead, self.off = main, x_faces, behind, ahead, off


class Mix:
    def __init__(self, *parts):
        self.parts, self.shape = parts, parts[0][1].shape

    def __getitem__(self, key):
        return total([w * field[key] for w, field in self.parts])


def scaled(weight, value):
    return value if isinstance(weight, float) and weight == 1.0 else weight * value


def total(terms):
    result = terms[0]
    for term in terms[1:]:
        result = result + term
    return result


def each(count, unrolled=False):
    def wrap(body):
        if unrolled:
            for i in range(count):
                body(i)
        else:
            pl.loop(0, count)(body)

    return wrap


def fill(ext, parts, spread=(), unrolled=False):
    width, length = ext.shape[1] - 2, ext.shape[2] - 2 * PAD
    inner = slice(PAD, PAD + length)
    for c in range(3):
        for k, at in ((0, 0), (1, width + 1)):
            terms = [scaled(w, n.x_faces[n.off + c, k]) for w, n in parts]
            terms += [w * p[c, k * (width // 2 + 1)] for w, p, _ in spread]
            ext[c, at, inner] = total(terms)

    @each(width // 2, unrolled)
    def _(i):
        for q in range(2):
            x = 2 * i + q
            for c in range(3):
                terms = [scaled(w, n.main[c, x]) for w, n in parts]
                terms += [w * p[c, i + 1] for w, p, _ in spread]
                ext[c, x + 1, inner] = total(terms)
                row = pl.ds(x, 1)
                for k, at in ((0, PAD - 1), (1, PAD + length)):
                    terms = [scaled(w, (n.ahead if k else n.behind)[n.off + c, row]) for w, n in parts]
                    terms += [w * e[k, c, pl.ds(i, 1)] for w, _, e in spread]
                    ext[c, x + 1, at : at + 1] = total(terms)


def turned(value, by):
    return pltpu.roll(value, by % value.shape[-1], value.ndim - 1)


def sides(ext, c, x, r, n):
    here = ext[c, x, r : r + n]
    return (
        here,
        (ext[c, x + 1, r : r + n], ext[c, x, r + 1 : r + 1 + n], turned(here, -1)),
        (ext[c, x - 1, r : r + n], ext[c, x, r - 1 : r - 1 + n], turned(here, 1)),
    )


def rates(ext, x, r, n, speeds, grads_of, strength):
    here = [ext[b, x, r : r + n] for b in range(3)]
    toward = [strength - speed for speed in speeds]
    away = [strength + speed for speed in speeds]
    outputs = []
    for a in range(3):
        _, ahead, behind = sides(ext, a, x, r, n)
        grads = grads_of(a)
        result = here[a] * (grads[a] - 6.0 * strength)
        for b in range(3):
            if b != a:
                result = result + here[b] * grads[b]
            result = result + toward[b] * ahead[b] + away[b] * behind[b]
        outputs.append(result)
    return outputs


def slopes(half, a, x, r, n):
    _, ahead, behind = sides(half, a, x, r, n)
    return [ahead[b] - behind[b] for b in range(3)]


def fine_rates(ext, v, grads, x, r, n):
    speeds = [0.5 * v[b, x, r : r + n] for b in range(3)]

    def grads_of(a):
        return [grads[3 * a + b, x, r : r + n] for b in range(3)]

    return rates(ext, x + 1, PAD + r, n, speeds, grads_of, VISCOSITY)


def split(value):
    high = value.astype(BF16)
    low = (value - high.astype(F32)).astype(BF16)
    return high, low


def pair_table(rows, columns, by_row, entry):
    i = lax.broadcasted_iota(jnp.int32, (rows, columns), 0)
    j = lax.broadcasted_iota(jnp.int32, (rows, columns), 1)
    same = (i >> 1) == j if by_row else i == (j >> 1)
    return jnp.where(same, entry, 0.0).astype(BF16)


def squeeze(summed, rows, store, count):
    cx, y, z = summed.shape[1:]
    table = pair_table(z, z // 2, True, 0.125)
    for c in range(count):
        high, low = split(summed[c].reshape(cx * y, z))
        rows[...] = jnp.dot(high, table, preferred_element_type=F32) + jnp.dot(
            low, table, preferred_element_type=F32
        )
        half = cx * y // 2
        value = rows[pl.ds(0, half, stride=2)] + rows[pl.ds(1, half, stride=2)]
        store(c, value.reshape(cx, y // 2, z // 2))


def spread_along(value):
    cz = value.shape[1]
    single = pair_table(cz, 2 * cz, False, 1.0)
    table = jnp.concatenate([single, single], axis=0)
    high, low = split(value)
    return jnp.dot(jnp.concatenate([high, low], axis=1), table, preferred_element_type=F32)


def doubled(value, rows):
    count = value.shape[0]
    rows[pl.ds(0, count, stride=2)] = value
    rows[pl.ds(1, count, stride=2)] = value
    return rows[...]


def prolong_own(main, wide, rows):
    cx, cy, cz = main.shape[1:]
    for c in range(3):
        value = doubled(main[c].reshape(cx * cy, cz), rows)
        wide[c] = spread_along(value).reshape(cx, 2 * cy, 2 * cz)


def prolong(field, wide, edge, rows):
    cx, cy, cz = field.main.shape[1:]
    edges = []
    for c in range(3):
        layers = [field.x_faces[c, 0:1], field.main[c], field.x_faces[c, 1:2]]
        value = doubled(jnp.concatenate(layers, axis=0).reshape((cx + 2) * cy, cz), rows)
        wide[c] = spread_along(value).reshape(cx + 2, 2 * cy, 2 * cz)
        edges += [field.behind[c], field.ahead[c]]
    value = spread_along(jnp.concatenate(edges, axis=0))
    for c in range(3):
        for k in range(2):
            at = (2 * c + k) * cx
            edge[k, c] = value[at : at + cx]


def emit_faces(main, outs, off=0):
    x_faces, y_last, y_first = outs
    width, length = main.shape[1:3]
    for c in range(3):
        x_faces[off + c, 0] = main[c, width - 1]
        x_faces[off + c, 1] = main[c, 0]
        for x in range(width):
            y_last[off + c, x : x + 1] = main[c, x, length - 1 : length]
            y_first[off + c, x : x + 1] = main[c, x, 0:1]


def quadrant(c, rows, columns):
    up, along = c // 2, c % 2
    return slice(up * rows, (up + 1) * rows), slice(along * columns, (along + 1) * columns)


def emit_coarse_faces(main, outs, comp):
    x_faces, y_last, y_first = outs
    cx, cy, cz = main.shape[1:]
    for c in range(3):
        x_faces[(comp, 0) + quadrant(c, cy, cz)] = main[c, cx - 1]
        x_faces[(comp, 1) + quadrant(c, cy, cz)] = main[c, 0]
        rows, columns = quadrant(c, cx, cz)
        for i in range(cx):
            at = slice(rows.start + i, rows.start + i + 1)
            y_last[comp, at, columns] = main[c, i, cy - 1 : cy]
            y_first[comp, at, columns] = main[c, i, 0:1]


def take_coarse_faces(x_faces, behind, ahead, comp, outs):
    out_x, out_b, out_a = outs
    cy, cz = out_x.shape[2:]
    cx = out_b.shape[1]
    for c in range(3):
        for k in range(2):
            out_x[c, k] = x_faces[(comp, k) + quadrant(c, cy, cz)]
        out_b[c] = behind[(comp,) + quadrant(c, cx, cz)]
        out_a[c] = ahead[(comp,) + quadrant(c, cx, cz)]


def coarsen(field, summed, rows, store):
    @pl.loop(0, field.shape[1] // 2)
    def _(i):
        for c in range(3):
            summed[c, i] = field[c, 2 * i] + field[c, 2 * i + 1]

    squeeze(summed, rows, store, 3)


def offset_mix(f, s, g):
    return Mix((f / 6.0, s), (1.0 - f / 6.0, g))


def pack_kernel(v, s, g, end, x_faces, y_last, y_first, summed, rows):
    outs = (x_faces, y_last, y_first)
    emit_faces(v, outs, 0)
    f = jnp.where(lax.axis_index("tm") == 0, 1.0, 0.0)
    emit_faces(offset_mix(f, s, g), outs, 3)

    def store(c, value):
        end[c] = value

    coarsen(g, summed, rows, store)
    emit_coarse_faces(end, outs, 6)


def coarsen_kernel(first, v, s, end, speed, zero, summed, rows):
    f = first[0]

    def store_zero(c, value):
        zero[c] = f * value + (1.0 - f) * end[c]

    def store_speed(c, value):
        speed[c] = value * 0.25

    coarsen(s, summed, rows, store_zero)
    coarsen(v, summed, rows, store_speed)


def offset_start_kernel(
    first, v, s, g, x_faces, behind, ahead, zero,
    grads, integral, coarse_grads, zero_x, zero_b, zero_a, end, end_x, end_l, end_f,
    ext, half, summed, grads_summed, rows,
):
    f = first[0]
    fill(half, [(0.5, Node(v, x_faces, behind, ahead))])
    fill(ext, [(TIME_STEP, Node(offset_mix(f, s, g), x_faces, behind, ahead, 3))])
    width, length = v.shape[1:3]
    n = min(CHUNK, length)

    @pl.loop(0, width // 2)
    def _(i):
        for r in range(0, length, n):
            at = slice(r, r + n)
            for q in range(2):
                x = 2 * i + q
                for a in range(3):
                    row = slopes(half, a, x + 1, PAD + r, n)
                    for b in range(3):
                        grads[3 * a + b, x, at] = row[b]
                        if q:
                            row[b] = row[b] + grads_summed[3 * a + b, i, at]
                        grads_summed[3 * a + b, i, at] = row[b]
            pair = [fine_rates(ext, v, grads, 2 * i + q, r, n) for q in range(2)]
            for a in range(3):
                summed[a, i, at] = pair[0][a] + pair[1][a]

    def store(c, value):
        integral[c] = value
        end[c] = zero[c] + value

    squeeze(summed, rows, store, 3)
    emit_faces(end, (end_x, end_l, end_f))
    take_coarse_faces(x_faces, behind, ahead, 6, (zero_x, zero_b, zero_a))

    def store_grads(c, value):
        coarse_grads[c] = value

    squeeze(grads_summed, rows, store_grads, 9)


def offset_later_kernel(
    first, v, grads, s, x_faces, behind, ahead,
    u1, u1_x, u1_b, u1_a, u2, u2_x, u2_b, u2_a, zero, end_two,
    own, following, sent, sent_x, sent_l, sent_f,
    ext, ext_two, summed, summed_two, rows,
):
    f = first[0]
    sixth = TIME_STEP / 6.0
    last = Node(u2, u2_x, u2_b, u2_a)
    fill(ext_two, [(sixth, last)])
    fill(
        ext,
        [
            (f * sixth, Node(s, x_faces, behind, ahead)),
            (TIME_STEP * 2.0 / 3.0, Node(u1, u1_x, u1_b, u1_a)),
            (sixth, last),
        ],
    )
    width, length = v.shape[1:3]
    n = min(CHUNK, length)

    @pl.loop(0, width // 2)
    def _(i):
        for r in range(0, length, n):
            at = slice(r, r + n)
            pair = [fine_rates(ext, v, grads, 2 * i + q, r, n) for q in range(2)]
            for a in range(3):
                summed[a, i, at] = pair[0][a] + pair[1][a]
            pair = [fine_rates(ext_two, v, grads, 2 * i + q, r, n) for q in range(2)]
            for a in range(3):
                summed_two[a, i, at] = (pair[0][a] + u2[a, 2 * i, at]) + (pair[1][a] + u2[a, 2 * i + 1, at])

    def store(c, value):
        own[c] = value + (f * zero[c] - end_two[c])
        sent[c] = own[c]

    squeeze(summed, rows, store, 3)
    emit_faces(own, (sent_x, sent_l, sent_f))

    def store_following(c, value):
        following[c] = value
        sent[3 + c] = value

    squeeze(summed_two, rows, store_following, 3)


def chain_step(base, speed, coarse_grads, d0, ext, store):
    fill(ext, [(TIME_STEP, Node(*d0))], unrolled=True)
    width, length = speed.shape[1:3]
    for x in range(width):
        speeds = [speed[b, x] for b in range(3)]

        def grads_of(a):
            return [coarse_grads[3 * a + b, x] for b in range(3)]

        changes = rates(ext, x + 1, PAD, length, speeds, grads_of, VISCOSITY / 4.0)
        for a in range(3):
            store(a, x, base(a, x) + d0[0][a, x] + changes[a])


def arrival(refs):
    main, behind, ahead, x_faces = refs
    return main, x_faces, behind, ahead


def own_round(first, arrived):
    shares = [jnp.where(first[1] == float(k + 1), 1.0, 0.0) for k in range(len(arrived))]
    return lambda read: total([share * read(group) for share, group in zip(shares, arrived)])


def leave_empty(first, turn, outs):
    @pl.when(first[1] != float(turn))
    def _():
        for out in outs:
            out[...] = jnp.zeros(out.shape, F32)


def pass_start_kernel(turn, first, *refs):
    arrived, zero = arrival(refs[:4]), refs[4:8]
    integral, speed, coarse_grads, end, end_x, end_l, end_f = refs[8:15]
    d0, ext = refs[15:19], refs[19]

    @pl.when(first[1] == float(turn))
    def _():
        def base(a, x):
            return zero[0][a, x] + integral[a, x]

        def store(a, x, value):
            end[a, x] = value

        for k in range(4):
            d0[k][...] = arrived[k][...] - zero[k][...]
        chain_step(base, speed, coarse_grads, d0, ext, store)
        emit_faces(end, (end_x, end_l, end_f))

    leave_empty(first, turn, (end, end_x, end_l, end_f))


def settle_start_kernel(count, first, *refs):
    arrived = [arrival(refs[4 * k : 4 * k + 4]) for k in range(count)]
    refs = refs[4 * count :]
    zero, (integral, speed, coarse_grads, end_two, s) = refs[:4], refs[4:9]
    d0, d2, outs, ext = refs[9:13], refs[13], refs[14:17], refs[17]
    rest, own = 1.0 - first[0], own_round(first, arrived)

    def base(a, x):
        return zero[0][a, x] + integral[a, x] - end_two[a, x]

    def store(a, x, value):
        d2[a, x] = value

    for k in range(4):
        d0[k][...] = rest * (own(lambda group: group[k][...]) - zero[k][...])
    chain_step(base, speed, coarse_grads, d0, ext, store)
    emit_faces(s, outs, 0)
    emit_coarse_faces(d2, outs, 3)


def pass_later_kernel(turn, first, *refs):
    arrived, (own, following, speed, coarse_grads) = arrival(refs[:4]), refs[4:8]
    sent, sent_x, sent_l, sent_f, ext = refs[8:13]

    @pl.when(first[1] == float(turn))
    def _():
        def base(a, x):
            return own[a, x] + arrived[0][3 + a, x]

        def store(a, x, value):
            sent[a, x] = value
            sent[3 + a, x] = following[a, x]

        chain_step(base, speed, coarse_grads, arrived, ext, store)
        emit_faces(sent, (sent_x, sent_l, sent_f))

    leave_empty(first, turn, (sent, sent_x, sent_l, sent_f))


def settle_later_kernel(count, first, *refs):
    arrived = [arrival(refs[4 * k : 4 * k + 4]) for k in range(count)]
    own, speed, coarse_grads, s, u0, u1, u2, stage, stage_x, stage_l, stage_f, begin, rest = refs[4 * count : 4 * count + 13]
    d0, (d2, ext, wide0, wide2, rows) = refs[4 * count + 13 : 4 * count + 17], refs[4 * count + 17 :]
    f, picked = first[0], own_round(first, arrived)

    def base(a, x):
        return own[a, x] + picked(lambda group: group[0][3 + a, x])

    def store(a, x, value):
        d2[a, x] = value

    d0[0][...] = picked(lambda group: group[0][0:3])
    for k in range(1, 4):
        d0[k][...] = picked(lambda group: group[k][...])
    chain_step(base, speed, coarse_grads, d0, ext, store)
    prolong_own(d0[0], wide0, rows)
    prolong_own(d2, wide2, rows)

    @pl.loop(0, u0.shape[1] // 2)
    def _(i):
        for c in range(3):
            p0, p2 = wide0[c, i], wide2[c, i]
            toward_stage = TIME_STEP * (0.375 * p0 + 0.125 * p2)
            toward_rest = 0.125 * (p2 - p0)
            for q in range(2):
                x = 2 * i + q
                start, one, two = f * s[c, x] + (1.0 - f) * u0[c, x], u1[c, x], u2[c, x]
                stage[c, x] = toward_stage + TIME_STEP * (start * (5.0 / 24.0) + one / 3.0 - two / 24.0)
                begin[c, x] = start + p0
                rest[c, x] = toward_rest + (two * (5.0 / 24.0) - one / 6.0 - start / 24.0)

    emit_faces(stage, (stage_x, stage_l, stage_f))


def first_stage_kernel(first, v, grads, y, y_x, y_b, y_a, begin, rest, out, stage, stage_x, stage_l, stage_f, ext):
    fill(ext, [(1.0, Node(y, y_x, y_b, y_a))])
    width, length = v.shape[1:3]
    n = min(CHUNK, length)

    @pl.loop(0, width)
    def _(x):
        for r in range(0, length, n):
            at = slice(r, r + n)
            changes = fine_rates(ext, v, grads, x, r, n)
            for a in range(3):
                value = begin[a, x, at] + changes[a]
                out[a, x, at] = value
                stage[a, x, at] = TIME_STEP * (0.5 * value + rest[a, x, at])

    emit_faces(stage, (stage_x, stage_l, stage_f))


def last_stage_kernel(v, grads, y, y_x, y_b, y_a, begin, out, ext, made, sent):
    fill(ext, [(1.0, Node(y, y_x, y_b, y_a))])
    width, length = v.shape[1:3]
    n = min(CHUNK, length)

    @pl.loop(0, width)
    def _(x):
        for r in range(0, length, n):
            changes = fine_rates(ext, v, grads, x, r, n)
            for a in range(3):
                made[a, x, r : r + n] = begin[a, x, r : r + n] + changes[a]
        plane = pl.ds(x, 1)
        pltpu.make_async_copy(made.at[:, plane], out.at[:, plane], sent).start()

    pltpu.make_async_copy(made, out, sent).wait()


def middle_kernel(
    first, v, grads, s, g, w_x, w_b, w_a, d0, d0_x, d0_b, d0_a, d2, m_x, m_b, m_a,
    a1, a1_x, a1_l, a1_f, rest, rest_x, rest_b, rest_a,
    ext, wide0, edge0, wide2, edge2, rows, d2_x, d2_b, d2_a, g_x, g_b, g_a,
):
    f = first[0]
    take_coarse_faces(m_x, m_b, m_a, 3, (d2_x, d2_b, d2_a))
    for out, mixed, start, off in ((g_x, w_x, m_x, 3), (g_b, w_b, m_b, 3), (g_a, w_a, m_a, 3)):
        for c in range(3):
            out[c] = (1.0 + 0.2 * f) * mixed[off + c] - (0.2 * f) * start[c]
    parts = [Node(s, m_x, m_b, m_a), Node(g, g_x, g_b, g_a)]
    begin = list(zip((f, 1.0 - f), parts))
    first_stage = list(zip((5.0 / 24.0 * f, 0.5 - 5.0 / 24.0 * f), parts))
    second_stage = list(zip((f / -24.0, f / 24.0), parts))
    prolong(Node(d0, d0_x, d0_b, d0_a), wide0, edge0, rows)
    prolong(Node(d2, d2_x, d2_b, d2_a), wide2, edge2, rows)
    fill(
        ext,
        [(TIME_STEP * w, node) for w, node in first_stage],
        [(TIME_STEP * 0.375, wide0, edge0), (TIME_STEP * 0.125, wide2, edge2)],
    )
    width, length = a1.shape[1:3]
    n = min(CHUNK, length)
    last_cx = width // 2 + 1

    def rest_of(get, p0, p2):
        return total([w * get(node) for w, node in second_stage]) + 0.125 * (p2 - p0)

    for c in range(3):
        for k in range(2):
            rest_x[c, k] = rest_of(
                lambda nd: nd.x_faces[nd.off + c, k], wide0[c, k * last_cx], wide2[c, k * last_cx]
            )

    @pl.loop(0, width // 2)
    def _(i):
        for q in range(2):
            x = 2 * i + q
            row = pl.ds(x, 1)
            for r in range(0, length, n):
                changes = fine_rates(ext, v, grads, x, r, n)
                for a in range(3):
                    p0, p2 = wide0[a, i + 1, r : r + n], wide2[a, i + 1, r : r + n]
                    start = total([w * nd.main[a, x, r : r + n] for w, nd in begin])
                    a1[a, x, r : r + n] = start + p0 + changes[a]
                    rest[a, x, r : r + n] = rest_of(lambda nd: nd.main[a, x, r : r + n], p0, p2)
            for c in range(3):
                p0, p2 = edge0[0, c, pl.ds(i, 1)], edge2[0, c, pl.ds(i, 1)]
                rest_b[c, row] = rest_of(lambda nd: nd.behind[nd.off + c, row], p0, p2)
                p0, p2 = edge0[1, c, pl.ds(i, 1)], edge2[1, c, pl.ds(i, 1)]
                rest_a[c, row] = rest_of(lambda nd: nd.ahead[nd.off + c, row], p0, p2)

    emit_faces(a1, (a1_x, a1_l, a1_f))


def finish_kernel(
    first, v, grads, a1, a1_x, a1_b, a1_a, rest, rest_x, rest_b, rest_a,
    a2, a2_x, a2_l, a2_f, end, ext, summed, rows,
):
    fill(
        ext,
        [
            (TIME_STEP * 0.5, Node(a1, a1_x, a1_b, a1_a)),
            (TIME_STEP, Node(rest, rest_x, rest_b, rest_a)),
        ],
    )
    width, length = a1.shape[1:3]
    n = min(CHUNK, length)

    @pl.loop(0, width // 2)
    def _(i):
        for r in range(0, length, n):
            pair = []
            for q in range(2):
                x = 2 * i + q
                changes = fine_rates(ext, v, grads, x, r, n)
                pair.append([a1[a, x, r : r + n] + changes[a] for a in range(3)])
                for a in range(3):
                    a2[a, x, r : r + n] = pair[q][a]
            for a in range(3):
                summed[a, i, r : r + n] = pair[0][a] + pair[1][a]

    emit_faces(a2, (a2_x, a2_l, a2_f))

    def store(c, value):
        end[c] = value

    squeeze(summed, rows, store, 3)


def call(kernel, name, first, args, outs, scratch, flops=0, least=0, streamed=False):
    moved = sum(4 * a.size for a in args)
    room = moved + sum(4 * math.prod(dims) for dims in outs + scratch)
    values = pl.BlockSpec(memory_space=pltpu.VMEM)
    buffers = [pltpu.VMEM(dims, F32) for dims in scratch]
    if streamed:
        buffers += [pltpu.VMEM(dims, F32) for dims in outs] + [pltpu.SemaphoreType.DMA]
    return pl.pallas_call(
        kernel,
        name=name,
        out_shape=[jax.ShapeDtypeStruct(dims, F32) for dims in outs],
        in_specs=[pl.BlockSpec(memory_space=pltpu.SMEM)] * (first is not None) + [values] * len(args),
        out_specs=[pl.BlockSpec(memory_space=pl.ANY) if streamed else values] * len(outs),
        scratch_shapes=buffers,
        compiler_params=pltpu.CompilerParams(vmem_limit_bytes=min(max(room + ROOM, least), 56 << 20)),
        cost_estimate=pl.CostEstimate(flops=flops, bytes_accessed=moved, transcendentals=0),
    )(*([] if first is None else [first]), *args)


def shards(velocity, start_field, guess):
    own = guess[0]
    _, nx, ny, nz = own.shape
    cx, cy, cz = nx // 2, ny // 2, nz // 2
    slabs = lax.axis_size("tm")
    number = lax.axis_index("tm")
    first = jnp.stack([number == 0, number]).astype(F32)

    def layers_of(count):
        return [(count, 2, ny, nz), (count, nx, nz), (count, nx, nz)]

    fine, coarse = (3, nx, ny, nz), (3, cx, cy, cz)
    fine_faces, coarse_faces = layers_of(3), [(3, 2, cy, cz), (3, cx, cz), (3, cx, cz)]
    ext = (3, nx + 2, ny + 2 * PAD, nz)
    coarse_ext = (3, cx + 2, cy + 2 * PAD, cz)
    summed, rows = (3, cx, ny, nz), (cx * ny, cz)
    wide, edge, wide_rows = (3, cx + 2, ny, nz), (2, 3, cx, nz), ((cx + 2) * ny, cz)

    end_two, *packed = call(
        pack_kernel, "pack", None, [velocity, start_field, own],
        [coarse] + layers_of(7), [summed, rows], 5_000_000, 56 << 20,
    )
    layers = swap_faces(packed)
    speed, zero = call(
        coarsen_kernel, "coarsen", first, [velocity, start_field, end_two],
        [coarse, coarse], [summed, rows], 10_000_000,
    )
    grads, integral, coarse_grads, *results = call(
        offset_start_kernel, "offset_start", first, [velocity, start_field, own, *layers, zero],
        [(9, nx, ny, nz), coarse, (9, cx, cy, cz)] + coarse_faces + [coarse] + coarse_faces,
        [ext, ext, summed, (9, cx, ny, nz), rows], 40_000_000,
    )
    zero_faces, sent = results[:3], results[3:]

    def chain(step, sent, outs, scratch, own_terms):
        arrivals = []
        for turn in range(1, slabs):
            arrivals += hand_on(sent[0], sent[1:])
            if turn + 1 < slabs:
                sent = call(
                    lambda *refs, turn=turn: step(turn, *refs), "chain", first,
                    [*arrivals[-4:], *own_terms, speed, coarse_grads],
                    [outs] + coarse_faces, scratch + [coarse_ext], 2_000_000,
                )
        return arrivals

    terms = [zero, *zero_faces, integral]
    arrivals = chain(pass_start_kernel, sent, coarse, [coarse] + coarse_faces, terms)
    results = call(
        lambda *refs: settle_start_kernel(slabs - 1, *refs), "settle", first,
        [*arrivals, *terms, speed, coarse_grads, end_two, start_field],
        [coarse] + coarse_faces + [coarse] + layers_of(4), [coarse_ext], 2_000_000,
    )
    start_layers = swap_faces(results[5:])
    middle, m_x, m_l, m_f, *rest = call(
        middle_kernel, "middle", first,
        [velocity, grads, start_field, own, *layers, *results[:5], *start_layers],
        [fine] + fine_faces + [fine] + fine_faces,
        [ext, wide, edge, wide, edge, wide_rows] + coarse_faces + fine_faces, 60_000_000,
    )
    u1 = [middle, *swap_faces((m_x, m_l, m_f))]
    value, *results = call(
        finish_kernel, "finish", first, [velocity, grads, *u1, *rest],
        [fine] + fine_faces + [coarse], [ext, summed, rows], 40_000_000,
    )
    faces, end_two = results[:3], results[3]
    u0 = pass_on(value)
    u2 = [value, *swap_faces(faces)]

    own_part, following, *sent = call(
        offset_later_kernel, "offset_later", first,
        [velocity, grads, start_field, *start_layers, *u1, *u2, zero, end_two],
        [coarse, coarse, (6, cx, cy, cz)] + coarse_faces,
        [ext, ext, summed, summed, rows], 60_000_000,
    )
    arrivals = chain(pass_later_kernel, sent, (6, cx, cy, cz), [], [own_part, following])
    stage, *faces, begin, rest = call(
        lambda *refs: settle_later_kernel(slabs - 1, *refs), "settle", first,
        [*arrivals, own_part, speed, coarse_grads, start_field, u0, middle, value],
        [fine] + fine_faces + [fine, fine],
        [coarse, *coarse_faces, coarse, coarse_ext, summed, summed, rows], 10_000_000,
    )
    middle, stage, *faces = call(
        first_stage_kernel, "stage", first, [velocity, grads, stage, *swap_faces(faces), begin, rest],
        [fine, fine] + fine_faces, [ext], 40_000_000,
    )
    result, = call(
        last_stage_kernel, "last_stage", None, [velocity, grads, stage, *swap_faces(faces), middle],
        [fine], [ext], 40_000_000, streamed=True,
    )
    return result[None]


def solution(mesh):
    in_specs = (
        P(None, "gx", "gy", None),
        P(None, "gx", "gy", None),
        P("tm", None, "gx", "gy", None),
    )
    out_specs = P("tm", None, "gx", "gy", None)
    return jax.shard_map(shards, mesh=mesh, in_specs=in_specs, out_specs=out_specs, check_vma=False)
```

```python
import math

import jax
import jax.numpy as jnp
from jax import lax
from jax.experimental import pallas as pl
from jax.experimental.pallas import tpu as pltpu
from jax.sharding import PartitionSpec as P

VISCOSITY = 0.25
TIME_STEP = 0.5
PAD = 8
CHUNK = 8
ROOM = 4 << 20
F32 = jnp.float32
BF16 = jnp.bfloat16


def ring(size, by):
    return [(i, (i + by) % size) for i in range(size)]


def both_faces(faces, permute, size):
    if size == 2:
        return permute(faces, 1)
    before = permute(faces[:, 0:1], 1)
    after = permute(faces[:, 1:2], -1)
    return jnp.concatenate([before, after], axis=1)


def swap_faces(faces):
    x_faces, y_last, y_first = faces
    gx, gy = lax.axis_size("gx"), lax.axis_size("gy")
    before_after = both_faces(x_faces, lambda a, by: lax.ppermute(a, "gx", ring(gx, by)), gx)
    behind = lax.ppermute(y_last, "gy", ring(gy, 1))
    ahead = lax.ppermute(y_first, "gy", ring(gy, -1))
    return before_after, behind, ahead


def pass_on(array, dx=0, dy=0, turn=0):
    slabs, gx, gy = lax.axis_size("tm"), lax.axis_size("gx"), lax.axis_size("gy")
    pairs = []
    in_twos = turn % 2 == 1 and slabs % 2 == 0
    for t in range(slabs):
        following = t + 1 - 2 * (t % 2) if in_twos else (t + 1) % slabs
        for x in range(gx):
            for y in range(gy):
                source = (t * gx + x) * gy + y
                target = (following * gx + (x + dx) % gx) * gy + (y + dy) % gy
                pairs.append((source, target))
    return lax.ppermute(array, ("tm", "gx", "gy"), pairs)


def hand_on(turn, value, faces):
    x_faces, y_last, y_first = faces
    main = pass_on(value, 0, 0, turn)
    behind = pass_on(y_last, 0, 1, turn)
    ahead = pass_on(y_first, 0, -1, turn)
    before_after = both_faces(x_faces, lambda a, by: pass_on(a, by, 0, turn), lax.axis_size("gx"))
    return [main, behind, ahead, before_after]


class Node:
    def __init__(self, main, x_faces, behind, ahead, off=0):
        self.main, self.x_faces, self.behind, self.ahead, self.off = main, x_faces, behind, ahead, off


class Mix:
    def __init__(self, *parts):
        self.parts, self.shape = parts, parts[0][1].shape

    def __getitem__(self, key):
        return total([w * field[key] for w, field in self.parts])


def scaled(weight, value):
    return value if isinstance(weight, float) and weight == 1.0 else weight * value


def total(terms):
    result = terms[0]
    for term in terms[1:]:
        result = result + term
    return result


def each(count, unrolled=False):
    def wrap(body):
        if unrolled:
            for i in range(count):
                body(i)
        else:
            pl.loop(0, count)(body)

    return wrap


def fill(ext, parts, spread=(), unrolled=False):
    width, length = ext.shape[1] - 2, ext.shape[2] - 2 * PAD
    inner = slice(PAD, PAD + length)
    for c in range(3):
        for k, at in ((0, 0), (1, width + 1)):
            terms = [scaled(w, n.x_faces[n.off + c, k]) for w, n in parts]
            terms += [w * p[c, k * (width // 2 + 1)] for w, p, _ in spread]
            ext[c, at, inner] = total(terms)

    @each(width // 2, unrolled)
    def _(i):
        for q in range(2):
            x = 2 * i + q
            for c in range(3):
                terms = [scaled(w, n.main[c, x]) for w, n in parts]
                terms += [w * p[c, i + 1] for w, p, _ in spread]
                ext[c, x + 1, inner] = total(terms)
                row = pl.ds(x, 1)
                for k, at in ((0, PAD - 1), (1, PAD + length)):
                    terms = [scaled(w, (n.ahead if k else n.behind)[n.off + c, row]) for w, n in parts]
                    terms += [w * e[k, c, pl.ds(i, 1)] for w, _, e in spread]
                    ext[c, x + 1, at : at + 1] = total(terms)


def turned(value, by):
    return pltpu.roll(value, by % value.shape[-1], value.ndim - 1)


def sides(ext, c, x, r, n):
    here = ext[c, x, r : r + n]
    return (
        here,
        (ext[c, x + 1, r : r + n], ext[c, x, r + 1 : r + 1 + n], turned(here, -1)),
        (ext[c, x - 1, r : r + n], ext[c, x, r - 1 : r - 1 + n], turned(here, 1)),
    )


def rates(ext, x, r, n, speeds, grads_of, strength):
    here = [ext[b, x, r : r + n] for b in range(3)]
    toward = [strength - speed for speed in speeds]
    away = [strength + speed for speed in speeds]
    outputs = []
    for a in range(3):
        _, ahead, behind = sides(ext, a, x, r, n)
        grads = grads_of(a)
        result = here[a] * (grads[a] - 6.0 * strength)
        for b in range(3):
            if b != a:
                result = result + here[b] * grads[b]
            result = result + toward[b] * ahead[b] + away[b] * behind[b]
        outputs.append(result)
    return outputs


def slopes(half, a, x, r, n):
    _, ahead, behind = sides(half, a, x, r, n)
    return [ahead[b] - behind[b] for b in range(3)]


def fine_rates(ext, v, grads, x, r, n):
    speeds = [0.5 * v[b, x, r : r + n] for b in range(3)]

    def grads_of(a):
        return [grads[3 * a + b, x, r : r + n] for b in range(3)]

    return rates(ext, x + 1, PAD + r, n, speeds, grads_of, VISCOSITY)


def split(value):
    high = value.astype(BF16)
    low = (value - high.astype(F32)).astype(BF16)
    return high, low


def pair_table(rows, columns, by_row, entry):
    i = lax.broadcasted_iota(jnp.int32, (rows, columns), 0)
    j = lax.broadcasted_iota(jnp.int32, (rows, columns), 1)
    same = (i >> 1) == j if by_row else i == (j >> 1)
    return jnp.where(same, entry, 0.0).astype(BF16)


def squeeze(summed, rows, store, count):
    cx, y, z = summed.shape[1:]
    table = pair_table(z, z // 2, True, 0.125)
    for c in range(count):
        high, low = split(summed[c].reshape(cx * y, z))
        rows[...] = jnp.dot(high, table, preferred_element_type=F32) + jnp.dot(
            low, table, preferred_element_type=F32
        )
        half = cx * y // 2
        value = rows[pl.ds(0, half, stride=2)] + rows[pl.ds(1, half, stride=2)]
        store(c, value.reshape(cx, y // 2, z // 2))


def spread_along(value):
    cz = value.shape[1]
    single = pair_table(cz, 2 * cz, False, 1.0)
    table = jnp.concatenate([single, single], axis=0)
    high, low = split(value)
    return jnp.dot(jnp.concatenate([high, low], axis=1), table, preferred_element_type=F32)


def doubled(value, rows):
    count = value.shape[0]
    rows[pl.ds(0, count, stride=2)] = value
    rows[pl.ds(1, count, stride=2)] = value
    return rows[...]


def prolong_own(main, wide, rows):
    cx, cy, cz = main.shape[1:]
    for c in range(3):
        value = doubled(main[c].reshape(cx * cy, cz), rows)
        wide[c] = spread_along(value).reshape(cx, 2 * cy, 2 * cz)


def prolong(field, wide, edge, rows):
    cx, cy, cz = field.main.shape[1:]
    edges = []
    for c in range(3):
        layers = [field.x_faces[c, 0:1], field.main[c], field.x_faces[c, 1:2]]
        value = doubled(jnp.concatenate(layers, axis=0).reshape((cx + 2) * cy, cz), rows)
        wide[c] = spread_along(value).reshape(cx + 2, 2 * cy, 2 * cz)
        edges += [field.behind[c], field.ahead[c]]
    value = spread_along(jnp.concatenate(edges, axis=0))
    for c in range(3):
        for k in range(2):
            at = (2 * c + k) * cx
            edge[k, c] = value[at : at + cx]


def emit_faces(main, outs, off=0):
    x_faces, y_last, y_first = outs
    width, length = main.shape[1:3]
    for c in range(3):
        x_faces[off + c, 0] = main[c, width - 1]
        x_faces[off + c, 1] = main[c, 0]
        for x in range(width):
            y_last[off + c, x : x + 1] = main[c, x, length - 1 : length]
            y_first[off + c, x : x + 1] = main[c, x, 0:1]


def quadrant(c, rows, columns):
    up, along = c // 2, c % 2
    return slice(up * rows, (up + 1) * rows), slice(along * columns, (along + 1) * columns)


def emit_coarse_faces(main, outs, comp):
    x_faces, y_last, y_first = outs
    cx, cy, cz = main.shape[1:]
    for c in range(3):
        x_faces[(comp, 0) + quadrant(c, cy, cz)] = main[c, cx - 1]
        x_faces[(comp, 1) + quadrant(c, cy, cz)] = main[c, 0]
        rows, columns = quadrant(c, cx, cz)
        for i in range(cx):
            at = slice(rows.start + i, rows.start + i + 1)
            y_last[comp, at, columns] = main[c, i, cy - 1 : cy]
            y_first[comp, at, columns] = main[c, i, 0:1]


def take_coarse_faces(x_faces, behind, ahead, comp, outs):
    out_x, out_b, out_a = outs
    cy, cz = out_x.shape[2:]
    cx = out_b.shape[1]
    for c in range(3):
        for k in range(2):
            out_x[c, k] = x_faces[(comp, k) + quadrant(c, cy, cz)]
        out_b[c] = behind[(comp,) + quadrant(c, cx, cz)]
        out_a[c] = ahead[(comp,) + quadrant(c, cx, cz)]


def coarsen(field, summed, rows, store):
    @pl.loop(0, field.shape[1] // 2)
    def _(i):
        for c in range(3):
            summed[c, i] = field[c, 2 * i] + field[c, 2 * i + 1]

    squeeze(summed, rows, store, 3)


def offset_mix(f, s, g):
    return Mix((f / 6.0, s), (1.0 - f / 6.0, g))


def pack_kernel(v, s, g, end, x_faces, y_last, y_first, summed, rows):
    outs = (x_faces, y_last, y_first)
    emit_faces(v, outs, 0)
    f = jnp.where(lax.axis_index("tm") == 0, 1.0, 0.0)
    emit_faces(offset_mix(f, s, g), outs, 3)

    def store(c, value):
        end[c] = value

    coarsen(g, summed, rows, store)
    emit_coarse_faces(end, outs, 6)


def coarsen_kernel(first, v, s, end, speed, zero, summed, rows):
    f = first[0]

    def store_zero(c, value):
        zero[c] = f * value + (1.0 - f) * end[c]

    def store_speed(c, value):
        speed[c] = value * 0.25

    coarsen(s, summed, rows, store_zero)
    coarsen(v, summed, rows, store_speed)


def offset_start_kernel(
    first, v, s, g, x_faces, behind, ahead, zero,
    grads, integral, coarse_grads, zero_x, zero_b, zero_a, end, end_x, end_l, end_f,
    ext, half, summed, grads_summed, rows,
):
    f = first[0]
    fill(half, [(0.5, Node(v, x_faces, behind, ahead))])
    fill(ext, [(TIME_STEP, Node(offset_mix(f, s, g), x_faces, behind, ahead, 3))])
    width, length = v.shape[1:3]
    n = min(CHUNK, length)

    @pl.loop(0, width // 2)
    def _(i):
        for r in range(0, length, n):
            at = slice(r, r + n)
            for q in range(2):
                x = 2 * i + q
                for a in range(3):
                    row = slopes(half, a, x + 1, PAD + r, n)
                    for b in range(3):
                        grads[3 * a + b, x, at] = row[b]
                        if q:
                            row[b] = row[b] + grads_summed[3 * a + b, i, at]
                        grads_summed[3 * a + b, i, at] = row[b]
            pair = [fine_rates(ext, v, grads, 2 * i + q, r, n) for q in range(2)]
            for a in range(3):
                summed[a, i, at] = pair[0][a] + pair[1][a]

    def store(c, value):
        integral[c] = value
        end[c] = zero[c] + value

    squeeze(summed, rows, store, 3)
    emit_faces(end, (end_x, end_l, end_f))
    take_coarse_faces(x_faces, behind, ahead, 6, (zero_x, zero_b, zero_a))

    def store_grads(c, value):
        coarse_grads[c] = value

    squeeze(grads_summed, rows, store_grads, 9)


def offset_later_kernel(
    first, v, grads, s, x_faces, behind, ahead,
    u1, u1_x, u1_b, u1_a, u2, u2_x, u2_b, u2_a, zero, end_two,
    own, following, sent, sent_x, sent_l, sent_f,
    ext, ext_two, summed, summed_two, rows,
):
    f = first[0]
    sixth = TIME_STEP / 6.0
    last = Node(u2, u2_x, u2_b, u2_a)
    fill(ext_two, [(sixth, last)])
    fill(
        ext,
        [
            (f * sixth, Node(s, x_faces, behind, ahead)),
            (TIME_STEP * 2.0 / 3.0, Node(u1, u1_x, u1_b, u1_a)),
            (sixth, last),
        ],
    )
    width, length = v.shape[1:3]
    n = min(CHUNK, length)

    @pl.loop(0, width // 2)
    def _(i):
        for r in range(0, length, n):
            at = slice(r, r + n)
            pair = [fine_rates(ext, v, grads, 2 * i + q, r, n) for q in range(2)]
            for a in range(3):
                summed[a, i, at] = pair[0][a] + pair[1][a]
            pair = [fine_rates(ext_two, v, grads, 2 * i + q, r, n) for q in range(2)]
            for a in range(3):
                summed_two[a, i, at] = (pair[0][a] + u2[a, 2 * i, at]) + (pair[1][a] + u2[a, 2 * i + 1, at])

    def store(c, value):
        own[c] = value + (f * zero[c] - end_two[c])
        sent[c] = own[c]

    squeeze(summed, rows, store, 3)
    emit_faces(own, (sent_x, sent_l, sent_f))

    def store_following(c, value):
        following[c] = value
        sent[3 + c] = value

    squeeze(summed_two, rows, store_following, 3)


def chain_step(base, speed, coarse_grads, d0, ext, store):
    fill(ext, [(TIME_STEP, Node(*d0))], unrolled=True)
    width, length = speed.shape[1:3]
    for x in range(width):
        speeds = [speed[b, x] for b in range(3)]

        def grads_of(a):
            return [coarse_grads[3 * a + b, x] for b in range(3)]

        changes = rates(ext, x + 1, PAD, length, speeds, grads_of, VISCOSITY / 4.0)
        for a in range(3):
            store(a, x, base(a, x) + d0[0][a, x] + changes[a])


def arrival(refs):
    main, behind, ahead, x_faces = refs
    return main, x_faces, behind, ahead


def own_round(first, arrived):
    shares = [jnp.where(first[1] == float(k + 1), 1.0, 0.0) for k in range(len(arrived))]
    return lambda read: total([share * read(group) for share, group in zip(shares, arrived)])


def leave_empty(first, turn, outs):
    @pl.when(first[1] != float(turn))
    def _():
        for out in outs:
            out[...] = jnp.zeros(out.shape, F32)


def pass_start_kernel(turn, first, *refs):
    arrived, zero = arrival(refs[:4]), refs[4:8]
    integral, speed, coarse_grads, end, end_x, end_l, end_f = refs[8:15]
    d0, ext = refs[15:19], refs[19]

    @pl.when(first[1] == float(turn))
    def _():
        def base(a, x):
            return zero[0][a, x] + integral[a, x]

        def store(a, x, value):
            end[a, x] = value

        for k in range(4):
            d0[k][...] = arrived[k][...] - zero[k][...]
        chain_step(base, speed, coarse_grads, d0, ext, store)
        emit_faces(end, (end_x, end_l, end_f))

    leave_empty(first, turn, (end, end_x, end_l, end_f))


def settle_start_kernel(count, first, *refs):
    arrived = [arrival(refs[4 * k : 4 * k + 4]) for k in range(count)]
    refs = refs[4 * count :]
    zero, (integral, speed, coarse_grads, end_two, s) = refs[:4], refs[4:9]
    d0, d2, outs, ext = refs[9:13], refs[13], refs[14:17], refs[17]
    rest, own = 1.0 - first[0], own_round(first, arrived)

    def base(a, x):
        return zero[0][a, x] + integral[a, x] - end_two[a, x]

    def store(a, x, value):
        d2[a, x] = value

    for k in range(4):
        d0[k][...] = rest * (own(lambda group: group[k][...]) - zero[k][...])
    chain_step(base, speed, coarse_grads, d0, ext, store)
    emit_faces(s, outs, 0)
    emit_coarse_faces(d2, outs, 3)


def pass_later_kernel(turn, first, *refs):
    arrived, (own, following, speed, coarse_grads) = arrival(refs[:4]), refs[4:8]
    sent, sent_x, sent_l, sent_f, ext = refs[8:13]

    @pl.when(first[1] == float(turn))
    def _():
        def base(a, x):
            return own[a, x] + arrived[0][3 + a, x]

        def store(a, x, value):
            sent[a, x] = value
            sent[3 + a, x] = following[a, x]

        chain_step(base, speed, coarse_grads, arrived, ext, store)
        emit_faces(sent, (sent_x, sent_l, sent_f))

    leave_empty(first, turn, (sent, sent_x, sent_l, sent_f))


def settle_later_kernel(count, first, *refs):
    arrived = [arrival(refs[4 * k : 4 * k + 4]) for k in range(count)]
    own, speed, coarse_grads, s, u0, u1, u2, stage, stage_x, stage_l, stage_f, begin, rest = refs[4 * count : 4 * count + 13]
    d0, (d2, ext, wide0, wide2, rows) = refs[4 * count + 13 : 4 * count + 17], refs[4 * count + 17 :]
    f, picked = first[0], own_round(first, arrived)

    def base(a, x):
        return own[a, x] + picked(lambda group: group[0][3 + a, x])

    def store(a, x, value):
        d2[a, x] = value

    d0[0][...] = picked(lambda group: group[0][0:3])
    for k in range(1, 4):
        d0[k][...] = picked(lambda group: group[k][...])
    chain_step(base, speed, coarse_grads, d0, ext, store)
    prolong_own(d0[0], wide0, rows)
    prolong_own(d2, wide2, rows)

    @pl.loop(0, u0.shape[1] // 2)
    def _(i):
        for c in range(3):
            p0, p2 = wide0[c, i], wide2[c, i]
            toward_stage = TIME_STEP * (0.375 * p0 + 0.125 * p2)
            toward_rest = 0.125 * (p2 - p0)
            for q in range(2):
                x = 2 * i + q
                start, one, two = f * s[c, x] + (1.0 - f) * u0[c, x], u1[c, x], u2[c, x]
                stage[c, x] = toward_stage + TIME_STEP * (start * (5.0 / 24.0) + one / 3.0 - two / 24.0)
                begin[c, x] = start + p0
                rest[c, x] = toward_rest + (two * (5.0 / 24.0) - one / 6.0 - start / 24.0)

    emit_faces(stage, (stage_x, stage_l, stage_f))


def first_stage_kernel(first, v, grads, y, y_x, y_b, y_a, begin, rest, out, stage, stage_x, stage_l, stage_f, ext):
    fill(ext, [(1.0, Node(y, y_x, y_b, y_a))])
    width, length = v.shape[1:3]
    n = min(CHUNK, length)

    @pl.loop(0, width)
    def _(x):
        for r in range(0, length, n):
            at = slice(r, r + n)
            changes = fine_rates(ext, v, grads, x, r, n)
            for a in range(3):
                value = begin[a, x, at] + changes[a]
                out[a, x, at] = value
                stage[a, x, at] = TIME_STEP * (0.5 * value + rest[a, x, at])

    emit_faces(stage, (stage_x, stage_l, stage_f))


def last_stage_kernel(v, grads, y, y_x, y_b, y_a, begin, out, ext, made, sent):
    fill(ext, [(1.0, Node(y, y_x, y_b, y_a))])
    width, length = v.shape[1:3]
    n = min(CHUNK, length)

    @pl.loop(0, width)
    def _(x):
        for r in range(0, length, n):
            changes = fine_rates(ext, v, grads, x, r, n)
            for a in range(3):
                made[a, x, r : r + n] = begin[a, x, r : r + n] + changes[a]
        plane = pl.ds(x, 1)
        pltpu.make_async_copy(made.at[:, plane], out.at[:, plane], sent).start()

    pltpu.make_async_copy(made, out, sent).wait()


def middle_kernel(
    first, v, grads, s, g, w_x, w_b, w_a, d0, d0_x, d0_b, d0_a, d2, m_x, m_b, m_a,
    a1, a1_x, a1_l, a1_f, rest, rest_x, rest_b, rest_a,
    ext, wide0, edge0, wide2, edge2, rows, d2_x, d2_b, d2_a, g_x, g_b, g_a,
):
    f = first[0]
    take_coarse_faces(m_x, m_b, m_a, 3, (d2_x, d2_b, d2_a))
    for out, mixed, start, off in ((g_x, w_x, m_x, 3), (g_b, w_b, m_b, 3), (g_a, w_a, m_a, 3)):
        for c in range(3):
            out[c] = (1.0 + 0.2 * f) * mixed[off + c] - (0.2 * f) * start[c]
    parts = [Node(s, m_x, m_b, m_a), Node(g, g_x, g_b, g_a)]
    begin = list(zip((f, 1.0 - f), parts))
    first_stage = list(zip((5.0 / 24.0 * f, 0.5 - 5.0 / 24.0 * f), parts))
    second_stage = list(zip((f / -24.0, f / 24.0), parts))
    prolong(Node(d0, d0_x, d0_b, d0_a), wide0, edge0, rows)
    prolong(Node(d2, d2_x, d2_b, d2_a), wide2, edge2, rows)
    fill(
        ext,
        [(TIME_STEP * w, node) for w, node in first_stage],
        [(TIME_STEP * 0.375, wide0, edge0), (TIME_STEP * 0.125, wide2, edge2)],
    )
    width, length = a1.shape[1:3]
    n = min(CHUNK, length)
    last_cx = width // 2 + 1

    def rest_of(get, p0, p2):
        return total([w * get(node) for w, node in second_stage]) + 0.125 * (p2 - p0)

    for c in range(3):
        for k in range(2):
            rest_x[c, k] = rest_of(
                lambda nd: nd.x_faces[nd.off + c, k], wide0[c, k * last_cx], wide2[c, k * last_cx]
            )

    @pl.loop(0, width // 2)
    def _(i):
        for q in range(2):
            x = 2 * i + q
            row = pl.ds(x, 1)
            for r in range(0, length, n):
                changes = fine_rates(ext, v, grads, x, r, n)
                for a in range(3):
                    p0, p2 = wide0[a, i + 1, r : r + n], wide2[a, i + 1, r : r + n]
                    start = total([w * nd.main[a, x, r : r + n] for w, nd in begin])
                    a1[a, x, r : r + n] = start + p0 + changes[a]
                    rest[a, x, r : r + n] = rest_of(lambda nd: nd.main[a, x, r : r + n], p0, p2)
            for c in range(3):
                p0, p2 = edge0[0, c, pl.ds(i, 1)], edge2[0, c, pl.ds(i, 1)]
                rest_b[c, row] = rest_of(lambda nd: nd.behind[nd.off + c, row], p0, p2)
                p0, p2 = edge0[1, c, pl.ds(i, 1)], edge2[1, c, pl.ds(i, 1)]
                rest_a[c, row] = rest_of(lambda nd: nd.ahead[nd.off + c, row], p0, p2)

    emit_faces(a1, (a1_x, a1_l, a1_f))


def finish_kernel(
    first, v, grads, a1, a1_x, a1_b, a1_a, rest, rest_x, rest_b, rest_a,
    a2, a2_x, a2_l, a2_f, end, ext, summed, rows,
):
    fill(
        ext,
        [
            (TIME_STEP * 0.5, Node(a1, a1_x, a1_b, a1_a)),
            (TIME_STEP, Node(rest, rest_x, rest_b, rest_a)),
        ],
    )
    width, length = a1.shape[1:3]
    n = min(CHUNK, length)

    @pl.loop(0, width // 2)
    def _(i):
        for r in range(0, length, n):
            pair = []
            for q in range(2):
                x = 2 * i + q
                changes = fine_rates(ext, v, grads, x, r, n)
                pair.append([a1[a, x, r : r + n] + changes[a] for a in range(3)])
                for a in range(3):
                    a2[a, x, r : r + n] = pair[q][a]
            for a in range(3):
                summed[a, i, r : r + n] = pair[0][a] + pair[1][a]

    emit_faces(a2, (a2_x, a2_l, a2_f))

    def store(c, value):
        end[c] = value

    squeeze(summed, rows, store, 3)


def call(kernel, name, first, args, outs, scratch, flops=0, least=0, streamed=False):
    moved = sum(4 * a.size for a in args)
    room = moved + sum(4 * math.prod(dims) for dims in outs + scratch)
    values = pl.BlockSpec(memory_space=pltpu.VMEM)
    buffers = [pltpu.VMEM(dims, F32) for dims in scratch]
    if streamed:
        buffers += [pltpu.VMEM(dims, F32) for dims in outs] + [pltpu.SemaphoreType.DMA]
    return pl.pallas_call(
        kernel,
        name=name,
        out_shape=[jax.ShapeDtypeStruct(dims, F32) for dims in outs],
        in_specs=[pl.BlockSpec(memory_space=pltpu.SMEM)] * (first is not None) + [values] * len(args),
        out_specs=[pl.BlockSpec(memory_space=pl.ANY) if streamed else values] * len(outs),
        scratch_shapes=buffers,
        compiler_params=pltpu.CompilerParams(vmem_limit_bytes=min(max(room + ROOM, least), 56 << 20)),
        cost_estimate=pl.CostEstimate(flops=flops, bytes_accessed=moved, transcendentals=0),
    )(*([] if first is None else [first]), *args)


def shards(velocity, start_field, guess):
    own = guess[0]
    _, nx, ny, nz = own.shape
    cx, cy, cz = nx // 2, ny // 2, nz // 2
    slabs = lax.axis_size("tm")
    number = lax.axis_index("tm")
    first = jnp.stack([number == 0, number]).astype(F32)

    def layers_of(count):
        return [(count, 2, ny, nz), (count, nx, nz), (count, nx, nz)]

    fine, coarse = (3, nx, ny, nz), (3, cx, cy, cz)
    fine_faces, coarse_faces = layers_of(3), [(3, 2, cy, cz), (3, cx, cz), (3, cx, cz)]
    ext = (3, nx + 2, ny + 2 * PAD, nz)
    coarse_ext = (3, cx + 2, cy + 2 * PAD, cz)
    summed, rows = (3, cx, ny, nz), (cx * ny, cz)
    wide, edge, wide_rows = (3, cx + 2, ny, nz), (2, 3, cx, nz), ((cx + 2) * ny, cz)

    end_two, *packed = call(
        pack_kernel, "pack", None, [velocity, start_field, own],
        [coarse] + layers_of(7), [summed, rows], 5_000_000, 56 << 20,
    )
    layers = swap_faces(packed)
    speed, zero = call(
        coarsen_kernel, "coarsen", first, [velocity, start_field, end_two],
        [coarse, coarse], [summed, rows], 10_000_000,
    )
    grads, integral, coarse_grads, *results = call(
        offset_start_kernel, "offset_start", first, [velocity, start_field, own, *layers, zero],
        [(9, nx, ny, nz), coarse, (9, cx, cy, cz)] + coarse_faces + [coarse] + coarse_faces,
        [ext, ext, summed, (9, cx, ny, nz), rows], 40_000_000,
    )
    zero_faces, sent = results[:3], results[3:]

    def chain(step, sent, outs, scratch, own_terms):
        arrivals = []
        for turn in range(1, slabs):
            arrivals += hand_on(turn, sent[0], sent[1:])
            if turn + 1 < slabs:
                sent = call(
                    lambda *refs, turn=turn: step(turn, *refs), "chain", first,
                    [*arrivals[-4:], *own_terms, speed, coarse_grads],
                    [outs] + coarse_faces, scratch + [coarse_ext], 2_000_000,
                )
        return arrivals

    terms = [zero, *zero_faces, integral]
    arrivals = chain(pass_start_kernel, sent, coarse, [coarse] + coarse_faces, terms)
    results = call(
        lambda *refs: settle_start_kernel(slabs - 1, *refs), "settle", first,
        [*arrivals, *terms, speed, coarse_grads, end_two, start_field],
        [coarse] + coarse_faces + [coarse] + layers_of(4), [coarse_ext], 2_000_000,
    )
    start_layers = swap_faces(results[5:])
    middle, m_x, m_l, m_f, *rest = call(
        middle_kernel, "middle", first,
        [velocity, grads, start_field, own, *layers, *results[:5], *start_layers],
        [fine] + fine_faces + [fine] + fine_faces,
        [ext, wide, edge, wide, edge, wide_rows] + coarse_faces + fine_faces, 60_000_000,
    )
    u1 = [middle, *swap_faces((m_x, m_l, m_f))]
    value, *results = call(
        finish_kernel, "finish", first, [velocity, grads, *u1, *rest],
        [fine] + fine_faces + [coarse], [ext, summed, rows], 40_000_000,
    )
    faces, end_two = results[:3], results[3]
    u0 = pass_on(value)
    u2 = [value, *swap_faces(faces)]

    own_part, following, *sent = call(
        offset_later_kernel, "offset_later", first,
        [velocity, grads, start_field, *start_layers, *u1, *u2, zero, end_two],
        [coarse, coarse, (6, cx, cy, cz)] + coarse_faces,
        [ext, ext, summed, summed, rows], 60_000_000,
    )
    arrivals = chain(pass_later_kernel, sent, (6, cx, cy, cz), [], [own_part, following])
    stage, *faces, begin, rest = call(
        lambda *refs: settle_later_kernel(slabs - 1, *refs), "settle", first,
        [*arrivals, own_part, speed, coarse_grads, start_field, u0, middle, value],
        [fine] + fine_faces + [fine, fine],
        [coarse, *coarse_faces, coarse, coarse_ext, summed, summed, rows], 10_000_000,
    )
    middle, stage, *faces = call(
        first_stage_kernel, "stage", first, [velocity, grads, stage, *swap_faces(faces), begin, rest],
        [fine, fine] + fine_faces, [ext], 40_000_000,
    )
    result, = call(
        last_stage_kernel, "last_stage", None, [velocity, grads, stage, *swap_faces(faces), middle],
        [fine], [ext], 40_000_000, streamed=True,
    )
    return result[None]


def solution(mesh):
    in_specs = (
        P(None, "gx", "gy", None),
        P(None, "gx", "gy", None),
        P("tm", None, "gx", "gy", None),
    )
    out_specs = P("tm", None, "gx", "gy", None)
    return jax.shard_map(shards, mesh=mesh, in_specs=in_specs, out_specs=out_specs, check_vma=False)
```

```python
import math

import jax
import jax.numpy as jnp
from jax import lax
from jax.experimental import pallas as pl
from jax.experimental.pallas import tpu as pltpu
from jax.sharding import PartitionSpec as P

VISCOSITY = 0.25
TIME_STEP = 0.5
PAD = 8
CHUNK = 8
ROOM = 4 << 20
F32 = jnp.float32
BF16 = jnp.bfloat16


def ring(size, by):
    return [(i, (i + by) % size) for i in range(size)]


def both_faces(faces, permute, size):
    if size == 2:
        return permute(faces, 1)
    before = permute(faces[:, 0:1], 1)
    after = permute(faces[:, 1:2], -1)
    return jnp.concatenate([before, after], axis=1)


def swap_faces(faces):
    x_faces, y_last, y_first = faces
    gx, gy = lax.axis_size("gx"), lax.axis_size("gy")
    before_after = both_faces(x_faces, lambda a, by: lax.ppermute(a, "gx", ring(gx, by)), gx)
    behind = lax.ppermute(y_last, "gy", ring(gy, 1))
    ahead = lax.ppermute(y_first, "gy", ring(gy, -1))
    return before_after, behind, ahead


def pass_on(array, dx=0, dy=0, turn=0):
    slabs, gx, gy = lax.axis_size("tm"), lax.axis_size("gx"), lax.axis_size("gy")
    pairs = []
    in_twos = turn > 0 and slabs % 2 == 0
    for t in range(slabs):
        following = (t - 1 if in_twos and (t - turn) % 2 == 0 else t + 1) % slabs
        for x in range(gx):
            for y in range(gy):
                source = (t * gx + x) * gy + y
                target = (following * gx + (x + dx) % gx) * gy + (y + dy) % gy
                pairs.append((source, target))
    return lax.ppermute(array, ("tm", "gx", "gy"), pairs)


def hand_on(turn, value, faces):
    x_faces, y_last, y_first = faces
    main = pass_on(value, 0, 0, turn)
    behind = pass_on(y_last, 0, 1, turn)
    ahead = pass_on(y_first, 0, -1, turn)
    before_after = both_faces(x_faces, lambda a, by: pass_on(a, by, 0, turn), lax.axis_size("gx"))
    return [main, behind, ahead, before_after]


class Node:
    def __init__(self, main, x_faces, behind, ahead, off=0):
        self.main, self.x_faces, self.behind, self.ahead, self.off = main, x_faces, behind, ahead, off


class Mix:
    def __init__(self, *parts):
        self.parts, self.shape = parts, parts[0][1].shape

    def __getitem__(self, key):
        return total([w * field[key] for w, field in self.parts])


def scaled(weight, value):
    return value if isinstance(weight, float) and weight == 1.0 else weight * value


def total(terms):
    result = terms[0]
    for term in terms[1:]:
        result = result + term
    return result


def each(count, unrolled=False):
    def wrap(body):
        if unrolled:
            for i in range(count):
                body(i)
        else:
            pl.loop(0, count)(body)

    return wrap


def fill(ext, parts, spread=(), unrolled=False):
    width, length = ext.shape[1] - 2, ext.shape[2] - 2 * PAD
    inner = slice(PAD, PAD + length)
    for c in range(3):
        for k, at in ((0, 0), (1, width + 1)):
            terms = [scaled(w, n.x_faces[n.off + c, k]) for w, n in parts]
            terms += [w * p[c, k * (width // 2 + 1)] for w, p, _ in spread]
            ext[c, at, inner] = total(terms)

    @each(width // 2, unrolled)
    def _(i):
        for q in range(2):
            x = 2 * i + q
            for c in range(3):
                terms = [scaled(w, n.main[c, x]) for w, n in parts]
                terms += [w * p[c, i + 1] for w, p, _ in spread]
                ext[c, x + 1, inner] = total(terms)
                row = pl.ds(x, 1)
                for k, at in ((0, PAD - 1), (1, PAD + length)):
                    terms = [scaled(w, (n.ahead if k else n.behind)[n.off + c, row]) for w, n in parts]
                    terms += [w * e[k, c, pl.ds(i, 1)] for w, _, e in spread]
                    ext[c, x + 1, at : at + 1] = total(terms)


def turned(value, by):
    return pltpu.roll(value, by % value.shape[-1], value.ndim - 1)


def sides(ext, c, x, r, n):
    here = ext[c, x, r : r + n]
    return (
        here,
        (ext[c, x + 1, r : r + n], ext[c, x, r + 1 : r + 1 + n], turned(here, -1)),
        (ext[c, x - 1, r : r + n], ext[c, x, r - 1 : r - 1 + n], turned(here, 1)),
    )


def rates(ext, x, r, n, speeds, grads_of, strength):
    here = [ext[b, x, r : r + n] for b in range(3)]
    toward = [strength - speed for speed in speeds]
    away = [strength + speed for speed in speeds]
    outputs = []
    for a in range(3):
        _, ahead, behind = sides(ext, a, x, r, n)
        grads = grads_of(a)
        result = here[a] * (grads[a] - 6.0 * strength)
        for b in range(3):
            if b != a:
                result = result + here[b] * grads[b]
            result = result + toward[b] * ahead[b] + away[b] * behind[b]
        outputs.append(result)
    return outputs


def slopes(half, a, x, r, n):
    _, ahead, behind = sides(half, a, x, r, n)
    return [ahead[b] - behind[b] for b in range(3)]


def fine_rates(ext, v, grads, x, r, n):
    speeds = [0.5 * v[b, x, r : r + n] for b in range(3)]

    def grads_of(a):
        return [grads[3 * a + b, x, r : r + n] for b in range(3)]

    return rates(ext, x + 1, PAD + r, n, speeds, grads_of, VISCOSITY)


def split(value):
    high = value.astype(BF16)
    low = (value - high.astype(F32)).astype(BF16)
    return high, low


def pair_table(rows, columns, by_row, entry):
    i = lax.broadcasted_iota(jnp.int32, (rows, columns), 0)
    j = lax.broadcasted_iota(jnp.int32, (rows, columns), 1)
    same = (i >> 1) == j if by_row else i == (j >> 1)
    return jnp.where(same, entry, 0.0).astype(BF16)


def squeeze(summed, rows, store, count):
    cx, y, z = summed.shape[1:]
    table = pair_table(z, z // 2, True, 0.125)
    for c in range(count):
        high, low = split(summed[c].reshape(cx * y, z))
        rows[...] = jnp.dot(high, table, preferred_element_type=F32) + jnp.dot(
            low, table, preferred_element_type=F32
        )
        half = cx * y // 2
        value = rows[pl.ds(0, half, stride=2)] + rows[pl.ds(1, half, stride=2)]
        store(c, value.reshape(cx, y // 2, z // 2))


def spread_along(value):
    cz = value.shape[1]
    single = pair_table(cz, 2 * cz, False, 1.0)
    table = jnp.concatenate([single, single], axis=0)
    high, low = split(value)
    return jnp.dot(jnp.concatenate([high, low], axis=1), table, preferred_element_type=F32)


def doubled(value, rows):
    count = value.shape[0]
    rows[pl.ds(0, count, stride=2)] = value
    rows[pl.ds(1, count, stride=2)] = value
    return rows[...]


def prolong_own(main, wide, rows):
    cx, cy, cz = main.shape[1:]
    for c in range(3):
        value = doubled(main[c].reshape(cx * cy, cz), rows)
        wide[c] = spread_along(value).reshape(cx, 2 * cy, 2 * cz)


def prolong(field, wide, edge, rows):
    cx, cy, cz = field.main.shape[1:]
    edges = []
    for c in range(3):
        layers = [field.x_faces[c, 0:1], field.main[c], field.x_faces[c, 1:2]]
        value = doubled(jnp.concatenate(layers, axis=0).reshape((cx + 2) * cy, cz), rows)
        wide[c] = spread_along(value).reshape(cx + 2, 2 * cy, 2 * cz)
        edges += [field.behind[c], field.ahead[c]]
    value = spread_along(jnp.concatenate(edges, axis=0))
    for c in range(3):
        for k in range(2):
            at = (2 * c + k) * cx
            edge[k, c] = value[at : at + cx]


def emit_faces(main, outs, off=0):
    x_faces, y_last, y_first = outs
    width, length = main.shape[1:3]
    for c in range(3):
        x_faces[off + c, 0] = main[c, width - 1]
        x_faces[off + c, 1] = main[c, 0]
        for x in range(width):
            y_last[off + c, x : x + 1] = main[c, x, length - 1 : length]
            y_first[off + c, x : x + 1] = main[c, x, 0:1]


def quadrant(c, rows, columns):
    up, along = c // 2, c % 2
    return slice(up * rows, (up + 1) * rows), slice(along * columns, (along + 1) * columns)


def emit_coarse_faces(main, outs, comp):
    x_faces, y_last, y_first = outs
    cx, cy, cz = main.shape[1:]
    for c in range(3):
        x_faces[(comp, 0) + quadrant(c, cy, cz)] = main[c, cx - 1]
        x_faces[(comp, 1) + quadrant(c, cy, cz)] = main[c, 0]
        rows, columns = quadrant(c, cx, cz)
        for i in range(cx):
            at = slice(rows.start + i, rows.start + i + 1)
            y_last[comp, at, columns] = main[c, i, cy - 1 : cy]
            y_first[comp, at, columns] = main[c, i, 0:1]


def take_coarse_faces(x_faces, behind, ahead, comp, outs):
    out_x, out_b, out_a = outs
    cy, cz = out_x.shape[2:]
    cx = out_b.shape[1]
    for c in range(3):
        for k in range(2):
            out_x[c, k] = x_faces[(comp, k) + quadrant(c, cy, cz)]
        out_b[c] = behind[(comp,) + quadrant(c, cx, cz)]
        out_a[c] = ahead[(comp,) + quadrant(c, cx, cz)]


def coarsen(field, summed, rows, store):
    @pl.loop(0, field.shape[1] // 2)
    def _(i):
        for c in range(3):
            summed[c, i] = field[c, 2 * i] + field[c, 2 * i + 1]

    squeeze(summed, rows, store, 3)


def offset_mix(f, s, g):
    return Mix((f / 6.0, s), (1.0 - f / 6.0, g))


def pack_kernel(v, s, g, end, x_faces, y_last, y_first, summed, rows):
    outs = (x_faces, y_last, y_first)
    emit_faces(v, outs, 0)
    f = jnp.where(lax.axis_index("tm") == 0, 1.0, 0.0)
    emit_faces(offset_mix(f, s, g), outs, 3)

    def store(c, value):
        end[c] = value

    coarsen(g, summed, rows, store)
    emit_coarse_faces(end, outs, 6)


def coarsen_kernel(first, v, s, end, speed, zero, summed, rows):
    f = first[0]

    def store_zero(c, value):
        zero[c] = f * value + (1.0 - f) * end[c]

    def store_speed(c, value):
        speed[c] = value * 0.25

    coarsen(s, summed, rows, store_zero)
    coarsen(v, summed, rows, store_speed)


def offset_start_kernel(
    first, v, s, g, x_faces, behind, ahead, zero,
    grads, integral, coarse_grads, zero_x, zero_b, zero_a, end, end_x, end_l, end_f,
    ext, half, summed, grads_summed, rows,
):
    f = first[0]
    fill(half, [(0.5, Node(v, x_faces, behind, ahead))])
    fill(ext, [(TIME_STEP, Node(offset_mix(f, s, g), x_faces, behind, ahead, 3))])
    width, length = v.shape[1:3]
    n = min(CHUNK, length)

    @pl.loop(0, width // 2)
    def _(i):
        for r in range(0, length, n):
            at = slice(r, r + n)
            for q in range(2):
                x = 2 * i + q
                for a in range(3):
                    row = slopes(half, a, x + 1, PAD + r, n)
                    for b in range(3):
                        grads[3 * a + b, x, at] = row[b]
                        if q:
                            row[b] = row[b] + grads_summed[3 * a + b, i, at]
                        grads_summed[3 * a + b, i, at] = row[b]
            pair = [fine_rates(ext, v, grads, 2 * i + q, r, n) for q in range(2)]
            for a in range(3):
                summed[a, i, at] = pair[0][a] + pair[1][a]

    def store(c, value):
        integral[c] = value
        end[c] = zero[c] + value

    squeeze(summed, rows, store, 3)
    emit_faces(end, (end_x, end_l, end_f))
    take_coarse_faces(x_faces, behind, ahead, 6, (zero_x, zero_b, zero_a))

    def store_grads(c, value):
        coarse_grads[c] = value

    squeeze(grads_summed, rows, store_grads, 9)


def offset_later_kernel(
    first, v, grads, s, x_faces, behind, ahead,
    u1, u1_x, u1_b, u1_a, u2, u2_x, u2_b, u2_a, zero, end_two,
    own, following, sent, sent_x, sent_l, sent_f,
    ext, ext_two, summed, summed_two, rows,
):
    f = first[0]
    sixth = TIME_STEP / 6.0
    last = Node(u2, u2_x, u2_b, u2_a)
    fill(ext_two, [(sixth, last)])
    fill(
        ext,
        [
            (f * sixth, Node(s, x_faces, behind, ahead)),
            (TIME_STEP * 2.0 / 3.0, Node(u1, u1_x, u1_b, u1_a)),
            (sixth, last),
        ],
    )
    width, length = v.shape[1:3]
    n = min(CHUNK, length)

    @pl.loop(0, width // 2)
    def _(i):
        for r in range(0, length, n):
            at = slice(r, r + n)
            pair = [fine_rates(ext, v, grads, 2 * i + q, r, n) for q in range(2)]
            for a in range(3):
                summed[a, i, at] = pair[0][a] + pair[1][a]
            pair = [fine_rates(ext_two, v, grads, 2 * i + q, r, n) for q in range(2)]
            for a in range(3):
                summed_two[a, i, at] = (pair[0][a] + u2[a, 2 * i, at]) + (pair[1][a] + u2[a, 2 * i + 1, at])

    def store(c, value):
        own[c] = value + (f * zero[c] - end_two[c])
        sent[c] = own[c]

    squeeze(summed, rows, store, 3)
    emit_faces(own, (sent_x, sent_l, sent_f))

    def store_following(c, value):
        following[c] = value
        sent[3 + c] = value

    squeeze(summed_two, rows, store_following, 3)


def chain_step(base, speed, coarse_grads, d0, ext, store):
    fill(ext, [(TIME_STEP, Node(*d0))], unrolled=True)
    width, length = speed.shape[1:3]
    for x in range(width):
        speeds = [speed[b, x] for b in range(3)]

        def grads_of(a):
            return [coarse_grads[3 * a + b, x] for b in range(3)]

        changes = rates(ext, x + 1, PAD, length, speeds, grads_of, VISCOSITY / 4.0)
        for a in range(3):
            store(a, x, base(a, x) + d0[0][a, x] + changes[a])


def arrival(refs):
    main, behind, ahead, x_faces = refs
    return main, x_faces, behind, ahead


def own_round(first, arrived):
    shares = [jnp.where(first[1] == float(k + 1), 1.0, 0.0) for k in range(len(arrived))]
    return lambda read: total([share * read(group) for share, group in zip(shares, arrived)])


def leave_empty(first, turn, outs):
    @pl.when(first[1] != float(turn))
    def _():
        for out in outs:
            out[...] = jnp.zeros(out.shape, F32)


def pass_start_kernel(turn, first, *refs):
    arrived, zero = arrival(refs[:4]), refs[4:8]
    integral, speed, coarse_grads, end, end_x, end_l, end_f = refs[8:15]
    d0, ext = refs[15:19], refs[19]

    @pl.when(first[1] == float(turn))
    def _():
        def base(a, x):
            return zero[0][a, x] + integral[a, x]

        def store(a, x, value):
            end[a, x] = value

        for k in range(4):
            d0[k][...] = arrived[k][...] - zero[k][...]
        chain_step(base, speed, coarse_grads, d0, ext, store)
        emit_faces(end, (end_x, end_l, end_f))

    leave_empty(first, turn, (end, end_x, end_l, end_f))


def settle_start_kernel(count, first, *refs):
    arrived = [arrival(refs[4 * k : 4 * k + 4]) for k in range(count)]
    refs = refs[4 * count :]
    zero, (integral, speed, coarse_grads, end_two, s) = refs[:4], refs[4:9]
    d0, d2, outs, ext = refs[9:13], refs[13], refs[14:17], refs[17]
    rest, own = 1.0 - first[0], own_round(first, arrived)

    def base(a, x):
        return zero[0][a, x] + integral[a, x] - end_two[a, x]

    def store(a, x, value):
        d2[a, x] = value

    for k in range(4):
        d0[k][...] = rest * (own(lambda group: group[k][...]) - zero[k][...])
    chain_step(base, speed, coarse_grads, d0, ext, store)
    emit_faces(s, outs, 0)
    emit_coarse_faces(d2, outs, 3)


def pass_later_kernel(turn, first, *refs):
    arrived, (own, following, speed, coarse_grads) = arrival(refs[:4]), refs[4:8]
    sent, sent_x, sent_l, sent_f, ext = refs[8:13]

    @pl.when(first[1] == float(turn))
    def _():
        def base(a, x):
            return own[a, x] + arrived[0][3 + a, x]

        def store(a, x, value):
            sent[a, x] = value
            sent[3 + a, x] = following[a, x]

        chain_step(base, speed, coarse_grads, arrived, ext, store)
        emit_faces(sent, (sent_x, sent_l, sent_f))

    leave_empty(first, turn, (sent, sent_x, sent_l, sent_f))


def settle_later_kernel(count, first, *refs):
    arrived = [arrival(refs[4 * k : 4 * k + 4]) for k in range(count)]
    own, speed, coarse_grads, s, u0, u1, u2, stage, stage_x, stage_l, stage_f, begin, rest = refs[4 * count : 4 * count + 13]
    d0, (d2, ext, wide0, wide2, rows) = refs[4 * count + 13 : 4 * count + 17], refs[4 * count + 17 :]
    f, picked = first[0], own_round(first, arrived)

    def base(a, x):
        return own[a, x] + picked(lambda group: group[0][3 + a, x])

    def store(a, x, value):
        d2[a, x] = value

    d0[0][...] = picked(lambda group: group[0][0:3])
    for k in range(1, 4):
        d0[k][...] = picked(lambda group: group[k][...])
    chain_step(base, speed, coarse_grads, d0, ext, store)
    prolong_own(d0[0], wide0, rows)
    prolong_own(d2, wide2, rows)

    @pl.loop(0, u0.shape[1] // 2)
    def _(i):
        for c in range(3):
            p0, p2 = wide0[c, i], wide2[c, i]
            toward_stage = TIME_STEP * (0.375 * p0 + 0.125 * p2)
            toward_rest = 0.125 * (p2 - p0)
            for q in range(2):
                x = 2 * i + q
                start, one, two = f * s[c, x] + (1.0 - f) * u0[c, x], u1[c, x], u2[c, x]
                stage[c, x] = toward_stage + TIME_STEP * (start * (5.0 / 24.0) + one / 3.0 - two / 24.0)
                begin[c, x] = start + p0
                rest[c, x] = toward_rest + (two * (5.0 / 24.0) - one / 6.0 - start / 24.0)

    emit_faces(stage, (stage_x, stage_l, stage_f))


def first_stage_kernel(first, v, grads, y, y_x, y_b, y_a, begin, rest, out, stage, stage_x, stage_l, stage_f, ext):
    fill(ext, [(1.0, Node(y, y_x, y_b, y_a))])
    width, length = v.shape[1:3]
    n = min(CHUNK, length)

    @pl.loop(0, width)
    def _(x):
        for r in range(0, length, n):
            at = slice(r, r + n)
            changes = fine_rates(ext, v, grads, x, r, n)
            for a in range(3):
                value = begin[a, x, at] + changes[a]
                out[a, x, at] = value
                stage[a, x, at] = TIME_STEP * (0.5 * value + rest[a, x, at])

    emit_faces(stage, (stage_x, stage_l, stage_f))


def last_stage_kernel(v, grads, y, y_x, y_b, y_a, begin, out, ext, made, sent):
    fill(ext, [(1.0, Node(y, y_x, y_b, y_a))])
    width, length = v.shape[1:3]
    n = min(CHUNK, length)

    @pl.loop(0, width)
    def _(x):
        for r in range(0, length, n):
            changes = fine_rates(ext, v, grads, x, r, n)
            for a in range(3):
                made[a, x, r : r + n] = begin[a, x, r : r + n] + changes[a]
        plane = pl.ds(x, 1)
        pltpu.make_async_copy(made.at[:, plane], out.at[:, plane], sent).start()

    pltpu.make_async_copy(made, out, sent).wait()


def middle_kernel(
    first, v, grads, s, g, w_x, w_b, w_a, d0, d0_x, d0_b, d0_a, d2, m_x, m_b, m_a,
    a1, a1_x, a1_l, a1_f, rest, rest_x, rest_b, rest_a,
    ext, wide0, edge0, wide2, edge2, rows, d2_x, d2_b, d2_a, g_x, g_b, g_a,
):
    f = first[0]
    take_coarse_faces(m_x, m_b, m_a, 3, (d2_x, d2_b, d2_a))
    for out, mixed, start, off in ((g_x, w_x, m_x, 3), (g_b, w_b, m_b, 3), (g_a, w_a, m_a, 3)):
        for c in range(3):
            out[c] = (1.0 + 0.2 * f) * mixed[off + c] - (0.2 * f) * start[c]
    parts = [Node(s, m_x, m_b, m_a), Node(g, g_x, g_b, g_a)]
    begin = list(zip((f, 1.0 - f), parts))
    first_stage = list(zip((5.0 / 24.0 * f, 0.5 - 5.0 / 24.0 * f), parts))
    second_stage = list(zip((f / -24.0, f / 24.0), parts))
    prolong(Node(d0, d0_x, d0_b, d0_a), wide0, edge0, rows)
    prolong(Node(d2, d2_x, d2_b, d2_a), wide2, edge2, rows)
    fill(
        ext,
        [(TIME_STEP * w, node) for w, node in first_stage],
        [(TIME_STEP * 0.375, wide0, edge0), (TIME_STEP * 0.125, wide2, edge2)],
    )
    width, length = a1.shape[1:3]
    n = min(CHUNK, length)
    last_cx = width // 2 + 1

    def rest_of(get, p0, p2):
        return total([w * get(node) for w, node in second_stage]) + 0.125 * (p2 - p0)

    for c in range(3):
        for k in range(2):
            rest_x[c, k] = rest_of(
                lambda nd: nd.x_faces[nd.off + c, k], wide0[c, k * last_cx], wide2[c, k * last_cx]
            )

    @pl.loop(0, width // 2)
    def _(i):
        for q in range(2):
            x = 2 * i + q
            row = pl.ds(x, 1)
            for r in range(0, length, n):
                changes = fine_rates(ext, v, grads, x, r, n)
                for a in range(3):
                    p0, p2 = wide0[a, i + 1, r : r + n], wide2[a, i + 1, r : r + n]
                    start = total([w * nd.main[a, x, r : r + n] for w, nd in begin])
                    a1[a, x, r : r + n] = start + p0 + changes[a]
                    rest[a, x, r : r + n] = rest_of(lambda nd: nd.main[a, x, r : r + n], p0, p2)
            for c in range(3):
                p0, p2 = edge0[0, c, pl.ds(i, 1)], edge2[0, c, pl.ds(i, 1)]
                rest_b[c, row] = rest_of(lambda nd: nd.behind[nd.off + c, row], p0, p2)
                p0, p2 = edge0[1, c, pl.ds(i, 1)], edge2[1, c, pl.ds(i, 1)]
                rest_a[c, row] = rest_of(lambda nd: nd.ahead[nd.off + c, row], p0, p2)

    emit_faces(a1, (a1_x, a1_l, a1_f))


def finish_kernel(
    first, v, grads, a1, a1_x, a1_b, a1_a, rest, rest_x, rest_b, rest_a,
    a2, a2_x, a2_l, a2_f, end, ext, summed, rows,
):
    fill(
        ext,
        [
            (TIME_STEP * 0.5, Node(a1, a1_x, a1_b, a1_a)),
            (TIME_STEP, Node(rest, rest_x, rest_b, rest_a)),
        ],
    )
    width, length = a1.shape[1:3]
    n = min(CHUNK, length)

    @pl.loop(0, width // 2)
    def _(i):
        for r in range(0, length, n):
            pair = []
            for q in range(2):
                x = 2 * i + q
                changes = fine_rates(ext, v, grads, x, r, n)
                pair.append([a1[a, x, r : r + n] + changes[a] for a in range(3)])
                for a in range(3):
                    a2[a, x, r : r + n] = pair[q][a]
            for a in range(3):
                summed[a, i, r : r + n] = pair[0][a] + pair[1][a]

    emit_faces(a2, (a2_x, a2_l, a2_f))

    def store(c, value):
        end[c] = value

    squeeze(summed, rows, store, 3)


def call(kernel, name, first, args, outs, scratch, flops=0, least=0, streamed=False):
    moved = sum(4 * a.size for a in args)
    room = moved + sum(4 * math.prod(dims) for dims in outs + scratch)
    values = pl.BlockSpec(memory_space=pltpu.VMEM)
    buffers = [pltpu.VMEM(dims, F32) for dims in scratch]
    if streamed:
        buffers += [pltpu.VMEM(dims, F32) for dims in outs] + [pltpu.SemaphoreType.DMA]
    return pl.pallas_call(
        kernel,
        name=name,
        out_shape=[jax.ShapeDtypeStruct(dims, F32) for dims in outs],
        in_specs=[pl.BlockSpec(memory_space=pltpu.SMEM)] * (first is not None) + [values] * len(args),
        out_specs=[pl.BlockSpec(memory_space=pl.ANY) if streamed else values] * len(outs),
        scratch_shapes=buffers,
        compiler_params=pltpu.CompilerParams(vmem_limit_bytes=min(max(room + ROOM, least), 56 << 20)),
        cost_estimate=pl.CostEstimate(flops=flops, bytes_accessed=moved, transcendentals=0),
    )(*([] if first is None else [first]), *args)


def shards(velocity, start_field, guess):
    own = guess[0]
    _, nx, ny, nz = own.shape
    cx, cy, cz = nx // 2, ny // 2, nz // 2
    slabs = lax.axis_size("tm")
    number = lax.axis_index("tm")
    first = jnp.stack([number == 0, number]).astype(F32)

    def layers_of(count):
        return [(count, 2, ny, nz), (count, nx, nz), (count, nx, nz)]

    fine, coarse = (3, nx, ny, nz), (3, cx, cy, cz)
    fine_faces, coarse_faces = layers_of(3), [(3, 2, cy, cz), (3, cx, cz), (3, cx, cz)]
    ext = (3, nx + 2, ny + 2 * PAD, nz)
    coarse_ext = (3, cx + 2, cy + 2 * PAD, cz)
    summed, rows = (3, cx, ny, nz), (cx * ny, cz)
    wide, edge, wide_rows = (3, cx + 2, ny, nz), (2, 3, cx, nz), ((cx + 2) * ny, cz)

    end_two, *packed = call(
        pack_kernel, "pack", None, [velocity, start_field, own],
        [coarse] + layers_of(7), [summed, rows], 5_000_000, 56 << 20,
    )
    layers = swap_faces(packed)
    speed, zero = call(
        coarsen_kernel, "coarsen", first, [velocity, start_field, end_two],
        [coarse, coarse], [summed, rows], 10_000_000,
    )
    grads, integral, coarse_grads, *results = call(
        offset_start_kernel, "offset_start", first, [velocity, start_field, own, *layers, zero],
        [(9, nx, ny, nz), coarse, (9, cx, cy, cz)] + coarse_faces + [coarse] + coarse_faces,
        [ext, ext, summed, (9, cx, ny, nz), rows], 40_000_000,
    )
    zero_faces, sent = results[:3], results[3:]

    def chain(step, sent, outs, scratch, own_terms):
        arrivals = []
        for turn in range(1, slabs):
            arrivals += hand_on(turn, sent[0], sent[1:])
            if turn + 1 < slabs:
                sent = call(
                    lambda *refs, turn=turn: step(turn, *refs), "chain", first,
                    [*arrivals[-4:], *own_terms, speed, coarse_grads],
                    [outs] + coarse_faces, scratch + [coarse_ext], 2_000_000,
                )
        return arrivals

    terms = [zero, *zero_faces, integral]
    arrivals = chain(pass_start_kernel, sent, coarse, [coarse] + coarse_faces, terms)
    results = call(
        lambda *refs: settle_start_kernel(slabs - 1, *refs), "settle", first,
        [*arrivals, *terms, speed, coarse_grads, end_two, start_field],
        [coarse] + coarse_faces + [coarse] + layers_of(4), [coarse_ext], 2_000_000,
    )
    start_layers = swap_faces(results[5:])
    middle, m_x, m_l, m_f, *rest = call(
        middle_kernel, "middle", first,
        [velocity, grads, start_field, own, *layers, *results[:5], *start_layers],
        [fine] + fine_faces + [fine] + fine_faces,
        [ext, wide, edge, wide, edge, wide_rows] + coarse_faces + fine_faces, 60_000_000,
    )
    u1 = [middle, *swap_faces((m_x, m_l, m_f))]
    value, *results = call(
        finish_kernel, "finish", first, [velocity, grads, *u1, *rest],
        [fine] + fine_faces + [coarse], [ext, summed, rows], 40_000_000,
    )
    faces, end_two = results[:3], results[3]
    u0 = pass_on(value)
    u2 = [value, *swap_faces(faces)]

    own_part, following, *sent = call(
        offset_later_kernel, "offset_later", first,
        [velocity, grads, start_field, *start_layers, *u1, *u2, zero, end_two],
        [coarse, coarse, (6, cx, cy, cz)] + coarse_faces,
        [ext, ext, summed, summed, rows], 60_000_000,
    )
    arrivals = chain(pass_later_kernel, sent, (6, cx, cy, cz), [], [own_part, following])
    stage, *faces, begin, rest = call(
        lambda *refs: settle_later_kernel(slabs - 1, *refs), "settle", first,
        [*arrivals, own_part, speed, coarse_grads, start_field, u0, middle, value],
        [fine] + fine_faces + [fine, fine],
        [coarse, *coarse_faces, coarse, coarse_ext, summed, summed, rows], 10_000_000,
    )
    middle, stage, *faces = call(
        first_stage_kernel, "stage", first, [velocity, grads, stage, *swap_faces(faces), begin, rest],
        [fine, fine] + fine_faces, [ext], 40_000_000,
    )
    result, = call(
        last_stage_kernel, "last_stage", None, [velocity, grads, stage, *swap_faces(faces), middle],
        [fine], [ext], 40_000_000, streamed=True,
    )
    return result[None]


def solution(mesh):
    in_specs = (
        P(None, "gx", "gy", None),
        P(None, "gx", "gy", None),
        P("tm", None, "gx", "gy", None),
    )
    out_specs = P("tm", None, "gx", "gy", None)
    return jax.shard_map(shards, mesh=mesh, in_specs=in_specs, out_specs=out_specs, check_vma=False)
```
